32 devices in a mesh: tm: 4 (over y, x), space: 8 (over z, core).
Axes of the slice: x: 2, y: 2, z: 4, core: 2. Of those that a mesh axis runs over, the one named last changes fastest.
Arguments:
- residual: float32 [256, 16, 32, 256], P('tm', 'space'), may hold values from -8 to 8
- step_ratio: int32 [256], P('tm'), may hold values from 4 to 12
- forward_map: float32 [2, 256, 256], replicated, may hold values from -1 to 2
- back_map: float32 [2, 256, 256], replicated, may hold values from -1 to 2
- eigen_values: float32 [2, 256], replicated, may hold values from -3 to 4, as said below
Outputs:
- correction: float32 [2, 256, 16, 32, 256], P(None, 'tm', 'space')
The draws below stay inside these ranges and needn't reach their ends.
Inputs may be any that keep to these rules, and one draw needn't show every extreme that they name: `eigen_values`: real parts of the shifts are positive, from 0.2 to 4; imaginary parts lie in -3 to 3.
All inputs are finite; a program needn't handle non-finite values.
Results may differ from the reference program's by a relative error of at most 0.000098.
Values sent between devices are 32-bit elements; how exact they have to be, the bound alone decides.
No kernel may reach another device: no remote copies, remote signals or barrier semaphores. Data moves between devices by JAX's collectives and lax.ppermute only.
A program may use at most 128 MiB of HBM per device.

```python
import math
import jax
import jax.numpy as jnp
from jax import lax

STEPS = 256
NX = 32
NY = 256
SWEEPS = 2
NZ = 16


def with_diagonal(noise):
    eye_part = jnp.eye(STEPS, dtype=jnp.float32)[None] * jnp.array([1.0, 0.0], jnp.float32)[:, None, None]
    return eye_part + jnp.clip(noise, -6.0, 6.0) * (0.5 / math.sqrt(STEPS))


def draw_forward_map(key, part):
    key = jax.random.fold_in(key, 11)
    noise = jax.random.normal(key, (2, STEPS, STEPS), jnp.float32)
    return with_diagonal(noise)


def draw_back_map(key, part):
    key = jax.random.fold_in(key, 12)
    noise = jax.random.normal(key, (2, STEPS, STEPS), jnp.float32)
    return with_diagonal(noise)


def draw_eigen_values(key, part):
    key = jax.random.fold_in(key, 13)
    unit = jax.random.uniform(key, (2, STEPS), jnp.float32)
    first = unit[0]
    real_part = 0.2 * jnp.exp(first * 2.9957323)
    imag_part = 6.0 * unit[1] - 3.0
    return jnp.stack([real_part, imag_part])


def plant(values, stream_key, least, high):
    longest = values.shape.index(max(values.shape))
    spots = []
    for shift in (0, 1):
        where = [jax.random.randint(jax.random.fold_in(stream_key, axis), (), 0, length) for axis, length in enumerate(values.shape)]
        where[longest] = (where[longest] + shift) % values.shape[longest]
        spots.append(tuple(where))
    return values.at[spots[0]].set(least).at[spots[1]].set(high)


def shard_levels(stream_key, dims, cuts, least, top_value):
    loudness = 1.0
    for dim, blocks in cuts:
        heights = jax.random.uniform(jax.random.fold_in(jax.random.fold_in(stream_key, 6), dim), (blocks,), jnp.float32, least / len(cuts), top_value / len(cuts))
        loudness = loudness * jnp.repeat(jnp.exp(heights), dims[dim] // blocks).reshape((-1,) + (1,) * (len(dims) - 1 - dim))
    return loudness


def normal_values(key, extent, width, most, pieces=(), held_as=jnp.bfloat16):
    result = width * jax.random.normal(key, extent, jnp.float32)
    if pieces:
        result = result * shard_levels(key, extent, pieces, -0.22, 0.18)
    return jnp.clip(result, -most, most).astype(held_as)


def setup_inputs(seed: int = 0) -> dict:
    keys = jax.random.split(jax.random.key(seed), 6)
    residual = normal_values(keys[0], (STEPS, NZ, NX, NY), 1.0, 8.0, ((0, 4), (1, 8)), jnp.float32)
    step_ratio = plant(jax.random.randint(keys[1], (STEPS,), 4, 13), jax.random.fold_in(keys[1], 1), 4, 12).astype(jnp.int32)
    forward_map = draw_forward_map(jax.random.fold_in(keys[5], 71), 0)
    back_map = draw_back_map(jax.random.fold_in(keys[5], 71), 0)
    eigen_values = draw_eigen_values(jax.random.fold_in(keys[5], 71), 0)
    return dict(residual=residual, step_ratio=step_ratio, forward_map=forward_map, back_map=back_map, eigen_values=eigen_values)


def neighbours(field):
    padded = jnp.pad(field, ((0, 0), (0, 0), (1, 1), (1, 1), (1, 1)))
    total = padded[:, :, 2:, 1:-1, 1:-1] + padded[:, :, :-2, 1:-1, 1:-1]
    total = total + padded[:, :, 1:-1, 2:, 1:-1] + padded[:, :, 1:-1, :-2, 1:-1]
    return total + padded[:, :, 1:-1, 1:-1, 2:] + padded[:, :, 1:-1, 1:-1, :-2]


def reference(residual, step_ratio, forward_map, back_map, eigen_values):
    shape = residual.shape
    ratio = step_ratio.astype(jnp.float32) / 8.0
    scaled = (residual * ratio[:, None, None, None]).reshape(shape[0], -1)
    hi = lax.Precision.HIGHEST
    source = jnp.stack([jnp.dot(forward_map[0], scaled, precision=hi),
                        jnp.dot(forward_map[1], scaled, precision=hi)])
    source = source.reshape((2,) + shape)
    real_part = 6.0 + eigen_values[0]
    imag_part = eigen_values[1]
    denom = real_part * real_part + imag_part * imag_part
    coef_re = (real_part / denom)[:, None, None, None]
    coef_im = (-imag_part / denom)[:, None, None, None]

    def divide(total):
        return jnp.stack([total[0] * coef_re - total[1] * coef_im,
                          total[0] * coef_im + total[1] * coef_re])

    field = divide(source)
    for sweep in range(SWEEPS - 1):
        field = divide(source + neighbours(field))
    flat = field.reshape(2, shape[0], -1)
    out_re = jnp.dot(back_map[0], flat[0], precision=hi) - jnp.dot(back_map[1], flat[1], precision=hi)
    out_im = jnp.dot(back_map[0], flat[1], precision=hi) + jnp.dot(back_map[1], flat[0], precision=hi)
    return jnp.stack([out_re, out_im]).reshape((2,) + shape)
```

```python
import functools

import jax
import jax.numpy as jnp
from jax import lax
from jax.experimental import pallas as pl
from jax.experimental.pallas import tpu as pltpu
from jax.sharding import PartitionSpec as P


CUTS = 2


def block_row(stream, side, row, depth, rows_x):
    if stream == 0:
        return row + side * (rows_x - 1 - 2 * row)
    return depth * (1 + side) + row


def chunk_rows(stream, chunk, depth):
    high = depth // CUTS
    first = chunk * high + 1 if chunk else (0 if stream == 0 else -1)
    return list(range(first, (chunk + 1) * high + 1))


def spread_kernel(depth, planes, sides_ref, ratio_ref, in_ref, *outs):
    steps, _, rows_x, _ = in_ref.shape
    flat = in_ref.reshape(steps * planes * rows_x, in_ref.shape[3])
    ratio = ratio_ref[...]
    place = 0
    for stream in range(2):
        for other in range(2):
            side = sides_ref[stream] if other == 0 else 1 - sides_ref[stream]
            for chunk in range(CUTS):
                out = outs[place]
                place += 1
                for at, row in enumerate(chunk_rows(stream, chunk, depth)):
                    x = block_row(stream, side, row, depth, rows_x)
                    for z in range(planes):
                        part = flat[pl.ds(z * rows_x + x, steps, stride=planes * rows_x), :]
                        out[at, z] = part * ratio


def spread(residual, ratio, sides, depth):
    steps, planes, rows_x, rows_y = residual.shape
    lanes = 128
    block = min(steps, 32)
    shapes, specs = [], []
    for stream in range(2):
        for _ in range(2):
            for chunk in range(CUTS):
                count = len(chunk_rows(stream, chunk, depth))
                shapes.append(jax.ShapeDtypeStruct((count, planes, steps, rows_y), jnp.float32))
                specs.append(pl.BlockSpec((count, planes, block, lanes), lambda i, j: (0, 0, i, j)))
    outs = pl.pallas_call(
        functools.partial(spread_kernel, depth, planes),
        out_shape=shapes,
        grid=(steps // block, rows_y // lanes),
        in_specs=[
            pl.BlockSpec(memory_space=pltpu.SMEM),
            pl.BlockSpec((block, 1), lambda i, j: (i, 0)),
            pl.BlockSpec((block, planes, rows_x, lanes), lambda i, j: (i, 0, 0, j)),
        ],
        out_specs=specs,
        compiler_params=pltpu.CompilerParams(vmem_limit_bytes=48 * 2**20),
        cost_estimate=pl.CostEstimate(flops=residual.size * 2, bytes_accessed=residual.size * 10, transcendentals=0),
        name="spread",
    )(sides, ratio, residual)
    outs = list(outs)
    return [[outs[(2 * s + o) * CUTS : (2 * s + o + 1) * CUTS] for o in range(2)] for s in range(2)]


def halves(value):
    high = value.astype(jnp.bfloat16)
    return high, (value - high.astype(jnp.float32)).astype(jnp.bfloat16)


def apply_kernel(stream, chunk, depth, planes, groups, near_ref, far_ref, *refs):
    outs = refs[-4:]
    raws = refs[:-4]
    count = len(raws) // groups
    own_ref, send_ref, down_ref, up_ref = outs
    rows_y = own_ref.shape[-1]
    where = {}
    for c in range(count):
        for at, row in enumerate(chunk_rows(stream, chunk - count + 1 + c, depth)):
            where[row] = (c, at)

    def load(row, z):
        if row not in where:
            return None
        c, at = where[row]
        return jnp.concatenate([raws[c * groups + g][at, z] for g in range(groups)], axis=0)

    near, far = near_ref[...], far_ref[...]
    half = near.shape[0] // 2
    high = depth // CUTS
    for at in range(high):
        row = chunk * high + at
        across = []
        for z in range(planes):
            mid = load(row, z)
            lane = lax.broadcasted_iota(jnp.int32, mid.shape, 1)
            total = jnp.where(lane == 0, 0.0, pltpu.roll(mid, 1, 1))
            total = total + jnp.where(lane == rows_y - 1, 0.0, pltpu.roll(mid, rows_y - 1, 1))
            for beside in (load(row - 1, z), load(row + 1, z)):
                if beside is not None:
                    total = total + beside
            mid_h, mid_l = halves(mid)
            sum_h, sum_l = halves(total)
            thick = jnp.concatenate([mid_h, mid_h, mid_l, sum_h, sum_h, sum_l], axis=0)
            thin = jnp.concatenate([mid_h, mid_h, mid_l], axis=0)
            value = jnp.dot(near, thick, preferred_element_type=jnp.float32)
            own_ref[at, z] = value[:half]
            send_ref[at, z] = value[half:]
            across.append(jnp.dot(far, thin, preferred_element_type=jnp.float32))
        down_ref[0, at] = across[0][:half]
        down_ref[1, at] = across[0][half:]
        up_ref[0, at] = across[-1][:half]
        up_ref[1, at] = across[-1][half:]
        for z in range(planes):
            for beside in across[max(z - 1, 0) : z] + across[z + 1 : z + 2]:
                own_ref[at, z] += beside[:half]
                send_ref[at, z] += beside[half:]


def apply(stream, chunk, depth, near, far, raws):
    groups = len(raws[0])
    _, planes, steps, rows_y = raws[0][0].shape
    high = depth // CUTS
    half = near.shape[0] // 2
    flat = [r for chunk_raws in raws for r in chunk_raws]
    shapes = [jax.ShapeDtypeStruct((high, planes, half, rows_y), jnp.float32)] * 2
    shapes += [jax.ShapeDtypeStruct((2, high, half, rows_y), jnp.float32)] * 2
    flops = 2 * high * planes * rows_y * (near.size + far.size)
    return pl.pallas_call(
        functools.partial(apply_kernel, stream, chunk, depth, planes, groups),
        out_shape=shapes,
        in_specs=[pl.BlockSpec(memory_space=pltpu.VMEM)] * (2 + len(flat)),
        out_specs=[pl.BlockSpec(memory_space=pltpu.VMEM)] * 4,
        compiler_params=pltpu.CompilerParams(vmem_limit_bytes=48 * 2**20),
        cost_estimate=pl.CostEstimate(flops=flops, bytes_accessed=12 * 2**20, transcendentals=0),
        name="apply",
    )(near, far, *flat)


def add_kernel(send_ref, low_ref, high_ref, out_ref):
    planes = out_ref.shape[1]
    for z in range(planes):
        value = send_ref[:, z]
        if z == 0:
            value = value + low_ref[0]
        if z == planes - 1:
            value = value + high_ref[0]
        out_ref[:, z] = value


def add_far(send, low, high):
    count, planes, half, rows_y = send.shape
    return pl.pallas_call(
        add_kernel,
        out_shape=jax.ShapeDtypeStruct(send.shape, jnp.float32),
        grid=(count,),
        in_specs=[
            pl.BlockSpec((1, planes, half, rows_y), lambda i: (i, 0, 0, 0)),
            pl.BlockSpec((1, 1, half, rows_y), lambda i: (1, i, 0, 0)),
            pl.BlockSpec((1, 1, half, rows_y), lambda i: (1, i, 0, 0)),
        ],
        out_specs=pl.BlockSpec((1, planes, half, rows_y), lambda i: (i, 0, 0, 0)),
        cost_estimate=pl.CostEstimate(flops=send.size, bytes_accessed=send.size * 12, transcendentals=0),
        name="add_far",
    )(send, low, high)


def gather_kernel(depth, sides_ref, *refs):
    out_ref = refs[-1]
    place = 0
    count, planes, rows_x, lanes = out_ref.shape
    flat = out_ref.reshape(count * planes * rows_x, lanes)
    high = depth // CUTS
    for stream in range(2):
        side = sides_ref[stream]
        for chunk in range(CUTS):
            own, low, up, got = refs[place : place + 4]
            place += 4
            for at in range(high):
                row = chunk * high + at
                x = block_row(stream, side, row, depth, rows_x)
                y = block_row(stream, 1 - side, row, depth, rows_x)
                for z in range(planes):
                    value = own[at, z]
                    if z == 0:
                        value = value + low[0, at]
                    if z == planes - 1:
                        value = value + up[0, at]
                    flat[pl.ds(z * rows_x + x, count, stride=planes * rows_x), :] = value
                    flat[pl.ds(z * rows_x + y, count, stride=planes * rows_x), :] = got[at, z]


def collect(parts, sides, depth, rows_x):
    high, planes, half, rows_y = parts[0][0].shape
    lanes = 128
    block = min(half, 32)
    cells = pl.BlockSpec((high, planes, block, lanes), lambda i, j: (0, 0, i, j))
    edge = pl.BlockSpec((1, high, block, lanes), lambda i, j: (0, 0, i, j))
    flat = [a for part in parts for a in part]
    return pl.pallas_call(
        functools.partial(gather_kernel, depth),
        out_shape=jax.ShapeDtypeStruct((half, planes, rows_x, rows_y), jnp.float32),
        grid=(half // block, rows_y // lanes),
        in_specs=[pl.BlockSpec(memory_space=pltpu.SMEM)] + [cells, edge, edge, cells] * len(parts),
        out_specs=pl.BlockSpec((block, planes, rows_x, lanes), lambda i, j: (i, 0, 0, j)),
        compiler_params=pltpu.CompilerParams(vmem_limit_bytes=48 * 2**20),
        name="collect",
    )(sides, *flat)


def make_maps(forward_map, back_map, eigen_values, me, count, bits):
    steps = forward_map.shape[1]
    local_steps = steps // count
    highest = lax.Precision.HIGHEST
    real_part = 6.0 + eigen_values[0]
    imag_part = eigen_values[1]
    denom = real_part * real_part + imag_part * imag_part
    coef_re = (real_part / denom)[:, None]
    coef_im = (-imag_part / denom)[:, None]
    order = jnp.bitwise_xor(me, jnp.arange(count))
    ahead = forward_map.reshape(2, steps, count, local_steps)
    ahead = jnp.take(ahead, order, axis=2).reshape(2, steps, steps)
    once_re = coef_re * ahead[0] - coef_im * ahead[1]
    once_im = coef_re * ahead[1] + coef_im * ahead[0]
    twice_re = coef_re * once_re - coef_im * once_im
    twice_im = coef_re * once_im + coef_im * once_re
    right = jnp.concatenate(
        [jnp.concatenate([once_re, twice_re], axis=1), jnp.concatenate([once_im, twice_im], axis=1)], axis=0
    )
    blocks = jnp.stack([me, jnp.bitwise_xor(me, bits[0]), jnp.bitwise_xor(me, bits[1])])
    back = jnp.take(back_map.reshape(2, count, local_steps, steps), blocks, axis=1)
    left_re = jnp.concatenate([back[0], -back[1]], axis=2)
    left_im = jnp.concatenate([back[1], back[0]], axis=2)
    left = jnp.stack([left_re, left_im], axis=1).reshape(3, 2 * local_steps, 2 * steps)
    maps = jnp.einsum("bmk,kn->bmn", left, right, precision=highest)
    maps = [jnp.concatenate([maps[0], maps[1 + s]], axis=0) for s in range(2)]
    result = []
    for both in maps:
        one_h, one_l = halves(both[:, :steps])
        two_h, two_l = halves(both[:, steps:])
        near = jnp.concatenate([one_h, one_l, one_h, two_h, two_l, two_h], axis=1)
        far = jnp.concatenate([two_h, two_l, two_h], axis=1)
        result.append((near, far))
    return result


def local(residual, step_ratio, forward_map, back_map, eigen_values):
    local_steps, planes, rows_x, rows_y = residual.shape
    depth = rows_x // 4
    count = lax.axis_size("tm")
    bits = (1, count // 2)
    all_bits = [1 << k for k in range(count.bit_length() - 1)]
    me = lax.axis_index("tm")
    sides = jnp.stack([jnp.where(jnp.bitwise_and(me, b) > 0, 1, 0) for b in bits]).astype(jnp.int32)
    ratio = (step_ratio.astype(jnp.float32) / 8.0)[:, None]

    def swap(data, bit):
        return lax.ppermute(data, "tm", [(i, i ^ bit) for i in range(count)])

    spaces = lax.axis_size("space")
    upward = [(i, i + 1) for i in range(spaces - 1)]
    downward = [(i + 1, i) for i in range(spaces - 1)]

    raws = spread(residual, ratio, sides, depth)
    maps = make_maps(forward_map, back_map, eigen_values, me, count, bits)

    held = [[None] * CUTS for _ in range(2)]
    for chunk in range(CUTS):
        for stream in range(2):
            keep, send = raws[stream][0][chunk], raws[stream][1][chunk]
            have = {0: keep, bits[stream]: swap(send, bits[stream])}
            for bit in all_bits:
                if bit != bits[stream]:
                    have.update({mask | bit: swap(have[mask], bit) for mask in list(have)})
            held[stream][chunk] = [have[mask] for mask in range(count)]

    parts = [[None] * CUTS for _ in range(2)]
    for chunk in range(CUTS):
        for stream in range(2):
            near, far = maps[stream]
            used = held[stream][max(chunk - 1, 0) : chunk + 1]
            own, send, down, up = apply(stream, chunk, depth, near, far, used)
            low = lax.ppermute(up, "space", upward)
            high = lax.ppermute(down, "space", downward)
            got = swap(add_far(send, low, high), bits[stream])
            parts[stream][chunk] = (own, low, high, got)

    flat = [parts[s][c] for s in range(2) for c in range(CUTS)]
    result = collect(flat, sides, depth, rows_x)
    return result.reshape(2, local_steps, planes, rows_x, rows_y)


def solution(mesh):
    in_specs = (P("tm", "space", None, None), P("tm"), P(), P(), P())
    out_specs = P(None, "tm", "space", None, None)
    return jax.shard_map(local, mesh=mesh, in_specs=in_specs, out_specs=out_specs, check_vma=False)
```

```python
import functools

import jax
import jax.numpy as jnp
from jax import lax
from jax.experimental import pallas as pl
from jax.experimental.pallas import tpu as pltpu
from jax.sharding import PartitionSpec as P


CUTS = 2
VMEM_LIMIT = 60 * 2**20


def block_row(stream, side, row, depth, rows_x):
    if stream == 0:
        return row + side * (rows_x - 1 - 2 * row)
    return depth * (1 + side) + row


def chunk_rows(stream, chunk, depth):
    high = depth // CUTS
    first = chunk * high + 1 if chunk else (0 if stream == 0 else -1)
    return list(range(first, (chunk + 1) * high + 1))


def spread_kernel(chunk, depth, planes, sides_ref, ratio_ref, in_ref, *outs):
    steps, _, rows_x, _ = in_ref.shape
    flat = in_ref.reshape(steps * planes * rows_x, in_ref.shape[3])
    ratio = ratio_ref[...]
    place = 0
    for stream in range(2):
        for other in range(2):
            side = sides_ref[stream] if other == 0 else 1 - sides_ref[stream]
            out = outs[place]
            place += 1
            for at, row in enumerate(chunk_rows(stream, chunk, depth)):
                x = block_row(stream, side, row, depth, rows_x)
                for z in range(planes):
                    part = flat[pl.ds(z * rows_x + x, steps, stride=planes * rows_x), :]
                    out[at, z] = part * ratio


def spread(chunk, residual, ratio, sides, depth):
    steps, planes, rows_x, rows_y = residual.shape
    lanes = 128
    block = min(steps, 32)
    shapes, specs = [], []
    for stream in range(2):
        for _ in range(2):
            count = len(chunk_rows(stream, chunk, depth))
            shapes.append(jax.ShapeDtypeStruct((count, planes, steps, rows_y), jnp.float32))
            specs.append(pl.BlockSpec((count, planes, block, lanes), lambda i, j: (0, 0, i, j)))
    outs = pl.pallas_call(
        functools.partial(spread_kernel, chunk, depth, planes),
        out_shape=shapes,
        grid=(steps // block, rows_y // lanes),
        in_specs=[
            pl.BlockSpec(memory_space=pltpu.SMEM),
            pl.BlockSpec((block, 1), lambda i, j: (i, 0)),
            pl.BlockSpec((block, planes, rows_x, lanes), lambda i, j: (i, 0, 0, j)),
        ],
        out_specs=specs,
        compiler_params=pltpu.CompilerParams(vmem_limit_bytes=VMEM_LIMIT),
        cost_estimate=pl.CostEstimate(flops=residual.size * 2, bytes_accessed=residual.size * 10, transcendentals=0),
        name="spread",
    )(sides, ratio, residual)
    return [outs[0:2], outs[2:4]]


def halves(value):
    high = value.astype(jnp.bfloat16)
    return high, (value - high.astype(jnp.float32)).astype(jnp.bfloat16)


def apply_kernel(stream, chunk, depth, planes, groups, near_ref, far_ref, *refs):
    outs = refs[-4:]
    raws = refs[:-4]
    count = len(raws) // groups
    own_ref, send_ref, down_ref, up_ref = outs
    rows_y = own_ref.shape[-1]
    where = {}
    for c in range(count):
        for at, row in enumerate(chunk_rows(stream, chunk - count + 1 + c, depth)):
            where[row] = (c, at)

    def load(row, z):
        if row not in where:
            return None
        c, at = where[row]
        return jnp.concatenate([raws[c * groups + g][at, z] for g in range(groups)], axis=0)

    near, far = near_ref[...], far_ref[...]
    half = near.shape[0] // 2
    high = depth // CUTS
    for at in range(high):
        row = chunk * high + at
        across = []
        for z in range(planes):
            mid = load(row, z)
            lane = lax.broadcasted_iota(jnp.int32, mid.shape, 1)
            total = jnp.where(lane == 0, 0.0, pltpu.roll(mid, 1, 1))
            total = total + jnp.where(lane == rows_y - 1, 0.0, pltpu.roll(mid, rows_y - 1, 1))
            for beside in (load(row - 1, z), load(row + 1, z)):
                if beside is not None:
                    total = total + beside
            mid_h, mid_l = halves(mid)
            sum_h, sum_l = halves(total)
            thick = jnp.concatenate([mid_h, mid_h, mid_l, sum_h, sum_h, sum_l], axis=0)
            thin = jnp.concatenate([mid_h, mid_h, mid_l], axis=0)
            value = jnp.dot(near, thick, preferred_element_type=jnp.float32)
            own_ref[at, z] = value[:half]
            send_ref[at, z] = value[half:]
            across.append(jnp.dot(far, thin, preferred_element_type=jnp.float32))
        down_ref[0, at] = across[0][:half]
        down_ref[1, at] = across[0][half:]
        up_ref[0, at] = across[-1][:half]
        up_ref[1, at] = across[-1][half:]
        for z in range(planes):
            for beside in across[max(z - 1, 0) : z] + across[z + 1 : z + 2]:
                own_ref[at, z] += beside[:half]
                send_ref[at, z] += beside[half:]


def apply(stream, chunk, depth, near, far, raws):
    groups = len(raws[0])
    _, planes, steps, rows_y = raws[0][0].shape
    high = depth // CUTS
    half = near.shape[0] // 2
    flat = [r for chunk_raws in raws for r in chunk_raws]
    shapes = [jax.ShapeDtypeStruct((high, planes, half, rows_y), jnp.float32)] * 2
    shapes += [jax.ShapeDtypeStruct((2, high, half, rows_y), jnp.float32)] * 2
    flops = 2 * high * planes * rows_y * (near.size + far.size)
    return pl.pallas_call(
        functools.partial(apply_kernel, stream, chunk, depth, planes, groups),
        out_shape=shapes,
        in_specs=[pl.BlockSpec(memory_space=pltpu.VMEM)] * (2 + len(flat)),
        out_specs=[pl.BlockSpec(memory_space=pltpu.VMEM)] * 4,
        compiler_params=pltpu.CompilerParams(vmem_limit_bytes=VMEM_LIMIT),
        cost_estimate=pl.CostEstimate(flops=flops, bytes_accessed=12 * 2**20, transcendentals=0),
        name="apply",
    )(near, far, *flat)


def add_kernel(send_ref, low_ref, high_ref, out_ref):
    planes = out_ref.shape[1]
    for z in range(planes):
        value = send_ref[:, z]
        if z == 0:
            value = value + low_ref[0]
        if z == planes - 1:
            value = value + high_ref[0]
        out_ref[:, z] = value


def add_far(send, low, high):
    count, planes, half, rows_y = send.shape
    return pl.pallas_call(
        add_kernel,
        out_shape=jax.ShapeDtypeStruct(send.shape, jnp.float32),
        grid=(count,),
        in_specs=[
            pl.BlockSpec((1, planes, half, rows_y), lambda i: (i, 0, 0, 0)),
            pl.BlockSpec((1, 1, half, rows_y), lambda i: (1, i, 0, 0)),
            pl.BlockSpec((1, 1, half, rows_y), lambda i: (1, i, 0, 0)),
        ],
        out_specs=pl.BlockSpec((1, planes, half, rows_y), lambda i: (i, 0, 0, 0)),
        compiler_params=pltpu.CompilerParams(vmem_limit_bytes=VMEM_LIMIT),
        cost_estimate=pl.CostEstimate(flops=send.size, bytes_accessed=send.size * 12, transcendentals=0),
        name="add_far",
    )(send, low, high)


def place_kernel(depth, other, sides_ref, *refs):
    out_ref = refs[-1]
    refs = refs[other:-1]
    each = 1 if other else 3
    count, planes, _, lanes = out_ref.shape
    flat = out_ref.reshape(count * planes * depth, lanes)
    high = depth // CUTS
    stream = pl.program_id(0)
    for which in range(2):

        @pl.when(stream == which)
        def _():
            side = 1 - sides_ref[which] if other else sides_ref[which]
            for chunk in range(CUTS):
                part = refs[(which * CUTS + chunk) * each : (which * CUTS + chunk + 1) * each]
                for at in range(high):
                    row = chunk * high + at
                    at_x = row if which else row + side * (depth - 1 - 2 * row)
                    for z in range(planes):
                        value = part[0][at, z]
                        if not other and z == 0:
                            value = value + part[1][0, at]
                        if not other and z == planes - 1:
                            value = value + part[2][0, at]
                        flat[pl.ds(z * depth + at_x, count, stride=planes * depth), :] = value


def place(parts, sides, depth, rows_x, result=None):
    high, planes, half, rows_y = parts[0][0].shape
    lanes = 128
    block = min(half, 64)
    other = int(result is not None)

    def cells(which):
        def index(s, i, j, sides):
            mine = (s == which).astype(jnp.int32)
            last_i, last_j = half // block - 1, rows_y // lanes - 1
            stay_i, stay_j = (last_i, last_j) if which == 0 else (0, 0)
            return (0, 0, mine * i + (1 - mine) * stay_i, mine * j + (1 - mine) * stay_j)

        return pl.BlockSpec((high, planes, block, lanes), index)

    def edge(which):
        def index(s, i, j, sides):
            return cells(which).index_map(s, i, j, sides)

        return pl.BlockSpec((1, high, block, lanes), index)

    def out_index(s, i, j, sides):
        side = 1 - sides[s] if other else sides[s]
        tile = s * (1 + side) + (1 - s) * 3 * side
        return (i, 0, tile, j)

    specs, flat = [], []
    for place_of, part in enumerate(parts):
        which = place_of // CUTS
        specs += [cells(which)] if other else [cells(which), edge(which), edge(which)]
        flat += list(part)
    first = [result] if other else []
    return pl.pallas_call(
        functools.partial(place_kernel, depth, other),
        out_shape=jax.ShapeDtypeStruct((half, planes, rows_x, rows_y), jnp.float32),
        grid_spec=pltpu.PrefetchScalarGridSpec(
            num_scalar_prefetch=1,
            grid=(2, half // block, rows_y // lanes),
            in_specs=[pl.BlockSpec(memory_space=pl.ANY)] * other + specs,
            out_specs=pl.BlockSpec((block, planes, depth, lanes), out_index),
        ),
        input_output_aliases={1: 0} if other else {},
        compiler_params=pltpu.CompilerParams(vmem_limit_bytes=VMEM_LIMIT),
        cost_estimate=pl.CostEstimate(flops=0, bytes_accessed=16 * 2**20, transcendentals=0),
        name="place_got" if other else "place_own",
    )(sides, *first, *flat)


def after(value, *others):
    return lax.optimization_barrier((value, *others))[0]


def make_maps(forward_map, back_map, eigen_values, me, count, bits):
    steps = forward_map.shape[1]
    local_steps = steps // count
    highest = lax.Precision.HIGHEST
    real_part = 6.0 + eigen_values[0]
    imag_part = eigen_values[1]
    denom = real_part * real_part + imag_part * imag_part
    coef_re = (real_part / denom)[:, None]
    coef_im = (-imag_part / denom)[:, None]
    order = jnp.bitwise_xor(me, jnp.arange(count))
    ahead = forward_map.reshape(2, steps, count, local_steps)
    ahead = jnp.take(ahead, order, axis=2).reshape(2, steps, steps)
    once_re = coef_re * ahead[0] - coef_im * ahead[1]
    once_im = coef_re * ahead[1] + coef_im * ahead[0]
    twice_re = coef_re * once_re - coef_im * once_im
    twice_im = coef_re * once_im + coef_im * once_re
    right = jnp.concatenate(
        [jnp.concatenate([once_re, twice_re], axis=1), jnp.concatenate([once_im, twice_im], axis=1)], axis=0
    )
    blocks = jnp.stack([me, jnp.bitwise_xor(me, bits[0]), jnp.bitwise_xor(me, bits[1])])
    back = jnp.take(back_map.reshape(2, count, local_steps, steps), blocks, axis=1)
    left_re = jnp.concatenate([back[0], -back[1]], axis=2)
    left_im = jnp.concatenate([back[1], back[0]], axis=2)
    left = jnp.stack([left_re, left_im], axis=1).reshape(3, 2 * local_steps, 2 * steps)
    maps = jnp.einsum("bmk,kn->bmn", left, right, precision=highest)
    maps = [jnp.concatenate([maps[0], maps[1 + s]], axis=0) for s in range(2)]
    result = []
    for both in maps:
        one_h, one_l = halves(both[:, :steps])
        two_h, two_l = halves(both[:, steps:])
        near = jnp.concatenate([one_h, one_l, one_h, two_h, two_l, two_h], axis=1)
        far = jnp.concatenate([two_h, two_l, two_h], axis=1)
        result.append((near, far))
    return result


def local(residual, step_ratio, forward_map, back_map, eigen_values):
    local_steps, planes, rows_x, rows_y = residual.shape
    depth = rows_x // 4
    count = lax.axis_size("tm")
    bits = (1, count // 2)
    all_bits = [1 << k for k in range(count.bit_length() - 1)]
    me = lax.axis_index("tm")
    sides = jnp.stack([jnp.where(jnp.bitwise_and(me, b) > 0, 1, 0) for b in bits]).astype(jnp.int32)
    ratio = (step_ratio.astype(jnp.float32) / 8.0)[:, None]

    def swap(data, bit):
        return lax.ppermute(data, "tm", [(i, i ^ bit) for i in range(count)])

    spaces = lax.axis_size("space")
    upward = [(i, i + 1) for i in range(spaces - 1)]
    downward = [(i + 1, i) for i in range(spaces - 1)]

    maps = make_maps(forward_map, back_map, eigen_values, me, count, bits)

    queues = [[], []]

    def swap_in_turn(data, bit):
        queue = queues[0 if bit == bits[0] else 1]
        if len(queue) > 1:
            data = after(data, queue[-2])
        got = swap(data, bit)
        queue.append(got)
        return got

    held = [[None] * CUTS for _ in range(2)]
    parts = [[None] * CUTS for _ in range(2)]

    def raw(chunk):
        raws = spread(chunk, residual, ratio, sides, depth)
        have = [{0: raws[s][0], bits[s]: swap_in_turn(raws[s][1], bits[s])} for s in range(2)]
        for bit in all_bits:
            for mask in range(count):
                for stream in (1, 0):
                    now = have[stream]
                    free = bit != bits[stream] and not mask & bit
                    if free and mask in now and (mask | bit) not in now:
                        now[mask | bit] = swap_in_turn(now[mask], bit)
        for stream in range(2):
            held[stream][chunk] = [have[stream][mask] for mask in range(count)]

    def products(chunk):
        for stream in range(2):
            near, far = maps[stream]
            used = held[stream][max(chunk - 1, 0) : chunk + 1]
            own, send, down, up = apply(stream, chunk, depth, near, far, used)
            low = lax.ppermute(up, "space", upward)
            high = lax.ppermute(down, "space", downward)
            parts[stream][chunk] = [own, low, high, add_far(send, low, high)]

    def give(chunk):
        for stream in range(2):
            parts[stream][chunk][3] = swap_in_turn(parts[stream][chunk][3], bits[stream])

    for chunk in range(CUTS):
        raw(chunk)
        products(chunk)
    for chunk in range(CUTS):
        give(chunk)

    flat = [parts[s][c] for s in range(2) for c in range(CUTS)]
    result = place([p[:3] for p in flat], sides, depth, rows_x)
    result = place([p[3:] for p in flat], sides, depth, rows_x, result)
    return result.reshape(2, local_steps, planes, rows_x, rows_y)


def solution(mesh):
    in_specs = (P("tm", "space", None, None), P("tm"), P(), P(), P())
    out_specs = P(None, "tm", "space", None, None)
    return jax.shard_map(local, mesh=mesh, in_specs=in_specs, out_specs=out_specs, check_vma=False)
```

```python
import functools

import jax
import jax.numpy as jnp
from jax import lax
from jax.experimental import pallas as pl
from jax.experimental.pallas import tpu as pltpu
from jax.sharding import PartitionSpec as P


CUTS = 2
VMEM_LIMIT = 28 * 2**20
HBM = pl.BlockSpec(memory_space=pl.ANY)
SCALARS = pl.BlockSpec(memory_space=pltpu.SMEM)
LIGHT = pl.CostEstimate(flops=1024, bytes_accessed=4096, transcendentals=0)
HEAVY = pl.CostEstimate(flops=2**33, bytes_accessed=2**25, transcendentals=0)
PARAMS = pltpu.CompilerParams(vmem_limit_bytes=4 * 2**20)


def block_row(stream, side, row, depth, rows_x):
    if stream == 0:
        return row + side * (rows_x - 1 - 2 * row)
    return depth * (1 + side) + row


def own_rows(chunk, depth):
    high = depth // CUTS
    return list(range(chunk * high, (chunk + 1) * high))


def chunk_rows(stream, chunk, depth):
    rows = own_rows(chunk, depth)
    first = rows[0] + 1 if chunk else (0 if stream == 0 else -1)
    return list(range(first, rows[-1] + 2))


def where_rows(stream, chunk, depth):
    places = {}
    for back in (1, 0):
        if chunk >= back:
            for at, row in enumerate(chunk_rows(stream, chunk - back, depth)):
                places[row] = (1 - back, at)
    return places


def run(copies):
    for copy in copies:
        copy.start()
    for copy in copies:
        copy.wait()


def pick_kernel(chunk, depth, sides_ref, in_ref, *refs):
    outs, sems = refs[:-1], refs[-1]
    _, planes, rows_x, _ = in_ref.shape
    copies = []
    for stream in range(2):
        for other in range(2):
            side = 1 - sides_ref[stream] if other else sides_ref[stream]
            for at, row in enumerate(chunk_rows(stream, chunk, depth)):
                x = block_row(stream, side, row, depth, rows_x)
                for z in range(planes):
                    out = outs[2 * stream + other].at[at, z]
                    copies.append(pltpu.make_async_copy(in_ref.at[:, z, x], out, sems.at[len(copies)]))
    run(copies)


def pick(chunk, residual, sides, depth):
    steps, planes, _, rows_y = residual.shape
    counts = [len(chunk_rows(stream, chunk, depth)) for stream in (0, 0, 1, 1)]
    outs = pl.pallas_call(
        functools.partial(pick_kernel, chunk, depth),
        out_shape=[jax.ShapeDtypeStruct((c, planes, steps, rows_y), jnp.float32) for c in counts],
        in_specs=[SCALARS, HBM],
        out_specs=[HBM] * 4,
        scratch_shapes=[pltpu.SemaphoreType.DMA((sum(counts) * planes,))],
        compiler_params=PARAMS,
        cost_estimate=LIGHT,
        name="pick",
    )(sides, residual)
    return [outs[0:2], outs[2:4]]


def edge_kernel(chunk, depth, groups, *refs):
    raws, (up_ref, down_ref, sems) = refs[:-3], refs[-3:]
    planes = raws[0].shape[1]
    backs = 2 if chunk else 1
    copies = []
    for stream in range(2):
        places = where_rows(stream, chunk, depth)
        for at, row in enumerate(own_rows(chunk, depth)):
            back, index = places[row]
            for group in range(groups):
                raw = raws[(stream * backs + back - 2 + backs) * groups + group]
                for z, out in ((planes - 1, up_ref), (0, down_ref)):
                    copy = pltpu.make_async_copy(
                        raw.at[index, z], out.at[stream, at, group], sems.at[len(copies)]
                    )
                    copies.append(copy)
    run(copies)


def edges(chunk, depth, raws):
    groups = len(raws[0][0])
    _, _, steps, rows_y = raws[0][0][0].shape
    flat = [raw for stream in raws for arrays in stream for raw in arrays]
    high = depth // CUTS
    shape = jax.ShapeDtypeStruct((2, high, groups, steps, rows_y), jnp.float32)
    return pl.pallas_call(
        functools.partial(edge_kernel, chunk, depth, groups),
        out_shape=[shape] * 2,
        in_specs=[HBM] * len(flat),
        out_specs=[HBM] * 2,
        scratch_shapes=[pltpu.SemaphoreType.DMA((4 * high * groups,))],
        compiler_params=PARAMS,
        cost_estimate=LIGHT,
        name="edges",
    )(*flat)


def halves(value):
    high = value.astype(jnp.bfloat16)
    return high, (value - high.astype(jnp.float32)).astype(jnp.bfloat16)


def map_halves(value):
    high = lax.reduce_precision(value, exponent_bits=8, mantissa_bits=7)
    return high.astype(jnp.bfloat16), (value - high).astype(jnp.bfloat16)


def apply_kernel(chunk, depth, order, sides_ref, map_a_ref, map_b_ref, *refs):
    refs = list(refs)
    early_low, early_high, late_low, late_high = refs[:4]
    out_ref, gives = refs[-11], refs[-10:-8]
    cells, low_cells, high_cells, own, give, raw_sems, edge_sems, out_sems = refs[-8:]
    raws = refs[4:-11]
    if chunk:
        raws = raws[:-1]
    groups = len(order[0][0]) + len(order[0][1])
    backs = 2 if chunk else 1
    _, planes, rows_x, rows_y = out_ref.shape
    steps = cells.shape[2] // groups
    high = depth // CUTS
    loads, edge_loads, slots = [{}, {}], [{}, {}], [{}, {}]
    slot = 0
    number = 0
    for stream in range(2):
        places = where_rows(stream, chunk, depth)
        rows = own_rows(chunk, depth)
        for row in range(rows[0] - 1, rows[-1] + 2):
            if row in places:
                back, index = places[row]
                copies = []
                for group in range(groups):
                    raw = raws[(stream * backs + back - 2 + backs) * groups + group]
                    span = pl.ds(group * steps, steps)
                    copies.append(
                        pltpu.make_async_copy(raw.at[index], cells.at[slot, :, span], raw_sems.at[slot, group])
                    )
                loads[stream][row] = copies
                slots[stream][row] = slot
                slot += 1
            if row in rows:
                at = row - rows[0]
                copies = []
                for kind, (low, up) in enumerate(((early_low, early_high), (late_low, late_high))):
                    for place, group in enumerate(order[stream][kind]):
                        span = pl.ds(group * steps, steps)
                        for way, (source, target) in enumerate(((low, low_cells), (up, high_cells))):
                            copies.append(
                                pltpu.make_async_copy(
                                    source.at[stream, at, place],
                                    target.at[number, span],
                                    edge_sems.at[number, group, way],
                                )
                            )
                edge_loads[stream][row] = (number, copies)
                number += 1
    for stream in range(2):
        for row in sorted(loads[stream]):
            for copy in loads[stream][row]:
                copy.start()
            if row in edge_loads[stream]:
                for copy in edge_loads[stream][row][1]:
                    copy.start()

    stores = []
    for stream in range(2):
        maps = (map_a_ref, map_b_ref)[stream][...]
        half = maps.shape[0] // 2
        waited = set()
        for at, row in enumerate(own_rows(chunk, depth)):
            for beside in (row - 1, row, row + 1):
                if beside in loads[stream] and beside not in waited:
                    waited.add(beside)
                    for copy in loads[stream][beside]:
                        copy.wait()
            number, copies = edge_loads[stream][row]
            for copy in copies:
                copy.wait()
            x = block_row(stream, sides_ref[stream], row, depth, rows_x)
            for z in range(planes):
                mid = cells[slots[stream][row], z]
                lane = lax.broadcasted_iota(jnp.int32, mid.shape, 1)
                total = jnp.where(lane == 0, 0.0, pltpu.roll(mid, 1, 1))
                total = total + jnp.where(lane == rows_y - 1, 0.0, pltpu.roll(mid, rows_y - 1, 1))
                for beside in (row - 1, row + 1):
                    if beside in slots[stream]:
                        total = total + cells[slots[stream][beside], z]
                total = total + (cells[slots[stream][row], z - 1] if z else low_cells[number])
                total = total + (
                    cells[slots[stream][row], z + 1] if z < planes - 1 else high_cells[number]
                )
                mid_h, mid_l = halves(mid)
                sum_h, sum_l = halves(total)
                stack = jnp.concatenate([mid_h, mid_h, mid_l, sum_h, sum_h, sum_l], axis=0)
                value = jnp.dot(maps, stack, preferred_element_type=jnp.float32)
                own[number, z] = value[:half]
                give[number, z] = value[half:]
                stores.append(
                    pltpu.make_async_copy(own.at[number, z], out_ref.at[:, z, x], out_sems.at[number, z])
                )
                stores[-1].start()
            stores.append(
                pltpu.make_async_copy(give.at[number], gives[stream].at[at], out_sems.at[number, planes])
            )
            stores[-1].start()
    for copy in stores:
        copy.wait()


def apply(chunk, depth, order, sides, maps, early, late, raws, shape, result):
    groups = len(raws[0][0])
    _, planes, steps, rows_y = raws[0][0][0].shape
    high = depth // CUTS
    half = shape[0]
    flat = [raw for stream in raws for arrays in stream for raw in arrays]
    first = [] if result is None else [result]
    give = jax.ShapeDtypeStruct((high, planes, half, rows_y), jnp.float32)
    total = groups * steps
    slots = sum(len([r for r in range(-1 + chunk * high, (chunk + 1) * high + 1) if s or r >= 0]) for s in range(2))
    vmem = pl.BlockSpec(memory_space=pltpu.VMEM)
    count = 3 + 4 + len(flat)
    return pl.pallas_call(
        functools.partial(apply_kernel, chunk, depth, order),
        out_shape=[jax.ShapeDtypeStruct(shape, jnp.float32), give, give],
        in_specs=[SCALARS, vmem, vmem] + [HBM] * (4 + len(flat) + len(first)),
        out_specs=[HBM] * 3,
        scratch_shapes=[
            pltpu.VMEM((slots, planes, total, rows_y), jnp.float32),
            pltpu.VMEM((2 * high, total, rows_y), jnp.float32),
            pltpu.VMEM((2 * high, total, rows_y), jnp.float32),
            pltpu.VMEM((2 * high, planes, half, rows_y), jnp.float32),
            pltpu.VMEM((2 * high, planes, half, rows_y), jnp.float32),
            pltpu.SemaphoreType.DMA((slots, groups)),
            pltpu.SemaphoreType.DMA((2 * high, groups, 2)),
            pltpu.SemaphoreType.DMA((2 * high, planes + 1)),
        ],
        input_output_aliases={count: 0} if first else {},
        compiler_params=pltpu.CompilerParams(vmem_limit_bytes=VMEM_LIMIT),
        cost_estimate=HEAVY,
        name="apply",
    )(sides, *maps, *early, *late, *flat, *first)


def place_kernel(chunk, depth, sides_ref, got_a, got_b, _, out_ref, sems):
    _, planes, rows_x, _ = out_ref.shape
    copies = []
    for stream, got in enumerate((got_a, got_b)):
        for at, row in enumerate(own_rows(chunk, depth)):
            x = block_row(stream, 1 - sides_ref[stream], row, depth, rows_x)
            for z in range(planes):
                copies.append(pltpu.make_async_copy(got.at[at, z], out_ref.at[:, z, x], sems.at[len(copies)]))
    run(copies)


def place(chunk, depth, sides, got, result):
    planes = result.shape[1]
    return pl.pallas_call(
        functools.partial(place_kernel, chunk, depth),
        out_shape=jax.ShapeDtypeStruct(result.shape, jnp.float32),
        in_specs=[SCALARS] + [HBM] * 3,
        out_specs=HBM,
        scratch_shapes=[pltpu.SemaphoreType.DMA((2 * depth // CUTS * planes,))],
        input_output_aliases={3: 0},
        compiler_params=PARAMS,
        cost_estimate=LIGHT,
        name="place",
    )(sides, *got, result)


def after(value, *others):
    return lax.optimization_barrier((value, *others))[0]


def make_maps(forward_map, back_map, eigen_values, ratio, me, count, bits):
    steps = forward_map.shape[1]
    local_steps = steps // count
    highest = lax.Precision.HIGHEST
    real_part = 6.0 + eigen_values[0]
    imag_part = eigen_values[1]
    denom = real_part * real_part + imag_part * imag_part
    coef_re = (real_part / denom)[:, None]
    coef_im = (-imag_part / denom)[:, None]
    order = jnp.bitwise_xor(me, jnp.arange(count))
    ahead = (forward_map * ratio).reshape(2, steps, count, local_steps)
    ahead = jnp.take(ahead, order, axis=2).reshape(2, steps, steps)
    once_re = coef_re * ahead[0] - coef_im * ahead[1]
    once_im = coef_re * ahead[1] + coef_im * ahead[0]
    twice_re = coef_re * once_re - coef_im * once_im
    twice_im = coef_re * once_im + coef_im * once_re
    right = jnp.concatenate(
        [jnp.concatenate([once_re, twice_re], axis=1), jnp.concatenate([once_im, twice_im], axis=1)], axis=0
    )
    blocks = jnp.stack([me, jnp.bitwise_xor(me, bits[0]), jnp.bitwise_xor(me, bits[1])])
    back = jnp.take(back_map.reshape(2, count, local_steps, steps), blocks, axis=1)
    left_re = jnp.concatenate([back[0], -back[1]], axis=2)
    left_im = jnp.concatenate([back[1], back[0]], axis=2)
    left = jnp.stack([left_re, left_im], axis=1).reshape(3, 2 * local_steps, 2 * steps)
    maps = jnp.einsum("bmk,kn->bmn", left, right, precision=highest)
    result = []
    for other in (1, 2):
        both = jnp.concatenate([maps[0], maps[other]], axis=0)
        one_h, one_l = map_halves(both[:, :steps])
        two_h, two_l = map_halves(both[:, steps:])
        result.append(jnp.concatenate([one_h, one_l, one_h, two_h, two_l, two_h], axis=1))
    return result


def local(residual, step_ratio, forward_map, back_map, eigen_values):
    local_steps, planes, rows_x, rows_y = residual.shape
    depth = rows_x // 4
    count = lax.axis_size("tm")
    bits = (1, count // 2)
    all_bits = [1 << k for k in range(count.bit_length() - 1)]
    me = lax.axis_index("tm")
    sides = jnp.stack([jnp.where(jnp.bitwise_and(me, b) > 0, 1, 0) for b in bits]).astype(jnp.int32)
    ratio = lax.all_gather(step_ratio, "tm", tiled=True).astype(jnp.float32) / 8.0

    def swap(data, bit):
        return lax.ppermute(data, "tm", [(i, i ^ bit) for i in range(count)])

    spaces = lax.axis_size("space")
    upward = [(i, i + 1) for i in range(spaces - 1)]
    downward = [(i + 1, i) for i in range(spaces - 1)]

    queues = [[], []]

    def swap_in_turn(data, bit, *others, flight=2):
        queue = queues[0 if bit == bits[0] else 1]
        if len(queue) >= flight:
            others = (queue[-flight], *others)
        if others:
            data = after(data, *others)
        got = swap(data, bit)
        queue.append(got)
        return got

    masks = range(count)
    order = [[[m for m in masks if m in (0, b)], [m for m in masks if m not in (0, b)]] for b in bits]
    held = [[None] * CUTS for _ in range(2)]

    maps = make_maps(forward_map, back_map, eigen_values, ratio, me, count, bits)
    firsts = []

    def raw(chunk):
        data = after(residual, *firsts[-1]) if firsts else residual
        mine = pick(chunk, data, sides, depth)
        have = [{0: mine[s][0], bits[s]: swap_in_turn(mine[s][1], bits[s])} for s in range(2)]
        firsts.append([have[s][bits[s]] for s in range(2)])
        for bit in all_bits:
            for mask in masks:
                for stream in (1, 0):
                    now = have[stream]
                    free = bit != bits[stream] and not mask & bit
                    if free and mask in now and (mask | bit) not in now:
                        others = maps if mask and chunk == 0 else []
                        now[mask | bit] = swap_in_turn(now[mask], bit, *others)
        for stream in range(2):
            held[stream][chunk] = [have[stream][mask] for mask in masks]

    def beside(chunk, kind, *others):
        arrays = [
            [[a[m] for m in order[s][kind]] for a in held[s][max(chunk - 1, 0) : chunk + 1]] for s in range(2)
        ]
        if others:
            arrays[0][-1][0] = after(arrays[0][-1][0], *others)
        up, down = edges(chunk, depth, arrays)
        return lax.ppermute(up, "space", upward), lax.ppermute(down, "space", downward)

    gives = []
    result = None
    for chunk in range(CUTS):
        raw(chunk)
    shape = (2 * local_steps, planes, rows_x, rows_y)
    for chunk in range(CUTS):
        early = beside(chunk, 0, *(gives[-1] if gives else []))
        late = beside(chunk, 1, *early)
        if chunk + 1 < CUTS:
            late = [after(a, *firsts[chunk + 1]) for a in late]
        used = [held[s][max(chunk - 1, 0) : chunk + 1] for s in range(2)]
        result, *give = apply(chunk, depth, order, sides, maps, early, late, used, shape, result)
        gives.append(give)
    for chunk in range(CUTS):
        flight = 1 if chunk else 2
        got = [swap_in_turn(gives[chunk][s], bits[s], flight=flight) for s in range(2)]
        result = place(chunk, depth, sides, got, result)
    return result.reshape(2, local_steps, planes, rows_x, rows_y)


def solution(mesh):
    in_specs = (P("tm", "space", None, None), P("tm"), P(), P(), P())
    out_specs = P(None, "tm", "space", None, None)
    return jax.shard_map(local, mesh=mesh, in_specs=in_specs, out_specs=out_specs, check_vma=False)
```

```python
import functools

import jax
import jax.numpy as jnp
from jax import lax
from jax.experimental import pallas as pl
from jax.experimental.pallas import tpu as pltpu
from jax.sharding import PartitionSpec as P


CUTS = 2
VMEM_LIMIT = 28 * 2**20
HBM = pl.BlockSpec(memory_space=pl.ANY)
VMEM = pl.BlockSpec(memory_space=pltpu.VMEM)
SCALARS = pl.BlockSpec(memory_space=pltpu.SMEM)
LIGHT = pl.CostEstimate(flops=1024, bytes_accessed=4096, transcendentals=0)
PARAMS = pltpu.CompilerParams(vmem_limit_bytes=4 * 2**20)


def block_row(stream, side, row, depth, rows_x):
    if stream == 0:
        return row + side * (rows_x - 1 - 2 * row)
    return depth * (1 + side) + row


def own_rows(chunk, depth):
    high = depth // CUTS
    return list(range(chunk * high, (chunk + 1) * high))


def chunk_rows(stream, chunk, depth):
    rows = own_rows(chunk, depth)
    first = rows[0] + 1 if chunk else (0 if stream == 0 else -1)
    return list(range(first, rows[-1] + 2))


def where_rows(stream, chunk, depth):
    places = {}
    for back in (1, 0):
        if chunk >= back:
            for at, row in enumerate(chunk_rows(stream, chunk - back, depth)):
                places[row] = (1 - back, at)
    return places


def run(copies):
    for copy in copies:
        copy.start()
    for copy in copies:
        copy.wait()


def pick_kernel(chunk, depth, sides_ref, ratio_ref, in_ref, *refs):
    outs, sems = refs[:-1], refs[-1]
    _, planes, rows_x, _ = in_ref.shape
    jobs = []
    for stream in range(2):
        for other in (1, 0):
            side = 1 - sides_ref[stream] if other else sides_ref[stream]
            for at, row in enumerate(chunk_rows(stream, chunk, depth)):
                x = block_row(stream, side, row, depth, rows_x)
                for z in range(planes):
                    out = outs[2 * stream + other].at[at, z]
                    jobs.append((pltpu.make_async_copy(in_ref.at[:, z, x], out, sems.at[len(jobs)]), out))
    for copy, _ in jobs:
        copy.start()
    ratio = ratio_ref[...]
    for copy, out in jobs:
        copy.wait()
        out[...] = out[...] * ratio


def pick(chunk, residual, ratio, sides, depth):
    steps, planes, _, rows_y = residual.shape
    counts = [len(chunk_rows(stream, chunk, depth)) for stream in (0, 0, 1, 1)]
    outs = pl.pallas_call(
        functools.partial(pick_kernel, chunk, depth),
        out_shape=[jax.ShapeDtypeStruct((c, planes, steps, rows_y), jnp.float32) for c in counts],
        in_specs=[SCALARS, VMEM, HBM],
        out_specs=[VMEM] * 4,
        scratch_shapes=[pltpu.SemaphoreType.DMA((sum(counts) * planes,))],
        compiler_params=pltpu.CompilerParams(vmem_limit_bytes=56 * 2**20),
        cost_estimate=LIGHT,
        name="pick",
    )(sides, ratio, residual)
    return [outs[0:2], outs[2:4]]


def edge_kernel(chunk, depth, groups, *refs):
    raws, (up_ref, down_ref, sems) = refs[:-3], refs[-3:]
    planes = raws[0].shape[1]
    backs = 2 if chunk else 1
    copies = []
    for stream in range(2):
        places = where_rows(stream, chunk, depth)
        for at, row in enumerate(own_rows(chunk, depth)):
            back, index = places[row]
            for group in range(groups):
                raw = raws[(stream * backs + back - 2 + backs) * groups + group]
                for z, out in ((planes - 1, up_ref), (0, down_ref)):
                    copy = pltpu.make_async_copy(
                        raw.at[index, z], out.at[stream, at, group], sems.at[len(copies)]
                    )
                    copies.append(copy)
    run(copies)


def edges(chunk, depth, raws):
    groups = len(raws[0][0])
    _, _, steps, rows_y = raws[0][0][0].shape
    flat = [raw for stream in raws for arrays in stream for raw in arrays]
    high = depth // CUTS
    shape = jax.ShapeDtypeStruct((2, high, groups, steps, rows_y), jnp.float32)
    return pl.pallas_call(
        functools.partial(edge_kernel, chunk, depth, groups),
        out_shape=[shape] * 2,
        in_specs=[HBM] * len(flat),
        out_specs=[HBM] * 2,
        scratch_shapes=[pltpu.SemaphoreType.DMA((4 * high * groups,))],
        compiler_params=PARAMS,
        cost_estimate=LIGHT,
        name="edges",
    )(*flat)


def halves(value):
    high = value.astype(jnp.bfloat16)
    return high, (value - high.astype(jnp.float32)).astype(jnp.bfloat16)


def apply_kernel(chunk, depth, order, sides_ref, map_a_ref, map_b_ref, *refs):
    (early_low, early_high, late_low, late_high), raws = refs[:4], refs[4:-5]
    out_ref, gives, own, sems = refs[-5], refs[-4:-2], refs[-2], refs[-1]
    groups = sum(len(part) for part in order[0])
    backs = 2 if chunk else 1
    _, planes, rows_x, rows_y = out_ref.shape
    stores = []
    for stream in range(2):
        maps = (map_a_ref, map_b_ref)[stream][...]
        half = maps.shape[0] // 2
        places = where_rows(stream, chunk, depth)

        def load(row, z):
            back, index = places[row]
            start = (stream * backs + back - 2 + backs) * groups
            return jnp.concatenate([raw[index, z] for raw in raws[start : start + groups]], axis=0)

        def outside(early, late, at):
            parts = {}
            for kind, ref in enumerate((early, late)):
                for place, group in enumerate(order[stream][kind]):
                    parts[group] = ref[stream, at, place]
            return jnp.concatenate([parts[group] for group in range(groups)], axis=0)

        for at, row in enumerate(own_rows(chunk, depth)):
            number = stream * (depth // CUTS) + at
            x = block_row(stream, sides_ref[stream], row, depth, rows_x)
            mids = [load(row, z) for z in range(planes)]
            for z, mid in enumerate(mids):
                lane = lax.broadcasted_iota(jnp.int32, mid.shape, 1)
                total = jnp.where(lane == 0, 0.0, pltpu.roll(mid, 1, 1))
                total = total + jnp.where(lane == rows_y - 1, 0.0, pltpu.roll(mid, rows_y - 1, 1))
                for beside in (row - 1, row + 1):
                    if beside in places:
                        total = total + load(beside, z)
                total = total + (mids[z - 1] if z else outside(early_low, late_low, at))
                total = total + (mids[z + 1] if z < planes - 1 else outside(early_high, late_high, at))
                mid_h, mid_l = halves(mid)
                sum_h, sum_l = halves(total)
                stack = jnp.concatenate([mid_h, mid_h, mid_l, sum_h, sum_h, sum_l], axis=0)
                value = jnp.dot(maps, stack, preferred_element_type=jnp.float32)
                own[number, z] = value[:half]
                gives[stream][at, z] = value[half:]
                store = pltpu.make_async_copy(own.at[number, z], out_ref.at[:, z, x], sems.at[number, z])
                store.start()
                stores.append(store)
    for store in stores:
        store.wait()


def apply(chunk, depth, order, sides, maps, early, late, raws, shape, result):
    _, planes, _, rows_y = raws[0][0][0].shape
    high = depth // CUTS
    half = shape[0]
    flat = [raw for stream in raws for arrays in stream for raw in arrays]
    first = [] if result is None else [result]
    give = jax.ShapeDtypeStruct((high, planes, half, rows_y), jnp.float32)
    count = 3 + 4 + len(flat)

    def body(*refs):
        refs = refs[:count] + refs[count + len(first) :]
        apply_kernel(chunk, depth, order, *refs)

    return pl.pallas_call(
        body,
        out_shape=[jax.ShapeDtypeStruct(shape, jnp.float32), give, give],
        in_specs=[SCALARS] + [VMEM] * (count - 1) + [HBM] * len(first),
        out_specs=[HBM, VMEM, VMEM],
        scratch_shapes=[
            pltpu.VMEM((2 * high, planes, half, rows_y), jnp.float32),
            pltpu.SemaphoreType.DMA((2 * high, planes)),
        ],
        input_output_aliases={count: 0} if first else {},
        compiler_params=pltpu.CompilerParams(vmem_limit_bytes=VMEM_LIMIT),
        cost_estimate=LIGHT,
        name="apply",
    )(sides, *maps, *early, *late, *flat, *first)


def place_kernel(chunk, depth, sides_ref, got_a, got_b, _, out_ref, sems):
    _, planes, rows_x, _ = out_ref.shape
    copies = []
    for stream, got in enumerate((got_a, got_b)):
        for at, row in enumerate(own_rows(chunk, depth)):
            x = block_row(stream, 1 - sides_ref[stream], row, depth, rows_x)
            for z in range(planes):
                copies.append(pltpu.make_async_copy(got.at[at, z], out_ref.at[:, z, x], sems.at[len(copies)]))
    run(copies)


def place(chunk, depth, sides, got, result):
    planes = result.shape[1]
    return pl.pallas_call(
        functools.partial(place_kernel, chunk, depth),
        out_shape=jax.ShapeDtypeStruct(result.shape, jnp.float32),
        in_specs=[SCALARS] + [HBM] * 3,
        out_specs=HBM,
        scratch_shapes=[pltpu.SemaphoreType.DMA((2 * depth // CUTS * planes,))],
        input_output_aliases={3: 0},
        compiler_params=PARAMS,
        cost_estimate=LIGHT,
        name="place",
    )(sides, *got, result)


def after(value, *others):
    return lax.optimization_barrier((value, *others))[0]


def maps_kernel(bits, me_ref, ahead_ref, back_ref, eigen_ref, *outs):
    steps = ahead_ref.shape[1]
    local_steps = outs[0].shape[0] // 4
    me = me_ref[0]
    real_part = 6.0 + eigen_ref[0:1, :]
    imag_part = eigen_ref[1:2, :]
    denom = real_part * real_part + imag_part * imag_part
    coef_re = real_part / denom
    coef_im = -imag_part / denom
    left = []
    for block in (me, jnp.bitwise_xor(me, bits[0]), jnp.bitwise_xor(me, bits[1])):
        span = pl.ds(pl.multiple_of(block * local_steps, local_steps), local_steps)
        back_re, back_im = back_ref[0, span, :], back_ref[1, span, :]
        for _ in range(2):
            back_re, back_im = back_re * coef_re - back_im * coef_im, back_re * coef_im + back_im * coef_re
            left += [back_re, back_im]
    left = jnp.concatenate(left, axis=0)
    by_re = jnp.dot(left, ahead_ref[0], precision=lax.Precision.HIGHEST, preferred_element_type=jnp.float32)
    by_im = jnp.dot(left, ahead_ref[1], precision=lax.Precision.HIGHEST, preferred_element_type=jnp.float32)

    def piece(data, which):
        return data[which * local_steps : (which + 1) * local_steps]

    row = lax.broadcasted_iota(jnp.int32, (steps, steps), 0)
    column = lax.broadcasted_iota(jnp.int32, (steps, steps), 1)
    turn = (row == jnp.bitwise_xor(column, me * local_steps)).astype(jnp.float32).astype(jnp.bfloat16)
    parts = []
    for block in range(3):
        for power in range(2):
            at = 2 * (2 * block + power)
            both = jnp.concatenate(
                [piece(by_re, at) - piece(by_im, at + 1), piece(by_im, at) + piece(by_re, at + 1)], axis=0
            )
            pair = jnp.concatenate(halves(both), axis=0)
            parts.append(jnp.dot(pair, turn, preferred_element_type=jnp.float32).astype(jnp.bfloat16))
    half = 2 * local_steps
    for out, blocks in zip(outs, ((0, 1), (0, 2))):
        for place, block in enumerate(blocks):
            once, twice = parts[2 * block], parts[2 * block + 1]
            columns = (once[:half], once[half:], once[:half], twice[:half], twice[half:], twice[:half])
            for c, value in enumerate(columns):
                out[place * half : (place + 1) * half, c * steps : (c + 1) * steps] = value


def make_maps(forward_map, back_map, eigen_values, me, count, bits):
    steps = forward_map.shape[1]
    shape = jax.ShapeDtypeStruct((4 * steps // count, 6 * steps), jnp.bfloat16)
    return pl.pallas_call(
        functools.partial(maps_kernel, bits),
        out_shape=[shape, shape],
        in_specs=[SCALARS] + [VMEM] * 3,
        out_specs=[VMEM] * 2,
        compiler_params=pltpu.CompilerParams(vmem_limit_bytes=VMEM_LIMIT),
        cost_estimate=LIGHT,
        name="maps",
    )(me.astype(jnp.int32).reshape(1), forward_map, back_map, eigen_values)


def local(residual, step_ratio, forward_map, back_map, eigen_values):
    local_steps, planes, rows_x, rows_y = residual.shape
    depth = rows_x // 4
    count = lax.axis_size("tm")
    bits = (1, count // 2)
    all_bits = [1 << k for k in range(count.bit_length() - 1)]
    me = lax.axis_index("tm")
    sides = jnp.stack([jnp.where(jnp.bitwise_and(me, b) > 0, 1, 0) for b in bits]).astype(jnp.int32)
    ratio = jnp.broadcast_to((step_ratio.astype(jnp.float32) / 8.0)[:, None], (local_steps, rows_y))

    def swap(data, bit):
        return lax.ppermute(data, "tm", [(i, i ^ bit) for i in range(count)])

    spaces = lax.axis_size("space")
    upward = [(i, i + 1) for i in range(spaces - 1)]
    downward = [(i + 1, i) for i in range(spaces - 1)]

    queues = [[], []]

    def swap_in_turn(data, bit, *others, flight=2):
        queue = queues[0 if bit == bits[0] else 1]
        if len(queue) >= flight:
            others = (queue[-flight], *others)
        if others:
            data = after(data, *others)
        got = swap(data, bit)
        queue.append(got)
        return got

    masks = range(count)
    order = [[[m for m in masks if m in (0, b)], [m for m in masks if m not in (0, b)]] for b in bits]
    held = [[None] * CUTS for _ in range(2)]

    maps = make_maps(forward_map, back_map, eigen_values, me, count, bits)
    firsts = []

    def raw(chunk):
        data = after(residual, *firsts[-1]) if firsts else residual
        mine = pick(chunk, data, ratio, sides, depth)
        have = [{0: mine[s][0], bits[s]: swap_in_turn(mine[s][1], bits[s])} for s in range(2)]
        firsts.append([have[s][bits[s]] for s in range(2)])
        for bit in all_bits:
            for mask in masks:
                for stream in (1, 0):
                    now = have[stream]
                    free = bit != bits[stream] and not mask & bit
                    if free and mask in now and (mask | bit) not in now:
                        others = maps if mask and chunk == 0 else []
                        now[mask | bit] = swap_in_turn(now[mask], bit, *others)
        for stream in range(2):
            held[stream][chunk] = [have[stream][mask] for mask in masks]

    def beside(chunk, kind, *others):
        arrays = [
            [[a[m] for m in order[s][kind]] for a in held[s][max(chunk - 1, 0) : chunk + 1]] for s in range(2)
        ]
        if others:
            arrays[0][-1][0] = after(arrays[0][-1][0], *others)
        up, down = edges(chunk, depth, arrays)
        return lax.ppermute(up, "space", upward), lax.ppermute(down, "space", downward)

    gives = []
    result = None
    for chunk in range(CUTS):
        raw(chunk)
    shape = (2 * local_steps, planes, rows_x, rows_y)
    for chunk in range(CUTS):
        early = beside(chunk, 0)
        late = beside(chunk, 1, *early, *(gives[-1] if gives else []))
        used = [held[s][max(chunk - 1, 0) : chunk + 1] for s in range(2)]
        result, *give = apply(chunk, depth, order, sides, maps, early, late, used, shape, result)
        gives.append(give)
    for chunk in range(CUTS):
        flight = 1 if chunk else 2
        got = [swap_in_turn(gives[chunk][s], bits[s], flight=flight) for s in range(2)]
        result = place(chunk, depth, sides, got, result)
    return result.reshape(2, local_steps, planes, rows_x, rows_y)


def solution(mesh):
    in_specs = (P("tm", "space", None, None), P("tm"), P(), P(), P())
    out_specs = P(None, "tm", "space", None, None)
    return jax.shard_map(local, mesh=mesh, in_specs=in_specs, out_specs=out_specs, check_vma=False)
```

```python
import functools

import jax
import jax.numpy as jnp
from jax import lax
from jax.experimental import pallas as pl
from jax.experimental.pallas import tpu as pltpu
from jax.sharding import PartitionSpec as P


CUTS = (0, 4, 8)
CHUNKS = len(CUTS) - 1
VMEM_LIMIT = 28 * 2**20
HBM = pl.BlockSpec(memory_space=pl.ANY)
VMEM = pl.BlockSpec(memory_space=pltpu.VMEM)
SCALARS = pl.BlockSpec(memory_space=pltpu.SMEM)
COST = 370000


def cost(weight):
    return pl.CostEstimate(flops=0, bytes_accessed=weight * COST, transcendentals=0)


PARAMS = pltpu.CompilerParams(vmem_limit_bytes=4 * 2**20)


def block_row(stream, side, row, depth, rows_x):
    if stream == 0:
        return row + side * (rows_x - 1 - 2 * row)
    return depth * (1 + side) + row


def own_rows(chunk, depth):
    bounds = [depth * cut // 8 for cut in CUTS]
    return list(range(bounds[chunk], bounds[chunk + 1]))


def chunk_rows(stream, chunk, depth):
    rows = own_rows(chunk, depth)
    first = rows[0] + 1 if chunk else (0 if stream == 0 else -1)
    return list(range(first, rows[-1] + 2))


def where_rows(stream, chunk, depth):
    places = {}
    for back in (1, 0):
        if chunk >= back:
            for at, row in enumerate(chunk_rows(stream, chunk - back, depth)):
                places[row] = (1 - back, at)
    return places


def run(copies):
    for copy in copies:
        copy.start()
    for copy in copies:
        copy.wait()


def pick_kernel(chunk, depth, sides_ref, ratio_ref, in_ref, *refs):
    outs, sems = refs[:-1], refs[-1]
    _, planes, rows_x, _ = in_ref.shape
    jobs = []
    for stream in range(2):
        for other in (1, 0):
            side = 1 - sides_ref[stream] if other else sides_ref[stream]
            for at, row in enumerate(chunk_rows(stream, chunk, depth)):
                x = block_row(stream, side, row, depth, rows_x)
                for z in range(planes):
                    out = outs[2 * stream + other].at[at, z]
                    jobs.append((pltpu.make_async_copy(in_ref.at[:, z, x], out, sems.at[len(jobs)]), out))
    for copy, _ in jobs:
        copy.start()
    ratio = ratio_ref[...]
    for copy, out in jobs:
        copy.wait()
        out[...] = out[...] * ratio


def pick(chunk, residual, ratio, sides, depth):
    steps, planes, _, rows_y = residual.shape
    counts = [len(chunk_rows(stream, chunk, depth)) for stream in (0, 0, 1, 1)]
    outs = pl.pallas_call(
        functools.partial(pick_kernel, chunk, depth),
        out_shape=[jax.ShapeDtypeStruct((c, planes, steps, rows_y), jnp.float32) for c in counts],
        in_specs=[SCALARS, VMEM, HBM],
        out_specs=[VMEM] * 4,
        scratch_shapes=[pltpu.SemaphoreType.DMA((sum(counts) * planes,))],
        compiler_params=pltpu.CompilerParams(vmem_limit_bytes=56 * 2**20),
        cost_estimate=cost(5),
        name="pick",
    )(sides, ratio, residual)
    return [outs[0:2], outs[2:4]]


def edge_kernel(chunk, depth, groups, *refs):
    raws, (up_ref, down_ref, sems) = refs[:-3], refs[-3:]
    planes = raws[0].shape[1]
    backs = 2 if chunk else 1
    copies = []
    for stream in range(2):
        places = where_rows(stream, chunk, depth)
        for at, row in enumerate(own_rows(chunk, depth)):
            back, index = places[row]
            for group in range(groups):
                raw = raws[(stream * backs + back - 2 + backs) * groups + group]
                for z, out in ((planes - 1, up_ref), (0, down_ref)):
                    copy = pltpu.make_async_copy(
                        raw.at[index, z], out.at[stream, at, group], sems.at[len(copies)]
                    )
                    copies.append(copy)
    run(copies)


def edges(chunk, depth, raws):
    groups = len(raws[0][0])
    _, _, steps, rows_y = raws[0][0][0].shape
    flat = [raw for stream in raws for arrays in stream for raw in arrays]
    high = len(own_rows(chunk, depth))
    shape = jax.ShapeDtypeStruct((2, high, groups, steps, rows_y), jnp.float32)
    return pl.pallas_call(
        functools.partial(edge_kernel, chunk, depth, groups),
        out_shape=[shape] * 2,
        in_specs=[HBM] * len(flat),
        out_specs=[HBM] * 2,
        scratch_shapes=[pltpu.SemaphoreType.DMA((4 * high * groups,))],
        compiler_params=PARAMS,
        cost_estimate=cost(3),
        name="edges",
    )(*flat)


def halves(value):
    high = value.astype(jnp.bfloat16)
    return high, (value - high.astype(jnp.float32)).astype(jnp.bfloat16)


def apply_kernel(chunk, depth, order, sides_ref, map_a_ref, map_b_ref, *refs):
    (early_low, early_high, late_low, late_high), raws = refs[:4], refs[4:-5]
    out_ref, gives, own, sems = refs[-5], refs[-4:-2], refs[-2], refs[-1]
    groups = sum(len(part) for part in order[0])
    backs = 2 if chunk else 1
    _, planes, rows_x, rows_y = out_ref.shape
    stores = []
    for stream in range(2):
        maps = (map_a_ref, map_b_ref)[stream][...]
        half = maps.shape[0] // 2
        places = where_rows(stream, chunk, depth)

        def load(row, z):
            back, index = places[row]
            start = (stream * backs + back - 2 + backs) * groups
            return jnp.concatenate([raw[index, z] for raw in raws[start : start + groups]], axis=0)

        def outside(early, late, at):
            parts = {}
            for kind, ref in enumerate((early, late)):
                for place, group in enumerate(order[stream][kind]):
                    parts[group] = ref[stream, at, place]
            return jnp.concatenate([parts[group] for group in range(groups)], axis=0)

        for at, row in enumerate(own_rows(chunk, depth)):
            number = stream * len(own_rows(chunk, depth)) + at
            x = block_row(stream, sides_ref[stream], row, depth, rows_x)
            mids = [load(row, z) for z in range(planes)]
            for z, mid in enumerate(mids):
                lane = lax.broadcasted_iota(jnp.int32, mid.shape, 1)
                total = jnp.where(lane == 0, 0.0, pltpu.roll(mid, 1, 1))
                total = total + jnp.where(lane == rows_y - 1, 0.0, pltpu.roll(mid, rows_y - 1, 1))
                for beside in (row - 1, row + 1):
                    if beside in places:
                        total = total + load(beside, z)
                total = total + (mids[z - 1] if z else outside(early_low, late_low, at))
                total = total + (mids[z + 1] if z < planes - 1 else outside(early_high, late_high, at))
                mid_h, mid_l = halves(mid)
                sum_h, sum_l = halves(total)
                stack = jnp.concatenate([mid_h, mid_h, mid_l, sum_h, sum_h, sum_l], axis=0)
                value = jnp.dot(maps, stack, preferred_element_type=jnp.float32)
                own[number, z] = value[:half]
                gives[stream][at, z] = value[half:]
                store = pltpu.make_async_copy(own.at[number, z], out_ref.at[:, z, x], sems.at[number, z])
                store.start()
                stores.append(store)
    for store in stores:
        store.wait()


def apply(chunk, depth, order, sides, maps, early, late, raws, shape, result):
    _, planes, _, rows_y = raws[0][0][0].shape
    high = len(own_rows(chunk, depth))
    half = shape[0]
    flat = [raw for stream in raws for arrays in stream for raw in arrays]
    first = [] if result is None else [result]
    give = jax.ShapeDtypeStruct((high, planes, half, rows_y), jnp.float32)
    count = 3 + 4 + len(flat)

    def body(*refs):
        refs = refs[:count] + refs[count + len(first) :]
        apply_kernel(chunk, depth, order, *refs)

    return pl.pallas_call(
        body,
        out_shape=[jax.ShapeDtypeStruct(shape, jnp.float32), give, give],
        in_specs=[SCALARS] + [VMEM] * (count - 1) + [HBM] * len(first),
        out_specs=[HBM, VMEM, VMEM],
        scratch_shapes=[
            pltpu.VMEM((2 * high, planes, half, rows_y), jnp.float32),
            pltpu.SemaphoreType.DMA((2 * high, planes)),
        ],
        input_output_aliases={count: 0} if first else {},
        compiler_params=pltpu.CompilerParams(vmem_limit_bytes=VMEM_LIMIT),
        cost_estimate=cost(10),
        name="apply",
    )(sides, *maps, *early, *late, *flat, *first)


def place_kernel(chunk, depth, sides_ref, got_a, got_b, _, out_ref, sems):
    _, planes, rows_x, _ = out_ref.shape
    copies = []
    for stream, got in enumerate((got_a, got_b)):
        for at, row in enumerate(own_rows(chunk, depth)):
            x = block_row(stream, 1 - sides_ref[stream], row, depth, rows_x)
            for z in range(planes):
                copies.append(pltpu.make_async_copy(got.at[at, z], out_ref.at[:, z, x], sems.at[len(copies)]))
    run(copies)


def place(chunk, depth, sides, got, result):
    planes = result.shape[1]
    return pl.pallas_call(
        functools.partial(place_kernel, chunk, depth),
        out_shape=jax.ShapeDtypeStruct(result.shape, jnp.float32),
        in_specs=[SCALARS] + [HBM] * 3,
        out_specs=HBM,
        scratch_shapes=[pltpu.SemaphoreType.DMA((2 * len(own_rows(chunk, depth)) * planes,))],
        input_output_aliases={3: 0},
        compiler_params=PARAMS,
        cost_estimate=cost(2),
        name="place",
    )(sides, *got, result)


def after(value, *others):
    return lax.optimization_barrier((value, *others))[0]


def maps_kernel(bits, me_ref, ahead_ref, back_ref, eigen_ref, *outs):
    steps = ahead_ref.shape[1]
    local_steps = outs[0].shape[0] // 4
    me = me_ref[0]
    real_part = 6.0 + eigen_ref[0:1, :]
    imag_part = eigen_ref[1:2, :]
    denom = real_part * real_part + imag_part * imag_part
    coef_re = real_part / denom
    coef_im = -imag_part / denom
    left = []
    for block in (me, jnp.bitwise_xor(me, bits[0]), jnp.bitwise_xor(me, bits[1])):
        span = pl.ds(pl.multiple_of(block * local_steps, local_steps), local_steps)
        back_re, back_im = back_ref[0, span, :], back_ref[1, span, :]
        for _ in range(2):
            back_re, back_im = back_re * coef_re - back_im * coef_im, back_re * coef_im + back_im * coef_re
            left += [back_re, back_im]
    left = jnp.concatenate(left, axis=0)
    by_re = jnp.dot(left, ahead_ref[0], precision=lax.Precision.HIGHEST, preferred_element_type=jnp.float32)
    by_im = jnp.dot(left, ahead_ref[1], precision=lax.Precision.HIGHEST, preferred_element_type=jnp.float32)

    def piece(data, which):
        return data[which * local_steps : (which + 1) * local_steps]

    row = lax.broadcasted_iota(jnp.int32, (steps, steps), 0)
    column = lax.broadcasted_iota(jnp.int32, (steps, steps), 1)
    turn = (row == jnp.bitwise_xor(column, me * local_steps)).astype(jnp.float32).astype(jnp.bfloat16)
    parts = []
    for block in range(3):
        for power in range(2):
            at = 2 * (2 * block + power)
            both = jnp.concatenate(
                [piece(by_re, at) - piece(by_im, at + 1), piece(by_im, at) + piece(by_re, at + 1)], axis=0
            )
            pair = jnp.concatenate(halves(both), axis=0)
            parts.append(jnp.dot(pair, turn, preferred_element_type=jnp.float32).astype(jnp.bfloat16))
    half = 2 * local_steps
    for out, blocks in zip(outs, ((0, 1), (0, 2))):
        for place, block in enumerate(blocks):
            once, twice = parts[2 * block], parts[2 * block + 1]
            columns = (once[:half], once[half:], once[:half], twice[:half], twice[half:], twice[:half])
            for c, value in enumerate(columns):
                out[place * half : (place + 1) * half, c * steps : (c + 1) * steps] = value


def make_maps(forward_map, back_map, eigen_values, me, count, bits):
    steps = forward_map.shape[1]
    shape = jax.ShapeDtypeStruct((4 * steps // count, 6 * steps), jnp.bfloat16)
    return pl.pallas_call(
        functools.partial(maps_kernel, bits),
        out_shape=[shape, shape],
        in_specs=[SCALARS] + [VMEM] * 3,
        out_specs=[VMEM] * 2,
        compiler_params=pltpu.CompilerParams(vmem_limit_bytes=VMEM_LIMIT),
        cost_estimate=cost(2),
        name="maps",
    )(me.astype(jnp.int32).reshape(1), forward_map, back_map, eigen_values)


def local(residual, step_ratio, forward_map, back_map, eigen_values):
    local_steps, planes, rows_x, rows_y = residual.shape
    depth = rows_x // 4
    count = lax.axis_size("tm")
    bits = (1, count // 2)
    all_bits = [1 << k for k in range(count.bit_length() - 1)]
    me = lax.axis_index("tm")
    sides = jnp.stack([jnp.where(jnp.bitwise_and(me, b) > 0, 1, 0) for b in bits]).astype(jnp.int32)
    ratio = jnp.broadcast_to((step_ratio.astype(jnp.float32) / 8.0)[:, None], (local_steps, rows_y))

    def swap(data, bit):
        return lax.ppermute(data, "tm", [(i, i ^ bit) for i in range(count)])

    spaces = lax.axis_size("space")
    upward = [(i, i + 1) for i in range(spaces - 1)]
    downward = [(i + 1, i) for i in range(spaces - 1)]

    queues = [[], []]

    def swap_in_turn(data, bit, *others, flight=1):
        queue = queues[0 if bit == bits[0] else 1]
        if len(queue) >= flight:
            others = (queue[-flight], *others)
        if others:
            data = after(data, *others)
        got = swap(data, bit)
        queue.append(got)
        return got

    masks = range(count)
    order = [[[m for m in masks if m in (0, b)], [m for m in masks if m not in (0, b)]] for b in bits]
    held = [[None] * CHUNKS for _ in range(2)]

    maps = make_maps(forward_map, back_map, eigen_values, me, count, bits)
    firsts = []

    def raw(chunk):
        data = after(residual, *firsts[-1]) if firsts else residual
        mine = pick(chunk, data, ratio, sides, depth)
        have = [{0: mine[s][0], bits[s]: swap_in_turn(mine[s][1], bits[s])} for s in range(2)]
        firsts.append([have[s][bits[s]] for s in range(2)])
        for bit in all_bits:
            for mask in masks:
                for stream in (1, 0):
                    now = have[stream]
                    free = bit != bits[stream] and not mask & bit
                    if free and mask in now and (mask | bit) not in now:
                        others = maps if mask and chunk == 0 else []
                        now[mask | bit] = swap_in_turn(now[mask], bit, *others)
        for stream in range(2):
            held[stream][chunk] = [have[stream][mask] for mask in masks]

    def beside(chunk, kind, *others):
        arrays = [
            [[a[m] for m in order[s][kind]] for a in held[s][max(chunk - 1, 0) : chunk + 1]] for s in range(2)
        ]
        if others:
            arrays[0][-1][0] = after(arrays[0][-1][0], *others)
        up, down = edges(chunk, depth, arrays)
        return lax.ppermute(up, "space", upward), lax.ppermute(down, "space", downward)

    gives = []
    result = None
    for chunk in range(CHUNKS):
        raw(chunk)
    shape = (2 * local_steps, planes, rows_x, rows_y)
    for chunk in range(CHUNKS):
        early = beside(chunk, 0)
        late = beside(chunk, 1, *early)
        used = [held[s][max(chunk - 1, 0) : chunk + 1] for s in range(2)]
        result, *give = apply(chunk, depth, order, sides, maps, early, late, used, shape, result)
        gives.append(give)
    for chunk in range(CHUNKS):
        got = [swap_in_turn(gives[chunk][s], bits[s]) for s in range(2)]
        result = place(chunk, depth, sides, got, result)
    return result.reshape(2, local_steps, planes, rows_x, rows_y)


def solution(mesh):
    in_specs = (P("tm", "space", None, None), P("tm"), P(), P(), P())
    out_specs = P(None, "tm", "space", None, None)
    return jax.shard_map(local, mesh=mesh, in_specs=in_specs, out_specs=out_specs, check_vma=False)
```

```python
import functools

import jax
import jax.numpy as jnp
from jax import lax
from jax.experimental import pallas as pl
from jax.experimental.pallas import tpu as pltpu
from jax.sharding import PartitionSpec as P


CUTS = (0, 4, 8)
CHUNKS = len(CUTS) - 1
VMEM_LIMIT = 28 * 2**20
HBM = pl.BlockSpec(memory_space=pl.ANY)
VMEM = pl.BlockSpec(memory_space=pltpu.VMEM)
SCALARS = pl.BlockSpec(memory_space=pltpu.SMEM)
COST = 370000


def cost(weight):
    return pl.CostEstimate(flops=0, bytes_accessed=weight * COST, transcendentals=0)


PARAMS = pltpu.CompilerParams(vmem_limit_bytes=4 * 2**20)


def block_row(stream, side, row, depth, rows_x):
    if stream == 0:
        return row + side * (rows_x - 1 - 2 * row)
    return depth * (1 + side) + row


def own_rows(chunk, depth):
    bounds = [depth * cut // 8 for cut in CUTS]
    return list(range(bounds[chunk], bounds[chunk + 1]))


def chunk_rows(stream, chunk, depth):
    rows = own_rows(chunk, depth)
    first = rows[0] + 1 if chunk else (0 if stream == 0 else -1)
    return list(range(first, rows[-1] + 2))


def where_rows(stream, chunk, depth):
    places = {}
    for back in (1, 0):
        if chunk >= back:
            for at, row in enumerate(chunk_rows(stream, chunk - back, depth)):
                places[row] = (1 - back, at)
    return places


def run(copies):
    for copy in copies:
        copy.start()
    for copy in copies:
        copy.wait()


def pick_kernel(chunk, depth, sides_ref, ratio_ref, in_ref, *refs):
    outs, sems = refs[:-1], refs[-1]
    _, planes, rows_x, _ = in_ref.shape
    jobs = []
    for stream in range(2):
        for other in (1, 0):
            side = 1 - sides_ref[stream] if other else sides_ref[stream]
            for at, row in enumerate(chunk_rows(stream, chunk, depth)):
                x = block_row(stream, side, row, depth, rows_x)
                for z in range(planes):
                    out = outs[2 * stream + other].at[at, z]
                    jobs.append((pltpu.make_async_copy(in_ref.at[:, z, x], out, sems.at[len(jobs)]), out))
    for copy, _ in jobs:
        copy.start()
    ratio = ratio_ref[...]
    for copy, out in jobs:
        copy.wait()
        out[...] = out[...] * ratio


def pick(chunk, residual, ratio, sides, depth):
    steps, planes, _, rows_y = residual.shape
    counts = [len(chunk_rows(stream, chunk, depth)) for stream in (0, 0, 1, 1)]
    outs = pl.pallas_call(
        functools.partial(pick_kernel, chunk, depth),
        out_shape=[jax.ShapeDtypeStruct((c, planes, steps, rows_y), jnp.float32) for c in counts],
        in_specs=[SCALARS, VMEM, HBM],
        out_specs=[VMEM] * 4,
        scratch_shapes=[pltpu.SemaphoreType.DMA((sum(counts) * planes,))],
        compiler_params=pltpu.CompilerParams(vmem_limit_bytes=56 * 2**20),
        cost_estimate=cost(5),
        name="pick",
    )(sides, ratio, residual)
    return [outs[0:2], outs[2:4]]


def edge_kernel(chunk, depth, groups, *refs):
    raws, (up_ref, down_ref, sems) = refs[:-3], refs[-3:]
    planes = raws[0].shape[1]
    backs = 2 if chunk else 1
    copies = []
    for stream in range(2):
        places = where_rows(stream, chunk, depth)
        for at, row in enumerate(own_rows(chunk, depth)):
            back, index = places[row]
            for group in range(groups):
                raw = raws[(stream * backs + back - 2 + backs) * groups + group]
                for z, out in ((planes - 1, up_ref), (0, down_ref)):
                    copy = pltpu.make_async_copy(
                        raw.at[index, z], out.at[stream, at, group], sems.at[len(copies)]
                    )
                    copies.append(copy)
    run(copies)


def edges(chunk, depth, raws):
    groups = len(raws[0][0])
    _, _, steps, rows_y = raws[0][0][0].shape
    flat = [raw for stream in raws for arrays in stream for raw in arrays]
    high = len(own_rows(chunk, depth))
    shape = jax.ShapeDtypeStruct((2, high, groups, steps, rows_y), jnp.float32)
    return pl.pallas_call(
        functools.partial(edge_kernel, chunk, depth, groups),
        out_shape=[shape] * 2,
        in_specs=[HBM] * len(flat),
        out_specs=[HBM] * 2,
        scratch_shapes=[pltpu.SemaphoreType.DMA((4 * high * groups,))],
        compiler_params=PARAMS,
        cost_estimate=cost(3),
        name="edges",
    )(*flat)


def halves(value):
    high = value.astype(jnp.bfloat16)
    return high, (value - high.astype(jnp.float32)).astype(jnp.bfloat16)


def apply_kernel(chunk, depth, order, sides_ref, map_a_ref, map_b_ref, *refs):
    (early_low, early_high, late_low, late_high), raws = refs[:4], refs[4:-5]
    out_ref, gives, own, sems = refs[-5], refs[-4:-2], refs[-2], refs[-1]
    groups = sum(len(part) for part in order[0])
    backs = 2 if chunk else 1
    _, planes, rows_x, rows_y = out_ref.shape
    stores = []
    for stream in range(2):
        maps = (map_a_ref, map_b_ref)[stream][...]
        half = maps.shape[0] // 2
        places = where_rows(stream, chunk, depth)

        def load(row, z):
            back, index = places[row]
            start = (stream * backs + back - 2 + backs) * groups
            return jnp.concatenate([raw[index, z] for raw in raws[start : start + groups]], axis=0)

        def outside(early, late, at):
            parts = {}
            for kind, ref in enumerate((early, late)):
                for place, group in enumerate(order[stream][kind]):
                    parts[group] = ref[stream, at, place]
            return jnp.concatenate([parts[group] for group in range(groups)], axis=0)

        for at, row in enumerate(own_rows(chunk, depth)):
            number = stream * len(own_rows(chunk, depth)) + at
            x = block_row(stream, sides_ref[stream], row, depth, rows_x)
            mids = [load(row, z) for z in range(planes)]
            for z, mid in enumerate(mids):
                lane = lax.broadcasted_iota(jnp.int32, mid.shape, 1)
                total = jnp.where(lane == 0, 0.0, pltpu.roll(mid, 1, 1))
                total = total + jnp.where(lane == rows_y - 1, 0.0, pltpu.roll(mid, rows_y - 1, 1))
                for beside in (row - 1, row + 1):
                    if beside in places:
                        total = total + load(beside, z)
                total = total + (mids[z - 1] if z else outside(early_low, late_low, at))
                total = total + (mids[z + 1] if z < planes - 1 else outside(early_high, late_high, at))
                mid_h, mid_l = halves(mid)
                sum_h, sum_l = halves(total)
                stack = jnp.concatenate([mid_h, mid_h, mid_l, sum_h, sum_h, sum_l], axis=0)
                value = jnp.dot(maps, stack, preferred_element_type=jnp.float32)
                own[number, z] = value[:half]
                gives[stream][at, z] = value[half:]
                store = pltpu.make_async_copy(own.at[number, z], out_ref.at[:, z, x], sems.at[number, z])
                store.start()
                stores.append(store)
    for store in stores:
        store.wait()


def apply(chunk, depth, order, sides, maps, early, late, raws, shape, result):
    _, planes, _, rows_y = raws[0][0][0].shape
    high = len(own_rows(chunk, depth))
    half = shape[0]
    flat = [raw for stream in raws for arrays in stream for raw in arrays]
    first = [] if result is None else [result]
    give = jax.ShapeDtypeStruct((high, planes, half, rows_y), jnp.float32)
    count = 3 + 4 + len(flat)

    def body(*refs):
        refs = refs[:count] + refs[count + len(first) :]
        apply_kernel(chunk, depth, order, *refs)

    return pl.pallas_call(
        body,
        out_shape=[jax.ShapeDtypeStruct(shape, jnp.float32), give, give],
        in_specs=[SCALARS] + [VMEM] * (count - 1) + [HBM] * len(first),
        out_specs=[HBM, VMEM, VMEM],
        scratch_shapes=[
            pltpu.VMEM((2 * high, planes, half, rows_y), jnp.float32),
            pltpu.SemaphoreType.DMA((2 * high, planes)),
        ],
        input_output_aliases={count: 0} if first else {},
        compiler_params=pltpu.CompilerParams(vmem_limit_bytes=VMEM_LIMIT),
        cost_estimate=cost(10),
        name="apply",
    )(sides, *maps, *early, *late, *flat, *first)


def place_kernel(chunk, depth, sides_ref, got_a, got_b, _, out_ref, sems):
    _, planes, rows_x, _ = out_ref.shape
    copies = []
    for stream, got in enumerate((got_a, got_b)):
        for at, row in enumerate(own_rows(chunk, depth)):
            x = block_row(stream, 1 - sides_ref[stream], row, depth, rows_x)
            for z in range(planes):
                copies.append(pltpu.make_async_copy(got.at[at, z], out_ref.at[:, z, x], sems.at[len(copies)]))
    run(copies)


def place(chunk, depth, sides, got, result):
    planes = result.shape[1]
    return pl.pallas_call(
        functools.partial(place_kernel, chunk, depth),
        out_shape=jax.ShapeDtypeStruct(result.shape, jnp.float32),
        in_specs=[SCALARS] + [HBM] * 3,
        out_specs=HBM,
        scratch_shapes=[pltpu.SemaphoreType.DMA((2 * len(own_rows(chunk, depth)) * planes,))],
        input_output_aliases={3: 0},
        compiler_params=PARAMS,
        cost_estimate=cost(2),
        name="place",
    )(sides, *got, result)


def after(value, *others):
    return lax.optimization_barrier((value, *others))[0]


def maps_kernel(bits, me_ref, ahead_ref, back_ref, eigen_ref, *outs):
    steps = ahead_ref.shape[1]
    local_steps = outs[0].shape[0] // 4
    me = me_ref[0]
    real_part = 6.0 + eigen_ref[0:1, :]
    imag_part = eigen_ref[1:2, :]
    denom = real_part * real_part + imag_part * imag_part
    coef_re = real_part / denom
    coef_im = -imag_part / denom
    left = []
    for block in (me, jnp.bitwise_xor(me, bits[0]), jnp.bitwise_xor(me, bits[1])):
        span = pl.ds(pl.multiple_of(block * local_steps, local_steps), local_steps)
        back_re, back_im = back_ref[0, span, :], back_ref[1, span, :]
        for _ in range(2):
            back_re, back_im = back_re * coef_re - back_im * coef_im, back_re * coef_im + back_im * coef_re
            left += [back_re, back_im]
    left = jnp.concatenate(left, axis=0)
    by_re = jnp.dot(left, ahead_ref[0], precision=lax.Precision.HIGHEST, preferred_element_type=jnp.float32)
    by_im = jnp.dot(left, ahead_ref[1], precision=lax.Precision.HIGHEST, preferred_element_type=jnp.float32)

    def piece(data, which):
        return data[which * local_steps : (which + 1) * local_steps]

    row = lax.broadcasted_iota(jnp.int32, (steps, steps), 0)
    column = lax.broadcasted_iota(jnp.int32, (steps, steps), 1)
    turn = (row == jnp.bitwise_xor(column, me * local_steps)).astype(jnp.float32).astype(jnp.bfloat16)
    parts = []
    for block in range(3):
        for power in range(2):
            at = 2 * (2 * block + power)
            both = jnp.concatenate(
                [piece(by_re, at) - piece(by_im, at + 1), piece(by_im, at) + piece(by_re, at + 1)], axis=0
            )
            pair = jnp.concatenate(halves(both), axis=0)
            parts.append(jnp.dot(pair, turn, preferred_element_type=jnp.float32).astype(jnp.bfloat16))
    half = 2 * local_steps
    for out, blocks in zip(outs, ((0, 1), (0, 2))):
        for place, block in enumerate(blocks):
            once, twice = parts[2 * block], parts[2 * block + 1]
            columns = (once[:half], once[half:], once[:half], twice[:half], twice[half:], twice[:half])
            for c, value in enumerate(columns):
                out[place * half : (place + 1) * half, c * steps : (c + 1) * steps] = value


def make_maps(forward_map, back_map, eigen_values, me, count, bits):
    steps = forward_map.shape[1]
    shape = jax.ShapeDtypeStruct((4 * steps // count, 6 * steps), jnp.bfloat16)
    return pl.pallas_call(
        functools.partial(maps_kernel, bits),
        out_shape=[shape, shape],
        in_specs=[SCALARS] + [VMEM] * 3,
        out_specs=[VMEM] * 2,
        compiler_params=pltpu.CompilerParams(vmem_limit_bytes=VMEM_LIMIT),
        cost_estimate=cost(2),
        name="maps",
    )(me.astype(jnp.int32).reshape(1), forward_map, back_map, eigen_values)


def local(residual, step_ratio, forward_map, back_map, eigen_values):
    local_steps, planes, rows_x, rows_y = residual.shape
    depth = rows_x // 4
    count = lax.axis_size("tm")
    bits = (1, count // 2)
    all_bits = [1 << k for k in range(count.bit_length() - 1)]
    me = lax.axis_index("tm")
    sides = jnp.stack([jnp.where(jnp.bitwise_and(me, b) > 0, 1, 0) for b in bits]).astype(jnp.int32)
    ratio = jnp.broadcast_to((step_ratio.astype(jnp.float32) / 8.0)[:, None], (local_steps, rows_y))

    def swap(data, bit):
        return lax.ppermute(data, "tm", [(i, i ^ bit) for i in range(count)])

    spaces = lax.axis_size("space")
    upward = [(i, i + 1) for i in range(spaces - 1)]
    downward = [(i + 1, i) for i in range(spaces - 1)]

    queues = [[], []]

    def swap_in_turn(data, bit, *others, flight=1):
        queue = queues[0 if bit == bits[0] else 1]
        if len(queue) >= flight:
            others = (queue[-flight], *others)
        if others:
            data = after(data, *others)
        got = swap(data, bit)
        queue.append(got)
        return got

    masks = range(count)
    order = [[[m for m in masks if m in (0, b)], [m for m in masks if m not in (0, b)]] for b in bits]
    held = [[None] * CHUNKS for _ in range(2)]

    maps = make_maps(forward_map, back_map, eigen_values, me, count, bits)
    firsts = []

    def raw(chunk):
        data = after(residual, *firsts[-1]) if firsts else residual
        mine = pick(chunk, data, ratio, sides, depth)
        have = [{0: mine[s][0], bits[s]: swap_in_turn(mine[s][1], bits[s])} for s in range(2)]
        firsts.append([have[s][bits[s]] for s in range(2)])
        for bit in all_bits:
            for mask in masks:
                for stream in (1, 0):
                    now = have[stream]
                    free = bit != bits[stream] and not mask & bit
                    if free and mask in now and (mask | bit) not in now:
                        others = maps if mask and chunk == 0 else []
                        now[mask | bit] = swap_in_turn(now[mask], bit, *others, flight=2 if chunk == 0 else 1)
        for stream in range(2):
            held[stream][chunk] = [have[stream][mask] for mask in masks]

    def beside(chunk, kind, *others):
        arrays = [
            [[a[m] for m in order[s][kind]] for a in held[s][max(chunk - 1, 0) : chunk + 1]] for s in range(2)
        ]
        if others:
            arrays[0][-1][0] = after(arrays[0][-1][0], *others)
        up, down = edges(chunk, depth, arrays)
        return lax.ppermute(up, "space", upward), lax.ppermute(down, "space", downward)

    gots = []
    gives = []
    result = None
    for chunk in range(CHUNKS):
        raw(chunk)
    shape = (2 * local_steps, planes, rows_x, rows_y)
    for chunk in range(CHUNKS):
        early = beside(chunk, 0)
        late = beside(chunk, 1, *early, *(gives[-1] if gives else []))
        used = [held[s][max(chunk - 1, 0) : chunk + 1] for s in range(2)]
        result, *give = apply(chunk, depth, order, sides, maps, early, late, used, shape, result)
        gives.append(give)
        gots.append([swap_in_turn(give[s], bits[s], flight=1 + min(chunk, 1)) for s in range(2)])
    for chunk in range(CHUNKS):
        result = place(chunk, depth, sides, gots[chunk], result)
    return result.reshape(2, local_steps, planes, rows_x, rows_y)


def solution(mesh):
    in_specs = (P("tm", "space", None, None), P("tm"), P(), P(), P())
    out_specs = P(None, "tm", "space", None, None)
    return jax.shard_map(local, mesh=mesh, in_specs=in_specs, out_specs=out_specs, check_vma=False)
```

```python
import functools

import jax
import jax.numpy as jnp
from jax import lax
from jax.experimental import pallas as pl
from jax.experimental.pallas import tpu as pltpu
from jax.sharding import PartitionSpec as P


CUTS = (0, 4, 8)
CHUNKS = len(CUTS) - 1
VMEM_LIMIT = 28 * 2**20
HBM = pl.BlockSpec(memory_space=pl.ANY)
VMEM = pl.BlockSpec(memory_space=pltpu.VMEM)
SCALARS = pl.BlockSpec(memory_space=pltpu.SMEM)
COST = 370000


def cost(weight):
    return pl.CostEstimate(flops=0, bytes_accessed=weight * COST, transcendentals=0)


def block_row(stream, side, row, depth, rows_x):
    if stream == 0:
        return row + side * (rows_x - 1 - 2 * row)
    return depth * (1 + side) + row


def own_rows(chunk, depth):
    bounds = [depth * cut // 8 for cut in CUTS]
    return list(range(bounds[chunk], bounds[chunk + 1]))


def chunk_rows(stream, chunk, depth):
    rows = own_rows(chunk, depth)
    first = rows[0] + 1 if chunk else (0 if stream == 0 else -1)
    return list(range(first, rows[-1] + 2))


def where_rows(stream, chunk, depth):
    places = {}
    for back in (1, 0):
        if chunk >= back:
            for at, row in enumerate(chunk_rows(stream, chunk - back, depth)):
                places[row] = (1 - back, at)
    return places


def run(copies):
    for copy in copies:
        copy.start()
    for copy in copies:
        copy.wait()


def pick_kernel(chunk, depth, sides_ref, ratio_ref, in_ref, *refs):
    outs, sems = refs[:-1], refs[-1]
    _, planes, rows_x, _ = in_ref.shape
    jobs = []
    for stream in range(2):
        for other in (1, 0):
            side = 1 - sides_ref[stream] if other else sides_ref[stream]
            for at, row in enumerate(chunk_rows(stream, chunk, depth)):
                x = block_row(stream, side, row, depth, rows_x)
                for z in range(planes):
                    out = outs[2 * stream + other].at[at, z]
                    jobs.append((pltpu.make_async_copy(in_ref.at[:, z, x], out, sems.at[len(jobs)]), out))
    for copy, _ in jobs:
        copy.start()
    ratio = ratio_ref[...]
    for copy, out in jobs:
        copy.wait()
        out[...] = out[...] * ratio


def pick(chunk, residual, ratio, sides, depth):
    steps, planes, _, rows_y = residual.shape
    counts = [len(chunk_rows(stream, chunk, depth)) for stream in (0, 0, 1, 1)]
    outs = pl.pallas_call(
        functools.partial(pick_kernel, chunk, depth),
        out_shape=[jax.ShapeDtypeStruct((c, planes, steps, rows_y), jnp.float32) for c in counts],
        in_specs=[SCALARS, VMEM, HBM],
        out_specs=[VMEM] * 4,
        scratch_shapes=[pltpu.SemaphoreType.DMA((sum(counts) * planes,))],
        compiler_params=pltpu.CompilerParams(vmem_limit_bytes=56 * 2**20),
        cost_estimate=cost(5),
        name="pick",
    )(sides, ratio, residual)
    return [outs[0:2], outs[2:4]]


def edge_kernel(chunk, depth, groups, *refs):
    raws, (up_ref, down_ref, sems) = refs[:-3], refs[-3:]
    planes = raws[0].shape[1]
    backs = 2 if chunk else 1
    copies = []
    for stream in range(2):
        places = where_rows(stream, chunk, depth)
        for at, row in enumerate(own_rows(chunk, depth)):
            back, index = places[row]
            for group in range(groups):
                raw = raws[(stream * backs + back - 2 + backs) * groups + group]
                for z, out in ((planes - 1, up_ref), (0, down_ref)):
                    copy = pltpu.make_async_copy(
                        raw.at[index, z], out.at[stream, at, group], sems.at[len(copies)]
                    )
                    copies.append(copy)
    run(copies)


def edges(chunk, depth, raws):
    groups = len(raws[0][0])
    _, _, steps, rows_y = raws[0][0][0].shape
    flat = [raw for stream in raws for arrays in stream for raw in arrays]
    high = len(own_rows(chunk, depth))
    shape = jax.ShapeDtypeStruct((2, high, groups, steps, rows_y), jnp.float32)
    return pl.pallas_call(
        functools.partial(edge_kernel, chunk, depth, groups),
        out_shape=[shape] * 2,
        in_specs=[HBM] * len(flat),
        out_specs=[VMEM] * 2,
        scratch_shapes=[pltpu.SemaphoreType.DMA((4 * high * groups,))],
        compiler_params=pltpu.CompilerParams(vmem_limit_bytes=12 * 2**20),
        cost_estimate=cost(3),
        name="edges",
    )(*flat)


def halves(value):
    high = value.astype(jnp.bfloat16)
    return high, (value - high.astype(jnp.float32)).astype(jnp.bfloat16)


def apply_kernel(chunk, depth, order, sides_ref, map_a_ref, map_b_ref, *refs):
    (early_low, early_high, late_low, late_high), raws = refs[:4], refs[4:-5]
    out_ref, gives, own, sems = refs[-5], refs[-4:-2], refs[-2], refs[-1]
    groups = sum(len(part) for part in order[0])
    backs = 2 if chunk else 1
    _, planes, rows_x, rows_y = out_ref.shape
    stores = []
    for stream in range(2):
        maps = (map_a_ref, map_b_ref)[stream][...]
        half = maps.shape[0] // 2
        places = where_rows(stream, chunk, depth)

        def load(row, z):
            back, index = places[row]
            start = (stream * backs + back - 2 + backs) * groups
            return jnp.concatenate([raw[index, z] for raw in raws[start : start + groups]], axis=0)

        def outside(early, late, at):
            parts = {}
            for kind, ref in enumerate((early, late)):
                for place, group in enumerate(order[stream][kind]):
                    parts[group] = ref[stream, at, place]
            return jnp.concatenate([parts[group] for group in range(groups)], axis=0)

        for at, row in enumerate(own_rows(chunk, depth)):
            number = stream * len(own_rows(chunk, depth)) + at
            x = block_row(stream, sides_ref[stream], row, depth, rows_x)
            mids = [load(row, z) for z in range(planes)]
            for z, mid in enumerate(mids):
                lane = lax.broadcasted_iota(jnp.int32, mid.shape, 1)
                total = jnp.where(lane == 0, 0.0, pltpu.roll(mid, 1, 1))
                total = total + jnp.where(lane == rows_y - 1, 0.0, pltpu.roll(mid, rows_y - 1, 1))
                for beside in (row - 1, row + 1):
                    if beside in places:
                        total = total + load(beside, z)
                total = total + (mids[z - 1] if z else outside(early_low, late_low, at))
                total = total + (mids[z + 1] if z < planes - 1 else outside(early_high, late_high, at))
                mid_h, mid_l = halves(mid)
                sum_h, sum_l = halves(total)
                stack = jnp.concatenate([mid_h, mid_h, mid_l, sum_h, sum_h, sum_l], axis=0)
                value = jnp.dot(maps, stack, preferred_element_type=jnp.float32)
                own[number, z] = value[:half]
                gives[stream][at, z] = value[half:]
                store = pltpu.make_async_copy(own.at[number, z], out_ref.at[:, z, x], sems.at[number, z])
                store.start()
                stores.append(store)
    for store in stores:
        store.wait()


def apply(chunk, depth, order, sides, maps, early, late, raws, shape, result):
    _, planes, _, rows_y = raws[0][0][0].shape
    high = len(own_rows(chunk, depth))
    half = shape[0]
    flat = [raw for stream in raws for arrays in stream for raw in arrays]
    first = [] if result is None else [result]
    give = jax.ShapeDtypeStruct((high, planes, half, rows_y), jnp.float32)
    count = 3 + 4 + len(flat)

    def body(*refs):
        refs = refs[:count] + refs[count + len(first) :]
        apply_kernel(chunk, depth, order, *refs)

    return pl.pallas_call(
        body,
        out_shape=[jax.ShapeDtypeStruct(shape, jnp.float32), give, give],
        in_specs=[SCALARS] + [VMEM] * (count - 1) + [HBM] * len(first),
        out_specs=[HBM, VMEM, VMEM],
        scratch_shapes=[
            pltpu.VMEM((2 * high, planes, half, rows_y), jnp.float32),
            pltpu.SemaphoreType.DMA((2 * high, planes)),
        ],
        input_output_aliases={count: 0} if first else {},
        compiler_params=pltpu.CompilerParams(vmem_limit_bytes=VMEM_LIMIT),
        cost_estimate=cost(10),
        name="apply",
    )(sides, *maps, *early, *late, *flat, *first)


def place_kernel(chunk, depth, sides_ref, got_a, got_b, _, out_ref, sems):
    _, planes, rows_x, _ = out_ref.shape
    copies = []
    for stream, got in enumerate((got_a, got_b)):
        for at, row in enumerate(own_rows(chunk, depth)):
            x = block_row(stream, 1 - sides_ref[stream], row, depth, rows_x)
            for z in range(planes):
                copies.append(pltpu.make_async_copy(got.at[at, z], out_ref.at[:, z, x], sems.at[len(copies)]))
    run(copies)


def place(chunk, depth, sides, got, result):
    planes = result.shape[1]
    return pl.pallas_call(
        functools.partial(place_kernel, chunk, depth),
        out_shape=jax.ShapeDtypeStruct(result.shape, jnp.float32),
        in_specs=[SCALARS, VMEM, VMEM, HBM],
        out_specs=HBM,
        scratch_shapes=[pltpu.SemaphoreType.DMA((2 * len(own_rows(chunk, depth)) * planes,))],
        input_output_aliases={3: 0},
        compiler_params=pltpu.CompilerParams(vmem_limit_bytes=12 * 2**20),
        cost_estimate=cost(2),
        name="place",
    )(sides, *got, result)


def after(value, *others):
    return lax.optimization_barrier((value, *others))[0]


def maps_kernel(bits, me_ref, ahead_ref, back_ref, eigen_ref, *outs):
    steps = ahead_ref.shape[1]
    local_steps = outs[0].shape[0] // 4
    me = me_ref[0]
    real_part = 6.0 + eigen_ref[0:1, :]
    imag_part = eigen_ref[1:2, :]
    denom = real_part * real_part + imag_part * imag_part
    coef_re = real_part / denom
    coef_im = -imag_part / denom
    left = []
    for block in (me, jnp.bitwise_xor(me, bits[0]), jnp.bitwise_xor(me, bits[1])):
        span = pl.ds(pl.multiple_of(block * local_steps, local_steps), local_steps)
        back_re, back_im = back_ref[0, span, :], back_ref[1, span, :]
        for _ in range(2):
            back_re, back_im = back_re * coef_re - back_im * coef_im, back_re * coef_im + back_im * coef_re
            left += [back_re, back_im]
    left = jnp.concatenate(left, axis=0)
    by_re = jnp.dot(left, ahead_ref[0], precision=lax.Precision.HIGHEST, preferred_element_type=jnp.float32)
    by_im = jnp.dot(left, ahead_ref[1], precision=lax.Precision.HIGHEST, preferred_element_type=jnp.float32)

    def piece(data, which):
        return data[which * local_steps : (which + 1) * local_steps]

    row = lax.broadcasted_iota(jnp.int32, (steps, steps), 0)
    column = lax.broadcasted_iota(jnp.int32, (steps, steps), 1)
    turn = (row == jnp.bitwise_xor(column, me * local_steps)).astype(jnp.float32).astype(jnp.bfloat16)
    parts = []
    for block in range(3):
        for power in range(2):
            at = 2 * (2 * block + power)
            both = jnp.concatenate(
                [piece(by_re, at) - piece(by_im, at + 1), piece(by_im, at) + piece(by_re, at + 1)], axis=0
            )
            pair = jnp.concatenate(halves(both), axis=0)
            parts.append(jnp.dot(pair, turn, preferred_element_type=jnp.float32).astype(jnp.bfloat16))
    half = 2 * local_steps
    for out, blocks in zip(outs, ((0, 1), (0, 2))):
        for place, block in enumerate(blocks):
            once, twice = parts[2 * block], parts[2 * block + 1]
            columns = (once[:half], once[half:], once[:half], twice[:half], twice[half:], twice[:half])
            for c, value in enumerate(columns):
                out[place * half : (place + 1) * half, c * steps : (c + 1) * steps] = value


def make_maps(forward_map, back_map, eigen_values, me, count, bits):
    steps = forward_map.shape[1]
    shape = jax.ShapeDtypeStruct((4 * steps // count, 6 * steps), jnp.bfloat16)
    return pl.pallas_call(
        functools.partial(maps_kernel, bits),
        out_shape=[shape, shape],
        in_specs=[SCALARS] + [VMEM] * 3,
        out_specs=[VMEM] * 2,
        compiler_params=pltpu.CompilerParams(vmem_limit_bytes=VMEM_LIMIT),
        cost_estimate=cost(2),
        name="maps",
    )(me.astype(jnp.int32).reshape(1), forward_map, back_map, eigen_values)


def local(residual, step_ratio, forward_map, back_map, eigen_values):
    local_steps, planes, rows_x, rows_y = residual.shape
    depth = rows_x // 4
    count = lax.axis_size("tm")
    bits = (1, count // 2)
    all_bits = [1 << k for k in range(count.bit_length() - 1)]
    me = lax.axis_index("tm")
    sides = jnp.stack([jnp.where(jnp.bitwise_and(me, b) > 0, 1, 0) for b in bits]).astype(jnp.int32)
    ratio = jnp.broadcast_to((step_ratio.astype(jnp.float32) / 8.0)[:, None], (local_steps, rows_y))

    def swap(data, bit):
        return lax.ppermute(data, "tm", [(i, i ^ bit) for i in range(count)])

    spaces = lax.axis_size("space")
    upward = [(i, i + 1) for i in range(spaces - 1)]
    downward = [(i + 1, i) for i in range(spaces - 1)]

    queues = [[], []]

    def swap_in_turn(data, bit, *others, flight=1):
        queue = queues[0 if bit == bits[0] else 1]
        if len(queue) >= flight:
            others = (queue[-flight], *others)
        if others:
            data = after(data, *others)
        got = swap(data, bit)
        queue.append(got)
        return got

    masks = range(count)
    order = [[[m for m in masks if m in (0, b)], [m for m in masks if m not in (0, b)]] for b in bits]
    held = [[None] * CHUNKS for _ in range(2)]

    maps = make_maps(forward_map, back_map, eigen_values, me, count, bits)
    firsts = []

    def raw(chunk):
        data = after(residual, *firsts[-1]) if firsts else residual
        mine = pick(chunk, data, ratio, sides, depth)
        have = [{0: mine[s][0], bits[s]: swap_in_turn(mine[s][1], bits[s])} for s in range(2)]
        firsts.append([have[s][bits[s]] for s in range(2)])
        for bit in all_bits:
            for mask in masks:
                for stream in (1, 0):
                    now = have[stream]
                    free = bit != bits[stream] and not mask & bit
                    if free and mask in now and (mask | bit) not in now:
                        others = maps if mask and chunk == 0 else []
                        now[mask | bit] = swap_in_turn(now[mask], bit, *others, flight=2 if chunk == 0 else 1)
        for stream in range(2):
            held[stream][chunk] = [have[stream][mask] for mask in masks]

    def beside(chunk, kind, *others):
        arrays = [
            [[a[m] for m in order[s][kind]] for a in held[s][max(chunk - 1, 0) : chunk + 1]] for s in range(2)
        ]
        if others:
            arrays[0][-1][0] = after(arrays[0][-1][0], *others)
        up, down = edges(chunk, depth, arrays)
        return lax.ppermute(up, "space", upward), lax.ppermute(down, "space", downward)

    gots = []
    gives = []
    result = None
    for chunk in range(CHUNKS):
        raw(chunk)
    shape = (2 * local_steps, planes, rows_x, rows_y)
    for chunk in range(CHUNKS):
        early = beside(chunk, 0)
        late = beside(chunk, 1, *early, *(gives[-1] if gives else []))
        used = [held[s][max(chunk - 1, 0) : chunk + 1] for s in range(2)]
        result, *give = apply(chunk, depth, order, sides, maps, early, late, used, shape, result)
        gives.append(give)
        gots.append([swap_in_turn(give[s], bits[s], flight=1 + min(chunk, 1)) for s in range(2)])
    for chunk in range(CHUNKS):
        result = place(chunk, depth, sides, gots[chunk], result)
    return result.reshape(2, local_steps, planes, rows_x, rows_y)


def solution(mesh):
    in_specs = (P("tm", "space", None, None), P("tm"), P(), P(), P())
    out_specs = P(None, "tm", "space", None, None)
    return jax.shard_map(local, mesh=mesh, in_specs=in_specs, out_specs=out_specs, check_vma=False)
```

```python
import functools

import jax
import jax.numpy as jnp
from jax import lax
from jax.experimental import pallas as pl
from jax.experimental.pallas import tpu as pltpu
from jax.sharding import PartitionSpec as P


CUTS = (0, 4, 8)
CHUNKS = len(CUTS) - 1
VMEM_LIMIT = 28 * 2**20
HBM = pl.BlockSpec(memory_space=pl.ANY)
VMEM = pl.BlockSpec(memory_space=pltpu.VMEM)
SCALARS = pl.BlockSpec(memory_space=pltpu.SMEM)
COST = 370000


def cost(weight):
    return pl.CostEstimate(flops=0, bytes_accessed=weight * COST, transcendentals=0)


def block_row(stream, side, row, depth, rows_x):
    if stream == 0:
        return row + side * (rows_x - 1 - 2 * row)
    return depth * (1 + side) + row


def own_rows(chunk, depth):
    bounds = [depth * cut // 8 for cut in CUTS]
    return list(range(bounds[chunk], bounds[chunk + 1]))


def chunk_rows(stream, chunk, depth):
    rows = own_rows(chunk, depth)
    first = rows[0] + 1 if chunk else (0 if stream == 0 else -1)
    return list(range(first, rows[-1] + 2))


def where_rows(stream, chunk, depth):
    places = {}
    for back in (1, 0):
        if chunk >= back:
            for at, row in enumerate(chunk_rows(stream, chunk - back, depth)):
                places[row] = (1 - back, at)
    return places


def run(copies):
    for copy in copies:
        copy.start()
    for copy in copies:
        copy.wait()


def pick_kernel(chunk, depth, kinds, bits, step_ref, in_ref, *refs):
    outs, sems = refs[:-1], refs[-1]
    steps, planes, rows_x, _ = in_ref.shape
    me = lax.axis_index("tm")
    jobs = []
    for place, (stream, other) in enumerate(kinds):
        side = jnp.where(jnp.bitwise_and(me, bits[stream]) > 0, 1, 0)
        side = 1 - side if other else side
        for at, row in enumerate(chunk_rows(stream, chunk, depth)):
            x = block_row(stream, side, row, depth, rows_x)
            for z in range(planes):
                out = outs[place].at[at, z]
                jobs.append((pltpu.make_async_copy(in_ref.at[:, z, x], out, sems.at[len(jobs)]), out))
    for copy, _ in jobs:
        copy.start()
    line = step_ref[...].astype(jnp.float32) / 8.0
    down = lax.broadcasted_iota(jnp.int32, (steps, steps), 0)
    along = lax.broadcasted_iota(jnp.int32, (steps, steps), 1)
    ratio = jnp.sum(jnp.where(down == along, line, 0.0), axis=1, keepdims=True)
    for copy, out in jobs:
        copy.wait()
        out[...] = out[...] * ratio


def pick(chunk, kinds, residual, step_ratio, bits, depth):
    steps, planes, _, rows_y = residual.shape
    counts = [len(chunk_rows(stream, chunk, depth)) for stream, _ in kinds]
    outs = pl.pallas_call(
        functools.partial(pick_kernel, chunk, depth, kinds, bits),
        out_shape=[jax.ShapeDtypeStruct((c, planes, steps, rows_y), jnp.float32) for c in counts],
        in_specs=[VMEM, HBM],
        out_specs=[VMEM] * len(kinds),
        scratch_shapes=[pltpu.SemaphoreType.DMA((sum(counts) * planes,))],
        compiler_params=pltpu.CompilerParams(vmem_limit_bytes=56 * 2**20),
        cost_estimate=cost(5),
        name="pick",
    )(step_ratio.reshape(1, steps), residual)
    return dict(zip(kinds, outs))


def edge_kernel(chunk, depth, groups, *refs):
    raws, (up_ref, down_ref, sems) = refs[:-3], refs[-3:]
    planes = raws[0].shape[1]
    backs = 2 if chunk else 1
    copies = []
    for stream in range(2):
        places = where_rows(stream, chunk, depth)
        for at, row in enumerate(own_rows(chunk, depth)):
            back, index = places[row]
            for group in range(groups):
                raw = raws[(stream * backs + back - 2 + backs) * groups + group]
                for z, out in ((planes - 1, up_ref), (0, down_ref)):
                    copy = pltpu.make_async_copy(
                        raw.at[index, z], out.at[stream, at, group], sems.at[len(copies)]
                    )
                    copies.append(copy)
    run(copies)


def edges(chunk, depth, raws):
    groups = len(raws[0][0])
    _, _, steps, rows_y = raws[0][0][0].shape
    flat = [raw for stream in raws for arrays in stream for raw in arrays]
    high = len(own_rows(chunk, depth))
    shape = jax.ShapeDtypeStruct((2, high, groups, steps, rows_y), jnp.float32)
    return pl.pallas_call(
        functools.partial(edge_kernel, chunk, depth, groups),
        out_shape=[shape] * 2,
        in_specs=[HBM] * len(flat),
        out_specs=[VMEM] * 2,
        scratch_shapes=[pltpu.SemaphoreType.DMA((4 * high * groups,))],
        compiler_params=pltpu.CompilerParams(vmem_limit_bytes=12 * 2**20),
        cost_estimate=cost(3),
        name="edges",
    )(*flat)


def halves(value):
    high = value.astype(jnp.bfloat16)
    return high, (value - high.astype(jnp.float32)).astype(jnp.bfloat16)


def apply_kernel(chunk, depth, order, sides_ref, map_a_ref, map_b_ref, *refs):
    (early_low, early_high, late_low, late_high), raws = refs[:4], refs[4:-5]
    out_ref, gives, own, sems = refs[-5], refs[-4:-2], refs[-2], refs[-1]
    groups = sum(len(part) for part in order[0])
    backs = 2 if chunk else 1
    _, planes, rows_x, rows_y = out_ref.shape
    stores = []
    for stream in range(2):
        maps = (map_a_ref, map_b_ref)[stream][...]
        half = maps.shape[0] // 2
        places = where_rows(stream, chunk, depth)

        def load(row, z):
            back, index = places[row]
            start = (stream * backs + back - 2 + backs) * groups
            return jnp.concatenate([raw[index, z] for raw in raws[start : start + groups]], axis=0)

        def outside(early, late, at):
            parts = {}
            for kind, ref in enumerate((early, late)):
                for place, group in enumerate(order[stream][kind]):
                    parts[group] = ref[stream, at, place]
            return jnp.concatenate([parts[group] for group in range(groups)], axis=0)

        for at, row in enumerate(own_rows(chunk, depth)):
            number = stream * len(own_rows(chunk, depth)) + at
            x = block_row(stream, sides_ref[stream], row, depth, rows_x)
            mids = [load(row, z) for z in range(planes)]
            for z, mid in enumerate(mids):
                lane = lax.broadcasted_iota(jnp.int32, mid.shape, 1)
                total = jnp.where(lane == 0, 0.0, pltpu.roll(mid, 1, 1))
                total = total + jnp.where(lane == rows_y - 1, 0.0, pltpu.roll(mid, rows_y - 1, 1))
                for beside in (row - 1, row + 1):
                    if beside in places:
                        total = total + load(beside, z)
                total = total + (mids[z - 1] if z else outside(early_low, late_low, at))
                total = total + (mids[z + 1] if z < planes - 1 else outside(early_high, late_high, at))
                mid_h, mid_l = halves(mid)
                sum_h, sum_l = halves(total)
                stack = jnp.concatenate([mid_h, mid_h, mid_l, sum_h, sum_h, sum_l], axis=0)
                value = jnp.dot(maps, stack, preferred_element_type=jnp.float32)
                own[number, z] = value[:half]
                gives[stream][at, z] = value[half:]
                store = pltpu.make_async_copy(own.at[number, z], out_ref.at[:, z, x], sems.at[number, z])
                store.start()
                stores.append(store)
    for store in stores:
        store.wait()


def apply(chunk, depth, order, sides, maps, early, late, raws, shape, result):
    _, planes, _, rows_y = raws[0][0][0].shape
    high = len(own_rows(chunk, depth))
    half = shape[0]
    flat = [raw for stream in raws for arrays in stream for raw in arrays]
    first = [] if result is None else [result]
    give = jax.ShapeDtypeStruct((high, planes, half, rows_y), jnp.float32)
    count = 3 + 4 + len(flat)

    def body(*refs):
        refs = refs[:count] + refs[count + len(first) :]
        apply_kernel(chunk, depth, order, *refs)

    return pl.pallas_call(
        body,
        out_shape=[jax.ShapeDtypeStruct(shape, jnp.float32), give, give],
        in_specs=[SCALARS] + [VMEM] * (count - 1) + [HBM] * len(first),
        out_specs=[HBM, VMEM, VMEM],
        scratch_shapes=[
            pltpu.VMEM((2 * high, planes, half, rows_y), jnp.float32),
            pltpu.SemaphoreType.DMA((2 * high, planes)),
        ],
        input_output_aliases={count: 0} if first else {},
        compiler_params=pltpu.CompilerParams(vmem_limit_bytes=VMEM_LIMIT),
        cost_estimate=cost(10),
        name="apply",
    )(sides, *maps, *early, *late, *flat, *first)


def place_kernel(chunk, depth, sides_ref, got_a, got_b, _, out_ref, sems):
    _, planes, rows_x, _ = out_ref.shape
    copies = []
    for stream, got in enumerate((got_a, got_b)):
        for at, row in enumerate(own_rows(chunk, depth)):
            x = block_row(stream, 1 - sides_ref[stream], row, depth, rows_x)
            for z in range(planes):
                copies.append(pltpu.make_async_copy(got.at[at, z], out_ref.at[:, z, x], sems.at[len(copies)]))
    run(copies)


def place(chunk, depth, sides, got, result):
    planes = result.shape[1]
    return pl.pallas_call(
        functools.partial(place_kernel, chunk, depth),
        out_shape=jax.ShapeDtypeStruct(result.shape, jnp.float32),
        in_specs=[SCALARS, VMEM, VMEM, HBM],
        out_specs=HBM,
        scratch_shapes=[pltpu.SemaphoreType.DMA((2 * len(own_rows(chunk, depth)) * planes,))],
        input_output_aliases={3: 0},
        compiler_params=pltpu.CompilerParams(vmem_limit_bytes=12 * 2**20),
        cost_estimate=cost(2),
        name="place",
    )(sides, *got, result)


def after(value, *others):
    return lax.optimization_barrier((value, *others))[0]


def maps_kernel(bits, me_ref, ahead_ref, back_ref, eigen_ref, *outs):
    steps = ahead_ref.shape[1]
    local_steps = outs[0].shape[0] // 4
    me = me_ref[0]
    real_part = 6.0 + eigen_ref[0:1, :]
    imag_part = eigen_ref[1:2, :]
    denom = real_part * real_part + imag_part * imag_part
    coef_re = real_part / denom
    coef_im = -imag_part / denom
    left = []
    for block in (me, jnp.bitwise_xor(me, bits[0]), jnp.bitwise_xor(me, bits[1])):
        span = pl.ds(pl.multiple_of(block * local_steps, local_steps), local_steps)
        back_re, back_im = back_ref[0, span, :], back_ref[1, span, :]
        for _ in range(2):
            back_re, back_im = back_re * coef_re - back_im * coef_im, back_re * coef_im + back_im * coef_re
            left += [back_re, back_im]
    left = jnp.concatenate(left, axis=0)
    by_re = jnp.dot(left, ahead_ref[0], precision=lax.Precision.HIGHEST, preferred_element_type=jnp.float32)
    by_im = jnp.dot(left, ahead_ref[1], precision=lax.Precision.HIGHEST, preferred_element_type=jnp.float32)

    def piece(data, which):
        return data[which * local_steps : (which + 1) * local_steps]

    row = lax.broadcasted_iota(jnp.int32, (steps, steps), 0)
    column = lax.broadcasted_iota(jnp.int32, (steps, steps), 1)
    turn = (row == jnp.bitwise_xor(column, me * local_steps)).astype(jnp.float32).astype(jnp.bfloat16)
    parts = []
    for block in range(3):
        for power in range(2):
            at = 2 * (2 * block + power)
            both = jnp.concatenate(
                [piece(by_re, at) - piece(by_im, at + 1), piece(by_im, at) + piece(by_re, at + 1)], axis=0
            )
            pair = jnp.concatenate(halves(both), axis=0)
            parts.append(jnp.dot(pair, turn, preferred_element_type=jnp.float32).astype(jnp.bfloat16))
    half = 2 * local_steps
    for out, blocks in zip(outs, ((0, 1), (0, 2))):
        for place, block in enumerate(blocks):
            once, twice = parts[2 * block], parts[2 * block + 1]
            columns = (once[:half], once[half:], once[:half], twice[:half], twice[half:], twice[:half])
            for c, value in enumerate(columns):
                out[place * half : (place + 1) * half, c * steps : (c + 1) * steps] = value


def make_maps(forward_map, back_map, eigen_values, me, count, bits):
    steps = forward_map.shape[1]
    shape = jax.ShapeDtypeStruct((4 * steps // count, 6 * steps), jnp.bfloat16)
    return pl.pallas_call(
        functools.partial(maps_kernel, bits),
        out_shape=[shape, shape],
        in_specs=[SCALARS] + [VMEM] * 3,
        out_specs=[VMEM] * 2,
        compiler_params=pltpu.CompilerParams(vmem_limit_bytes=VMEM_LIMIT),
        cost_estimate=cost(2),
        name="maps",
    )(me.astype(jnp.int32).reshape(1), forward_map, back_map, eigen_values)


def local(residual, step_ratio, forward_map, back_map, eigen_values):
    local_steps, planes, rows_x, rows_y = residual.shape
    depth = rows_x // 4
    count = lax.axis_size("tm")
    bits = (1, count // 2)
    all_bits = [1 << k for k in range(count.bit_length() - 1)]
    me = lax.axis_index("tm")
    sides = jnp.stack([jnp.where(jnp.bitwise_and(me, b) > 0, 1, 0) for b in bits]).astype(jnp.int32)
    ratio = jnp.broadcast_to((step_ratio.astype(jnp.float32) / 8.0)[:, None], (local_steps, rows_y))

    def swap(data, bit):
        return lax.ppermute(data, "tm", [(i, i ^ bit) for i in range(count)])

    spaces = lax.axis_size("space")
    upward = [(i, i + 1) for i in range(spaces - 1)]
    downward = [(i + 1, i) for i in range(spaces - 1)]

    queues = [[], []]

    def swap_in_turn(data, bit, *others, flight=1):
        queue = queues[0 if bit == bits[0] else 1]
        if len(queue) >= flight:
            others = (queue[-flight], *others)
        if others:
            data = after(data, *others)
        got = swap(data, bit)
        queue.append(got)
        return got

    masks = range(count)
    order = [[[m for m in masks if m in (0, b)], [m for m in masks if m not in (0, b)]] for b in bits]
    held = [[None] * CHUNKS for _ in range(2)]

    maps = make_maps(forward_map, back_map, eigen_values, me, count, bits)
    firsts = []

    def raw(chunk):
        data = after(residual, *firsts[-1]) if firsts else residual
        sent, kept = ((0, 1), (1, 1)), ((0, 0), (1, 0))
        mine = {}
        for kinds in (sent + kept,) if chunk else (sent, kept):
            mine.update(pick(chunk, kinds, data, step_ratio, bits, depth))
        have = [{0: mine[s, 0], bits[s]: swap_in_turn(mine[s, 1], bits[s])} for s in range(2)]
        firsts.append([have[s][bits[s]] for s in range(2)])
        for bit in all_bits:
            for mask in masks:
                for stream in (1, 0):
                    now = have[stream]
                    free = bit != bits[stream] and not mask & bit
                    if free and mask in now and (mask | bit) not in now:
                        others = maps if mask and chunk == 0 else []
                        now[mask | bit] = swap_in_turn(now[mask], bit, *others, flight=2 if chunk == 0 else 1)
        for stream in range(2):
            held[stream][chunk] = [have[stream][mask] for mask in masks]

    def beside(chunk, kind, *others):
        arrays = [
            [[a[m] for m in order[s][kind]] for a in held[s][max(chunk - 1, 0) : chunk + 1]] for s in range(2)
        ]
        if others:
            arrays[0][-1][0] = after(arrays[0][-1][0], *others)
        up, down = edges(chunk, depth, arrays)
        return lax.ppermute(up, "space", upward), lax.ppermute(down, "space", downward)

    gots = []
    gives = []
    result = None
    for chunk in range(CHUNKS):
        raw(chunk)
    shape = (2 * local_steps, planes, rows_x, rows_y)
    for chunk in range(CHUNKS):
        early = beside(chunk, 0)
        late = beside(chunk, 1, *early, *(gives[-1] if gives else []))
        used = [held[s][max(chunk - 1, 0) : chunk + 1] for s in range(2)]
        result, *give = apply(chunk, depth, order, sides, maps, early, late, used, shape, result)
        gives.append(give)
        gots.append([swap_in_turn(give[s], bits[s], flight=1 + min(chunk, 1)) for s in range(2)])
    for chunk in range(CHUNKS):
        result = place(chunk, depth, sides, gots[chunk], result)
    return result.reshape(2, local_steps, planes, rows_x, rows_y)


def solution(mesh):
    in_specs = (P("tm", "space", None, None), P("tm"), P(), P(), P())
    out_specs = P(None, "tm", "space", None, None)
    return jax.shard_map(local, mesh=mesh, in_specs=in_specs, out_specs=out_specs, check_vma=False)
```

```python
import functools

import jax
import jax.numpy as jnp
from jax import lax
from jax.experimental import pallas as pl
from jax.experimental.pallas import tpu as pltpu
from jax.sharding import PartitionSpec as P


CUTS = (0, 4, 8)
CHUNKS = len(CUTS) - 1
VMEM_LIMIT = 28 * 2**20
HBM = pl.BlockSpec(memory_space=pl.ANY)
VMEM = pl.BlockSpec(memory_space=pltpu.VMEM)
SCALARS = pl.BlockSpec(memory_space=pltpu.SMEM)
COST = 370000


def cost(weight):
    return pl.CostEstimate(flops=0, bytes_accessed=weight * COST, transcendentals=0)


def block_row(stream, side, row, depth, rows_x):
    if stream == 0:
        return row + side * (rows_x - 1 - 2 * row)
    return depth * (1 + side) + row


def own_rows(chunk, depth):
    bounds = [depth * cut // 8 for cut in CUTS]
    return list(range(bounds[chunk], bounds[chunk + 1]))


def chunk_rows(stream, chunk, depth):
    rows = own_rows(chunk, depth)
    first = rows[0] + 1 if chunk else (0 if stream == 0 else -1)
    return list(range(first, rows[-1] + 2))


def where_rows(stream, chunk, depth):
    places = {}
    for back in (1, 0):
        if chunk >= back:
            for at, row in enumerate(chunk_rows(stream, chunk - back, depth)):
                places[row] = (1 - back, at)
    return places


def run(copies):
    for copy in copies:
        copy.start()
    for copy in copies:
        copy.wait()


def pick_kernel(chunk, depth, kinds, bits, step_ref, in_ref, *refs):
    outs, sems = refs[:-1], refs[-1]
    steps, planes, rows_x, _ = in_ref.shape
    me = lax.axis_index("tm")
    jobs = []
    for place, (stream, other) in enumerate(kinds):
        side = jnp.where(jnp.bitwise_and(me, bits[stream]) > 0, 1, 0)
        side = 1 - side if other else side
        for at, row in enumerate(chunk_rows(stream, chunk, depth)):
            x = block_row(stream, side, row, depth, rows_x)
            for z in range(planes):
                out = outs[place].at[at, z]
                jobs.append((pltpu.make_async_copy(in_ref.at[:, z, x], out, sems.at[len(jobs)]), out))
    for copy, _ in jobs:
        copy.start()
    line = step_ref[...].astype(jnp.float32) / 8.0
    down = lax.broadcasted_iota(jnp.int32, (steps, steps), 0)
    along = lax.broadcasted_iota(jnp.int32, (steps, steps), 1)
    ratio = jnp.sum(jnp.where(down == along, line, 0.0), axis=1, keepdims=True)
    for copy, out in jobs:
        copy.wait()
        out[...] = out[...] * ratio


def pick(chunk, kinds, residual, step_ratio, bits, depth):
    steps, planes, _, rows_y = residual.shape
    counts = [len(chunk_rows(stream, chunk, depth)) for stream, _ in kinds]
    first = chunk == 0 and kinds[0][1]
    limit = (56 if first else 8) * 2**20
    outs = pl.pallas_call(
        functools.partial(pick_kernel, chunk, depth, kinds, bits),
        out_shape=[jax.ShapeDtypeStruct((c, planes, steps, rows_y), jnp.float32) for c in counts],
        in_specs=[VMEM, HBM],
        out_specs=[VMEM] * len(kinds),
        scratch_shapes=[pltpu.SemaphoreType.DMA((sum(counts) * planes,))],
        compiler_params=pltpu.CompilerParams(vmem_limit_bytes=limit),
        cost_estimate=cost(5),
        name="pick",
    )(step_ratio.reshape(1, steps), residual)
    return dict(zip(kinds, outs))


def edge_kernel(chunk, depth, groups, *refs):
    raws, (up_ref, down_ref, sems) = refs[:-3], refs[-3:]
    planes = raws[0].shape[1]
    backs = 2 if chunk else 1
    copies = []
    for stream in range(2):
        places = where_rows(stream, chunk, depth)
        for at, row in enumerate(own_rows(chunk, depth)):
            back, index = places[row]
            for group in range(groups):
                raw = raws[(stream * backs + back - 2 + backs) * groups + group]
                for z, out in ((planes - 1, up_ref), (0, down_ref)):
                    copy = pltpu.make_async_copy(
                        raw.at[index, z], out.at[stream, at, group], sems.at[len(copies)]
                    )
                    copies.append(copy)
    run(copies)


def edges(chunk, depth, raws):
    groups = len(raws[0][0])
    _, _, steps, rows_y = raws[0][0][0].shape
    flat = [raw for stream in raws for arrays in stream for raw in arrays]
    high = len(own_rows(chunk, depth))
    shape = jax.ShapeDtypeStruct((2, high, groups, steps, rows_y), jnp.float32)
    return pl.pallas_call(
        functools.partial(edge_kernel, chunk, depth, groups),
        out_shape=[shape] * 2,
        in_specs=[HBM] * len(flat),
        out_specs=[VMEM] * 2,
        scratch_shapes=[pltpu.SemaphoreType.DMA((4 * high * groups,))],
        compiler_params=pltpu.CompilerParams(vmem_limit_bytes=12 * 2**20),
        cost_estimate=cost(3),
        name="edges",
    )(*flat)


def halves(value):
    high = value.astype(jnp.bfloat16)
    return high, (value - high.astype(jnp.float32)).astype(jnp.bfloat16)


def apply_kernel(chunk, depth, order, sides_ref, map_a_ref, map_b_ref, *refs):
    (early_low, early_high, late_low, late_high), raws = refs[:4], refs[4:-5]
    out_ref, gives, own, sems = refs[-5], refs[-4:-2], refs[-2], refs[-1]
    groups = sum(len(part) for part in order[0])
    backs = 2 if chunk else 1
    _, planes, rows_x, rows_y = out_ref.shape
    stores = []
    for stream in range(2):
        maps = (map_a_ref, map_b_ref)[stream][...]
        half = maps.shape[0] // 2
        places = where_rows(stream, chunk, depth)

        def load(row, z):
            back, index = places[row]
            start = (stream * backs + back - 2 + backs) * groups
            return jnp.concatenate([raw[index, z] for raw in raws[start : start + groups]], axis=0)

        def outside(early, late, at):
            parts = {}
            for kind, ref in enumerate((early, late)):
                for place, group in enumerate(order[stream][kind]):
                    parts[group] = ref[stream, at, place]
            return jnp.concatenate([parts[group] for group in range(groups)], axis=0)

        for at, row in enumerate(own_rows(chunk, depth)):
            number = stream * len(own_rows(chunk, depth)) + at
            x = block_row(stream, sides_ref[stream], row, depth, rows_x)
            mids = [load(row, z) for z in range(planes)]
            for z, mid in enumerate(mids):
                lane = lax.broadcasted_iota(jnp.int32, mid.shape, 1)
                total = jnp.where(lane == 0, 0.0, pltpu.roll(mid, 1, 1))
                total = total + jnp.where(lane == rows_y - 1, 0.0, pltpu.roll(mid, rows_y - 1, 1))
                for beside in (row - 1, row + 1):
                    if beside in places:
                        total = total + load(beside, z)
                total = total + (mids[z - 1] if z else outside(early_low, late_low, at))
                total = total + (mids[z + 1] if z < planes - 1 else outside(early_high, late_high, at))
                mid_h, mid_l = halves(mid)
                sum_h, sum_l = halves(total)
                stack = jnp.concatenate([mid_h, mid_h, mid_l, sum_h, sum_h, sum_l], axis=0)
                value = jnp.dot(maps, stack, preferred_element_type=jnp.float32)
                own[number, z] = value[:half]
                gives[stream][at, z] = value[half:]
                store = pltpu.make_async_copy(own.at[number, z], out_ref.at[:, z, x], sems.at[number, z])
                store.start()
                stores.append(store)
    for store in stores:
        store.wait()


def apply(chunk, depth, order, sides, maps, early, late, raws, shape, result):
    _, planes, _, rows_y = raws[0][0][0].shape
    high = len(own_rows(chunk, depth))
    half = shape[0]
    flat = [raw for stream in raws for arrays in stream for raw in arrays]
    first = [] if result is None else [result]
    give = jax.ShapeDtypeStruct((high, planes, half, rows_y), jnp.float32)
    count = 3 + 4 + len(flat)

    def body(*refs):
        refs = refs[:count] + refs[count + len(first) :]
        apply_kernel(chunk, depth, order, *refs)

    return pl.pallas_call(
        body,
        out_shape=[jax.ShapeDtypeStruct(shape, jnp.float32), give, give],
        in_specs=[SCALARS] + [VMEM] * (count - 1) + [HBM] * len(first),
        out_specs=[HBM, VMEM, VMEM],
        scratch_shapes=[
            pltpu.VMEM((2 * high, planes, half, rows_y), jnp.float32),
            pltpu.SemaphoreType.DMA((2 * high, planes)),
        ],
        input_output_aliases={count: 0} if first else {},
        compiler_params=pltpu.CompilerParams(vmem_limit_bytes=VMEM_LIMIT),
        cost_estimate=cost(10),
        name="apply",
    )(sides, *maps, *early, *late, *flat, *first)


def place_kernel(chunk, depth, sides_ref, got_a, got_b, _, out_ref, sems):
    _, planes, rows_x, _ = out_ref.shape
    copies = []
    for stream, got in enumerate((got_a, got_b)):
        for at, row in enumerate(own_rows(chunk, depth)):
            x = block_row(stream, 1 - sides_ref[stream], row, depth, rows_x)
            for z in range(planes):
                copies.append(pltpu.make_async_copy(got.at[at, z], out_ref.at[:, z, x], sems.at[len(copies)]))
    run(copies)


def place(chunk, depth, sides, got, result):
    planes = result.shape[1]
    return pl.pallas_call(
        functools.partial(place_kernel, chunk, depth),
        out_shape=jax.ShapeDtypeStruct(result.shape, jnp.float32),
        in_specs=[SCALARS, VMEM, VMEM, HBM],
        out_specs=HBM,
        scratch_shapes=[pltpu.SemaphoreType.DMA((2 * len(own_rows(chunk, depth)) * planes,))],
        input_output_aliases={3: 0},
        compiler_params=pltpu.CompilerParams(vmem_limit_bytes=12 * 2**20),
        cost_estimate=cost(2),
        name="place",
    )(sides, *got, result)


def after(value, *others):
    return lax.optimization_barrier((value, *others))[0]


def maps_kernel(bits, me_ref, ahead_ref, back_ref, eigen_ref, *outs):
    steps = ahead_ref.shape[1]
    local_steps = outs[0].shape[0] // 4
    me = me_ref[0]
    real_part = 6.0 + eigen_ref[0:1, :]
    imag_part = eigen_ref[1:2, :]
    denom = real_part * real_part + imag_part * imag_part
    coef_re = real_part / denom
    coef_im = -imag_part / denom
    left = []
    for block in (me, jnp.bitwise_xor(me, bits[0]), jnp.bitwise_xor(me, bits[1])):
        span = pl.ds(pl.multiple_of(block * local_steps, local_steps), local_steps)
        back_re, back_im = back_ref[0, span, :], back_ref[1, span, :]
        for _ in range(2):
            back_re, back_im = back_re * coef_re - back_im * coef_im, back_re * coef_im + back_im * coef_re
            left += [back_re, back_im]
    left = jnp.concatenate(left, axis=0)
    by_re = jnp.dot(left, ahead_ref[0], precision=lax.Precision.HIGHEST, preferred_element_type=jnp.float32)
    by_im = jnp.dot(left, ahead_ref[1], precision=lax.Precision.HIGHEST, preferred_element_type=jnp.float32)

    def piece(data, which):
        return data[which * local_steps : (which + 1) * local_steps]

    row = lax.broadcasted_iota(jnp.int32, (steps, steps), 0)
    column = lax.broadcasted_iota(jnp.int32, (steps, steps), 1)
    turn = (row == jnp.bitwise_xor(column, me * local_steps)).astype(jnp.float32).astype(jnp.bfloat16)
    parts = []
    for block in range(3):
        for power in range(2):
            at = 2 * (2 * block + power)
            both = jnp.concatenate(
                [piece(by_re, at) - piece(by_im, at + 1), piece(by_im, at) + piece(by_re, at + 1)], axis=0
            )
            pair = jnp.concatenate(halves(both), axis=0)
            parts.append(jnp.dot(pair, turn, preferred_element_type=jnp.float32).astype(jnp.bfloat16))
    half = 2 * local_steps
    for out, blocks in zip(outs, ((0, 1), (0, 2))):
        for place, block in enumerate(blocks):
            once, twice = parts[2 * block], parts[2 * block + 1]
            columns = (once[:half], once[half:], once[:half], twice[:half], twice[half:], twice[:half])
            for c, value in enumerate(columns):
                out[place * half : (place + 1) * half, c * steps : (c + 1) * steps] = value


def make_maps(forward_map, back_map, eigen_values, me, count, bits):
    steps = forward_map.shape[1]
    shape = jax.ShapeDtypeStruct((4 * steps // count, 6 * steps), jnp.bfloat16)
    return pl.pallas_call(
        functools.partial(maps_kernel, bits),
        out_shape=[shape, shape],
        in_specs=[SCALARS] + [VMEM] * 3,
        out_specs=[VMEM] * 2,
        compiler_params=pltpu.CompilerParams(vmem_limit_bytes=VMEM_LIMIT),
        cost_estimate=cost(2),
        name="maps",
    )(me.astype(jnp.int32).reshape(1), forward_map, back_map, eigen_values)


def local(residual, step_ratio, forward_map, back_map, eigen_values):
    local_steps, planes, rows_x, rows_y = residual.shape
    depth = rows_x // 4
    count = lax.axis_size("tm")
    bits = (1, count // 2)
    all_bits = [1 << k for k in range(count.bit_length() - 1)]
    me = lax.axis_index("tm")
    sides = jnp.stack([jnp.where(jnp.bitwise_and(me, b) > 0, 1, 0) for b in bits]).astype(jnp.int32)
    ratio = jnp.broadcast_to((step_ratio.astype(jnp.float32) / 8.0)[:, None], (local_steps, rows_y))

    def swap(data, bit):
        return lax.ppermute(data, "tm", [(i, i ^ bit) for i in range(count)])

    spaces = lax.axis_size("space")
    upward = [(i, i + 1) for i in range(spaces - 1)]
    downward = [(i + 1, i) for i in range(spaces - 1)]

    queues = [[], []]

    def swap_in_turn(data, bit, *others, flight=1):
        queue = queues[0 if bit == bits[0] else 1]
        if len(queue) >= flight:
            others = (queue[-flight], *others)
        if others:
            data = after(data, *others)
        got = swap(data, bit)
        queue.append(got)
        return got

    masks = range(count)
    order = [[[m for m in masks if m in (0, b)], [m for m in masks if m not in (0, b)]] for b in bits]
    held = [[None] * CHUNKS for _ in range(2)]

    maps = make_maps(forward_map, back_map, eigen_values, me, count, bits)
    firsts = []

    def raw(chunk):
        data = after(residual, *firsts[-1]) if firsts else residual
        sent, kept = ((0, 1), (1, 1)), ((0, 0), (1, 0))
        mine = {}
        for kinds in (sent + kept,) if chunk else (sent, kept):
            mine.update(pick(chunk, kinds, data, step_ratio, bits, depth))
        have = [{0: mine[s, 0], bits[s]: swap_in_turn(mine[s, 1], bits[s])} for s in range(2)]
        firsts.append([have[s][bits[s]] for s in range(2)])
        for bit in all_bits:
            for mask in masks:
                for stream in (1, 0):
                    now = have[stream]
                    free = bit != bits[stream] and not mask & bit
                    if free and mask in now and (mask | bit) not in now:
                        others = maps if mask and chunk == 0 else []
                        now[mask | bit] = swap_in_turn(now[mask], bit, *others, flight=2 if chunk == 0 else 1)
        for stream in range(2):
            held[stream][chunk] = [have[stream][mask] for mask in masks]

    def beside(chunk, kind, *others):
        arrays = [
            [[a[m] for m in order[s][kind]] for a in held[s][max(chunk - 1, 0) : chunk + 1]] for s in range(2)
        ]
        if others:
            arrays[0][-1][0] = after(arrays[0][-1][0], *others)
        up, down = edges(chunk, depth, arrays)
        return lax.ppermute(up, "space", upward), lax.ppermute(down, "space", downward)

    gots = []
    gives = []
    result = None
    for chunk in range(CHUNKS):
        raw(chunk)
    shape = (2 * local_steps, planes, rows_x, rows_y)
    for chunk in range(CHUNKS):
        early = beside(chunk, 0)
        late = beside(chunk, 1, *early, *(gives[-1] if gives else []))
        used = [held[s][max(chunk - 1, 0) : chunk + 1] for s in range(2)]
        result, *give = apply(chunk, depth, order, sides, maps, early, late, used, shape, result)
        gives.append(give)
        gots.append([swap_in_turn(give[s], bits[s], flight=1 + min(chunk, 1)) for s in range(2)])
    for chunk in range(CHUNKS):
        result = place(chunk, depth, sides, gots[chunk], result)
    return result.reshape(2, local_steps, planes, rows_x, rows_y)


def solution(mesh):
    in_specs = (P("tm", "space", None, None), P("tm"), P(), P(), P())
    out_specs = P(None, "tm", "space", None, None)
    return jax.shard_map(local, mesh=mesh, in_specs=in_specs, out_specs=out_specs, check_vma=False)
```

```python
import functools

import jax
import jax.numpy as jnp
from jax import lax
from jax.experimental import pallas as pl
from jax.experimental.pallas import tpu as pltpu
from jax.sharding import PartitionSpec as P


CUTS = (0, 4, 8)
CHUNKS = len(CUTS) - 1
VMEM_LIMIT = 16 * 2**20
HBM = pl.BlockSpec(memory_space=pl.ANY)
VMEM = pl.BlockSpec(memory_space=pltpu.VMEM)
SCALARS = pl.BlockSpec(memory_space=pltpu.SMEM)
COST = 370000


def cost(weight):
    return pl.CostEstimate(flops=0, bytes_accessed=weight * COST, transcendentals=0)


def block_row(stream, side, row, depth, rows_x):
    if stream == 0:
        return row + side * (rows_x - 1 - 2 * row)
    return depth * (1 + side) + row


def own_rows(chunk, depth):
    bounds = [depth * cut // 8 for cut in CUTS]
    return list(range(bounds[chunk], bounds[chunk + 1]))


def chunk_rows(stream, chunk, depth):
    rows = own_rows(chunk, depth)
    first = rows[0] + 1 if chunk else (0 if stream == 0 else -1)
    return list(range(first, rows[-1] + 2))


def where_rows(stream, chunk, depth):
    places = {}
    for back in (1, 0):
        if chunk >= back:
            for at, row in enumerate(chunk_rows(stream, chunk - back, depth)):
                places[row] = (1 - back, at)
    return places


def run(copies):
    for copy in copies:
        copy.start()
    for copy in copies:
        copy.wait()


def pick_kernel(chunk, depth, kinds, bits, step_ref, in_ref, *refs):
    outs, sems = refs[:-1], refs[-1]
    steps, planes, rows_x, _ = in_ref.shape
    me = lax.axis_index("tm")
    jobs = []
    for place, (stream, other) in enumerate(kinds):
        side = jnp.where(jnp.bitwise_and(me, bits[stream]) > 0, 1, 0)
        side = 1 - side if other else side
        for at, row in enumerate(chunk_rows(stream, chunk, depth)):
            x = block_row(stream, side, row, depth, rows_x)
            for z in range(planes):
                out = outs[place].at[at, z]
                jobs.append((pltpu.make_async_copy(in_ref.at[:, z, x], out, sems.at[len(jobs)]), out))
    for copy, _ in jobs:
        copy.start()
    line = step_ref[...].astype(jnp.float32) / 8.0
    down = lax.broadcasted_iota(jnp.int32, (steps, steps), 0)
    along = lax.broadcasted_iota(jnp.int32, (steps, steps), 1)
    ratio = jnp.sum(jnp.where(down == along, line, 0.0), axis=1, keepdims=True)
    for copy, out in jobs:
        copy.wait()
        out[...] = out[...] * ratio


def pick(chunk, kinds, residual, step_ratio, bits, depth):
    steps, planes, _, rows_y = residual.shape
    counts = [len(chunk_rows(stream, chunk, depth)) for stream, _ in kinds]
    first = chunk == 0 and kinds[0][1]
    limit = (56 if first else 8) * 2**20
    outs = pl.pallas_call(
        functools.partial(pick_kernel, chunk, depth, kinds, bits),
        out_shape=[jax.ShapeDtypeStruct((c, planes, steps, rows_y), jnp.float32) for c in counts],
        in_specs=[VMEM, HBM],
        out_specs=[VMEM] * len(kinds),
        scratch_shapes=[pltpu.SemaphoreType.DMA((sum(counts) * planes,))],
        compiler_params=pltpu.CompilerParams(vmem_limit_bytes=limit),
        cost_estimate=cost(5),
        name="pick",
    )(step_ratio.reshape(1, steps), residual)
    return dict(zip(kinds, outs))


def edge_kernel(chunk, depth, groups, *refs):
    raws, (up_ref, down_ref, sems) = refs[:-3], refs[-3:]
    planes = raws[0].shape[1]
    backs = 2 if chunk else 1
    copies = []
    for stream in range(2):
        places = where_rows(stream, chunk, depth)
        for at, row in enumerate(own_rows(chunk, depth)):
            back, index = places[row]
            for group in range(groups):
                raw = raws[(stream * backs + back - 2 + backs) * groups + group]
                for z, out in ((planes - 1, up_ref), (0, down_ref)):
                    copy = pltpu.make_async_copy(
                        raw.at[index, z], out.at[stream, at, group], sems.at[len(copies)]
                    )
                    copies.append(copy)
    run(copies)


def edges(chunk, depth, raws):
    groups = len(raws[0][0])
    _, _, steps, rows_y = raws[0][0][0].shape
    flat = [raw for stream in raws for arrays in stream for raw in arrays]
    high = len(own_rows(chunk, depth))
    shape = jax.ShapeDtypeStruct((2, high, groups, steps, rows_y), jnp.float32)
    return pl.pallas_call(
        functools.partial(edge_kernel, chunk, depth, groups),
        out_shape=[shape] * 2,
        in_specs=[HBM] * len(flat),
        out_specs=[VMEM] * 2,
        scratch_shapes=[pltpu.SemaphoreType.DMA((4 * high * groups,))],
        compiler_params=pltpu.CompilerParams(vmem_limit_bytes=8 * 2**20),
        cost_estimate=cost(3),
        name="edges",
    )(*flat)


def halves(value):
    high = value.astype(jnp.bfloat16)
    return high, (value - high.astype(jnp.float32)).astype(jnp.bfloat16)


def apply_kernel(chunk, depth, order, sides_ref, map_a_ref, map_b_ref, *refs):
    (early_low, early_high, late_low, late_high), raws = refs[:4], refs[4:-5]
    out_ref, gives, own, sems = refs[-5], refs[-4:-2], refs[-2], refs[-1]
    groups = sum(len(part) for part in order[0])
    backs = 2 if chunk else 1
    _, planes, rows_x, rows_y = out_ref.shape
    stores = []
    for stream in range(2):
        maps = (map_a_ref, map_b_ref)[stream][...]
        half = maps.shape[0] // 2
        places = where_rows(stream, chunk, depth)

        def load(row, z):
            back, index = places[row]
            start = (stream * backs + back - 2 + backs) * groups
            return jnp.concatenate([raw[index, z] for raw in raws[start : start + groups]], axis=0)

        def outside(early, late, at):
            parts = {}
            for kind, ref in enumerate((early, late)):
                for place, group in enumerate(order[stream][kind]):
                    parts[group] = ref[stream, at, place]
            return jnp.concatenate([parts[group] for group in range(groups)], axis=0)

        for at, row in enumerate(own_rows(chunk, depth)):
            number = stream * len(own_rows(chunk, depth)) + at
            x = block_row(stream, sides_ref[stream], row, depth, rows_x)
            mids = [load(row, z) for z in range(planes)]
            for z, mid in enumerate(mids):
                lane = lax.broadcasted_iota(jnp.int32, mid.shape, 1)
                total = jnp.where(lane == 0, 0.0, pltpu.roll(mid, 1, 1))
                total = total + jnp.where(lane == rows_y - 1, 0.0, pltpu.roll(mid, rows_y - 1, 1))
                for beside in (row - 1, row + 1):
                    if beside in places:
                        total = total + load(beside, z)
                total = total + (mids[z - 1] if z else outside(early_low, late_low, at))
                total = total + (mids[z + 1] if z < planes - 1 else outside(early_high, late_high, at))
                mid_h, mid_l = halves(mid)
                sum_h, sum_l = halves(total)
                stack = jnp.concatenate([mid_h, mid_h, mid_l, sum_h, sum_h, sum_l], axis=0)
                value = jnp.dot(maps, stack, preferred_element_type=jnp.float32)
                own[number, z] = value[:half]
                gives[stream][at, z] = value[half:]
                store = pltpu.make_async_copy(own.at[number, z], out_ref.at[:, z, x], sems.at[number, z])
                store.start()
                stores.append(store)
    for store in stores:
        store.wait()


def apply(chunk, depth, order, sides, maps, early, late, raws, shape, result):
    _, planes, _, rows_y = raws[0][0][0].shape
    high = len(own_rows(chunk, depth))
    half = shape[0]
    flat = [raw for stream in raws for arrays in stream for raw in arrays]
    first = [] if result is None else [result]
    give = jax.ShapeDtypeStruct((high, planes, half, rows_y), jnp.float32)
    count = 3 + 4 + len(flat)

    def body(*refs):
        refs = refs[:count] + refs[count + len(first) :]
        apply_kernel(chunk, depth, order, *refs)

    return pl.pallas_call(
        body,
        out_shape=[jax.ShapeDtypeStruct(shape, jnp.float32), give, give],
        in_specs=[SCALARS] + [VMEM] * (count - 1) + [HBM] * len(first),
        out_specs=[HBM, VMEM, VMEM],
        scratch_shapes=[
            pltpu.VMEM((2 * high, planes, half, rows_y), jnp.float32),
            pltpu.SemaphoreType.DMA((2 * high, planes)),
        ],
        input_output_aliases={count: 0} if first else {},
        compiler_params=pltpu.CompilerParams(vmem_limit_bytes=VMEM_LIMIT),
        cost_estimate=cost(10),
        name="apply",
    )(sides, *maps, *early, *late, *flat, *first)


def place_kernel(chunk, depth, sides_ref, got_a, got_b, _, out_ref, sems):
    _, planes, rows_x, _ = out_ref.shape
    copies = []
    for stream, got in enumerate((got_a, got_b)):
        for at, row in enumerate(own_rows(chunk, depth)):
            x = block_row(stream, 1 - sides_ref[stream], row, depth, rows_x)
            for z in range(planes):
                copies.append(pltpu.make_async_copy(got.at[at, z], out_ref.at[:, z, x], sems.at[len(copies)]))
    run(copies)


def place(chunk, depth, sides, got, result):
    planes = result.shape[1]
    return pl.pallas_call(
        functools.partial(place_kernel, chunk, depth),
        out_shape=jax.ShapeDtypeStruct(result.shape, jnp.float32),
        in_specs=[SCALARS, VMEM, VMEM, HBM],
        out_specs=HBM,
        scratch_shapes=[pltpu.SemaphoreType.DMA((2 * len(own_rows(chunk, depth)) * planes,))],
        input_output_aliases={3: 0},
        compiler_params=pltpu.CompilerParams(vmem_limit_bytes=8 * 2**20),
        cost_estimate=cost(2),
        name="place",
    )(sides, *got, result)


def after(value, *others):
    return lax.optimization_barrier((value, *others))[0]


def maps_kernel(bits, me_ref, ahead_ref, back_ref, eigen_ref, *outs):
    steps = ahead_ref.shape[1]
    local_steps = outs[0].shape[0] // 4
    me = me_ref[0]
    real_part = 6.0 + eigen_ref[0:1, :]
    imag_part = eigen_ref[1:2, :]
    denom = real_part * real_part + imag_part * imag_part
    coef_re = real_part / denom
    coef_im = -imag_part / denom
    left = []
    for block in (me, jnp.bitwise_xor(me, bits[0]), jnp.bitwise_xor(me, bits[1])):
        span = pl.ds(pl.multiple_of(block * local_steps, local_steps), local_steps)
        back_re, back_im = back_ref[0, span, :], back_ref[1, span, :]
        for _ in range(2):
            back_re, back_im = back_re * coef_re - back_im * coef_im, back_re * coef_im + back_im * coef_re
            left += [back_re, back_im]
    left = jnp.concatenate(left, axis=0)
    by_re = jnp.dot(left, ahead_ref[0], precision=lax.Precision.HIGHEST, preferred_element_type=jnp.float32)
    by_im = jnp.dot(left, ahead_ref[1], precision=lax.Precision.HIGHEST, preferred_element_type=jnp.float32)

    def piece(data, which):
        return data[which * local_steps : (which + 1) * local_steps]

    row = lax.broadcasted_iota(jnp.int32, (steps, steps), 0)
    column = lax.broadcasted_iota(jnp.int32, (steps, steps), 1)
    turn = (row == jnp.bitwise_xor(column, me * local_steps)).astype(jnp.float32).astype(jnp.bfloat16)
    parts = []
    for block in range(3):
        for power in range(2):
            at = 2 * (2 * block + power)
            both = jnp.concatenate(
                [piece(by_re, at) - piece(by_im, at + 1), piece(by_im, at) + piece(by_re, at + 1)], axis=0
            )
            pair = jnp.concatenate(halves(both), axis=0)
            parts.append(jnp.dot(pair, turn, preferred_element_type=jnp.float32).astype(jnp.bfloat16))
    half = 2 * local_steps
    for out, blocks in zip(outs, ((0, 1), (0, 2))):
        for place, block in enumerate(blocks):
            once, twice = parts[2 * block], parts[2 * block + 1]
            columns = (once[:half], once[half:], once[:half], twice[:half], twice[half:], twice[:half])
            for c, value in enumerate(columns):
                out[place * half : (place + 1) * half, c * steps : (c + 1) * steps] = value


def make_maps(forward_map, back_map, eigen_values, me, count, bits):
    steps = forward_map.shape[1]
    shape = jax.ShapeDtypeStruct((4 * steps // count, 6 * steps), jnp.bfloat16)
    return pl.pallas_call(
        functools.partial(maps_kernel, bits),
        out_shape=[shape, shape],
        in_specs=[SCALARS] + [VMEM] * 3,
        out_specs=[VMEM] * 2,
        compiler_params=pltpu.CompilerParams(vmem_limit_bytes=VMEM_LIMIT),
        cost_estimate=cost(2),
        name="maps",
    )(me.astype(jnp.int32).reshape(1), forward_map, back_map, eigen_values)


def local(residual, step_ratio, forward_map, back_map, eigen_values):
    local_steps, planes, rows_x, rows_y = residual.shape
    depth = rows_x // 4
    count = lax.axis_size("tm")
    bits = (1, count // 2)
    all_bits = [1 << k for k in range(count.bit_length() - 1)]
    me = lax.axis_index("tm")
    sides = jnp.stack([jnp.where(jnp.bitwise_and(me, b) > 0, 1, 0) for b in bits]).astype(jnp.int32)
    ratio = jnp.broadcast_to((step_ratio.astype(jnp.float32) / 8.0)[:, None], (local_steps, rows_y))

    def swap(data, bit):
        return lax.ppermute(data, "tm", [(i, i ^ bit) for i in range(count)])

    spaces = lax.axis_size("space")
    upward = [(i, i + 1) for i in range(spaces - 1)]
    downward = [(i + 1, i) for i in range(spaces - 1)]

    queues = [[], []]

    def swap_in_turn(data, bit, *others, flight=1):
        queue = queues[0 if bit == bits[0] else 1]
        if len(queue) >= flight:
            others = (queue[-flight], *others)
        if others:
            data = after(data, *others)
        got = swap(data, bit)
        queue.append(got)
        return got

    masks = range(count)
    order = [[[m for m in masks if m in (0, b)], [m for m in masks if m not in (0, b)]] for b in bits]
    held = [[None] * CHUNKS for _ in range(2)]

    maps = make_maps(forward_map, back_map, eigen_values, me, count, bits)
    firsts = []

    def raw(chunk):
        data = after(residual, *firsts[-1]) if firsts else residual
        sent, kept = ((0, 1), (1, 1)), ((0, 0), (1, 0))
        mine = {}
        for kinds in (sent + kept,) if chunk else (sent, kept):
            mine.update(pick(chunk, kinds, data, step_ratio, bits, depth))
        have = [{0: mine[s, 0], bits[s]: swap_in_turn(mine[s, 1], bits[s])} for s in range(2)]
        firsts.append([have[s][bits[s]] for s in range(2)])
        for bit in all_bits:
            for mask in masks:
                for stream in (1, 0):
                    now = have[stream]
                    free = bit != bits[stream] and not mask & bit
                    if free and mask in now and (mask | bit) not in now:
                        others = maps if mask and chunk == 0 else []
                        now[mask | bit] = swap_in_turn(now[mask], bit, *others, flight=2 if chunk == 0 else 1)
        for stream in range(2):
            held[stream][chunk] = [have[stream][mask] for mask in masks]

    def beside(chunk, kind, *others):
        arrays = [
            [[a[m] for m in order[s][kind]] for a in held[s][max(chunk - 1, 0) : chunk + 1]] for s in range(2)
        ]
        if others:
            arrays[0][-1][0] = after(arrays[0][-1][0], *others)
        up, down = edges(chunk, depth, arrays)
        return lax.ppermute(up, "space", upward), lax.ppermute(down, "space", downward)

    gots = []
    gives = []
    result = None
    for chunk in range(CHUNKS):
        raw(chunk)
    shape = (2 * local_steps, planes, rows_x, rows_y)
    for chunk in range(CHUNKS):
        early = beside(chunk, 0)
        late = beside(chunk, 1, *early, *(gives[-1] if gives else []))
        used = [held[s][max(chunk - 1, 0) : chunk + 1] for s in range(2)]
        result, *give = apply(chunk, depth, order, sides, maps, early, late, used, shape, result)
        gives.append(give)
        gots.append([swap_in_turn(give[s], bits[s], flight=1 + min(chunk, 1)) for s in range(2)])
    for chunk in range(CHUNKS):
        result = place(chunk, depth, sides, gots[chunk], result)
    return result.reshape(2, local_steps, planes, rows_x, rows_y)


def solution(mesh):
    in_specs = (P("tm", "space", None, None), P("tm"), P(), P(), P())
    out_specs = P(None, "tm", "space", None, None)
    return jax.shard_map(local, mesh=mesh, in_specs=in_specs, out_specs=out_specs, check_vma=False)
```

```python
import functools

import jax
import jax.numpy as jnp
from jax import lax
from jax.experimental import pallas as pl
from jax.experimental.pallas import tpu as pltpu
from jax.sharding import PartitionSpec as P


CUTS = (0, 4, 8)
CHUNKS = len(CUTS) - 1
VMEM_LIMIT = 16 * 2**20
HBM = pl.BlockSpec(memory_space=pl.ANY)
VMEM = pl.BlockSpec(memory_space=pltpu.VMEM)
COST = 370000


def cost(weight):
    return pl.CostEstimate(flops=0, bytes_accessed=weight * COST, transcendentals=0)


def my_side(bit):
    return jnp.where(jnp.bitwise_and(lax.axis_index("tm"), bit) > 0, 1, 0)


def block_row(stream, side, row, depth, rows_x):
    if stream == 0:
        return row + side * (rows_x - 1 - 2 * row)
    return depth * (1 + side) + row


def own_rows(chunk, depth):
    bounds = [depth * cut // 8 for cut in CUTS]
    return list(range(bounds[chunk], bounds[chunk + 1]))


def chunk_rows(stream, chunk, depth):
    rows = own_rows(chunk, depth)
    first = rows[0] + 1 if chunk else (0 if stream == 0 else -1)
    return list(range(first, rows[-1] + 2))


def where_rows(stream, chunk, depth):
    places = {}
    for back in (1, 0):
        if chunk >= back:
            for at, row in enumerate(chunk_rows(stream, chunk - back, depth)):
                places[row] = (1 - back, at)
    return places


def run(copies):
    for copy in copies:
        copy.start()
    for copy in copies:
        copy.wait()


def pick_kernel(chunk, depth, kinds, bits, step_ref, in_ref, *refs):
    outs, sems = refs[:-1], refs[-1]
    steps, planes, rows_x, _ = in_ref.shape
    jobs = []
    for place, (stream, other) in enumerate(kinds):
        side = my_side(bits[stream])
        side = 1 - side if other else side
        for at, row in enumerate(chunk_rows(stream, chunk, depth)):
            x = block_row(stream, side, row, depth, rows_x)
            for z in range(planes):
                out = outs[place].at[at, z]
                jobs.append((pltpu.make_async_copy(in_ref.at[:, z, x], out, sems.at[len(jobs)]), out))
    for copy, _ in jobs:
        copy.start()
    line = step_ref[...].astype(jnp.float32) / 8.0
    down = lax.broadcasted_iota(jnp.int32, (steps, steps), 0)
    along = lax.broadcasted_iota(jnp.int32, (steps, steps), 1)
    ratio = jnp.sum(jnp.where(down == along, line, 0.0), axis=1, keepdims=True)
    for copy, out in jobs:
        copy.wait()
        out[...] = out[...] * ratio


def pick(chunk, kinds, residual, step_ratio, bits, depth):
    steps, planes, _, rows_y = residual.shape
    counts = [len(chunk_rows(stream, chunk, depth)) for stream, _ in kinds]
    first = chunk == 0 and kinds[0][1]
    limit = (56 if first else 8) * 2**20
    outs = pl.pallas_call(
        functools.partial(pick_kernel, chunk, depth, kinds, bits),
        out_shape=[jax.ShapeDtypeStruct((c, planes, steps, rows_y), jnp.float32) for c in counts],
        in_specs=[VMEM, HBM],
        out_specs=[VMEM] * len(kinds),
        scratch_shapes=[pltpu.SemaphoreType.DMA((sum(counts) * planes,))],
        compiler_params=pltpu.CompilerParams(vmem_limit_bytes=limit),
        cost_estimate=cost(5),
        name="pick",
    )(step_ratio.reshape(1, steps), residual)
    return dict(zip(kinds, outs))


def edge_kernel(chunk, depth, groups, *refs):
    raws, (up_ref, down_ref, sems) = refs[:-3], refs[-3:]
    planes = raws[0].shape[1]
    backs = 2 if chunk else 1
    copies = []
    for stream in range(2):
        places = where_rows(stream, chunk, depth)
        for at, row in enumerate(own_rows(chunk, depth)):
            back, index = places[row]
            for group in range(groups):
                raw = raws[(stream * backs + back - 2 + backs) * groups + group]
                for z, out in ((planes - 1, up_ref), (0, down_ref)):
                    copy = pltpu.make_async_copy(
                        raw.at[index, z], out.at[stream, at, group], sems.at[len(copies)]
                    )
                    copies.append(copy)
    run(copies)


def edges(chunk, depth, raws):
    groups = len(raws[0][0])
    _, _, steps, rows_y = raws[0][0][0].shape
    flat = [raw for stream in raws for arrays in stream for raw in arrays]
    high = len(own_rows(chunk, depth))
    shape = jax.ShapeDtypeStruct((2, high, groups, steps, rows_y), jnp.float32)
    return pl.pallas_call(
        functools.partial(edge_kernel, chunk, depth, groups),
        out_shape=[shape] * 2,
        in_specs=[HBM] * len(flat),
        out_specs=[VMEM] * 2,
        scratch_shapes=[pltpu.SemaphoreType.DMA((4 * high * groups,))],
        compiler_params=pltpu.CompilerParams(vmem_limit_bytes=8 * 2**20),
        cost_estimate=cost(3),
        name="edges",
    )(*flat)


def halves(value):
    high = value.astype(jnp.bfloat16)
    return high, (value - high.astype(jnp.float32)).astype(jnp.bfloat16)


def apply_kernel(chunk, depth, order, bits, map_a_ref, map_b_ref, *refs):
    (early_low, early_high, late_low, late_high), raws = refs[:4], refs[4:-5]
    out_ref, gives, own, sems = refs[-5], refs[-4:-2], refs[-2], refs[-1]
    groups = sum(len(part) for part in order[0])
    backs = 2 if chunk else 1
    _, planes, rows_x, rows_y = out_ref.shape
    stores = []
    for stream in range(2):
        maps = (map_a_ref, map_b_ref)[stream][...]
        half = maps.shape[0] // 2
        places = where_rows(stream, chunk, depth)

        def load(row, z):
            back, index = places[row]
            start = (stream * backs + back - 2 + backs) * groups
            return jnp.concatenate([raw[index, z] for raw in raws[start : start + groups]], axis=0)

        def outside(early, late, at):
            parts = {}
            for kind, ref in enumerate((early, late)):
                for place, group in enumerate(order[stream][kind]):
                    parts[group] = ref[stream, at, place]
            return jnp.concatenate([parts[group] for group in range(groups)], axis=0)

        for at, row in enumerate(own_rows(chunk, depth)):
            number = stream * len(own_rows(chunk, depth)) + at
            x = block_row(stream, my_side(bits[stream]), row, depth, rows_x)
            mids = [load(row, z) for z in range(planes)]
            for z, mid in enumerate(mids):
                lane = lax.broadcasted_iota(jnp.int32, mid.shape, 1)
                total = jnp.where(lane == 0, 0.0, pltpu.roll(mid, 1, 1))
                total = total + jnp.where(lane == rows_y - 1, 0.0, pltpu.roll(mid, rows_y - 1, 1))
                for beside in (row - 1, row + 1):
                    if beside in places:
                        total = total + load(beside, z)
                total = total + (mids[z - 1] if z else outside(early_low, late_low, at))
                total = total + (mids[z + 1] if z < planes - 1 else outside(early_high, late_high, at))
                mid_h, mid_l = halves(mid)
                sum_h, sum_l = halves(total)
                stack = jnp.concatenate([mid_h, mid_h, mid_l, sum_h, sum_h, sum_l], axis=0)
                value = jnp.dot(maps, stack, preferred_element_type=jnp.float32)
                own[number, z] = value[:half]
                gives[stream][at, z] = value[half:]
                store = pltpu.make_async_copy(own.at[number, z], out_ref.at[:, z, x], sems.at[number, z])
                store.start()
                stores.append(store)
    for store in stores:
        store.wait()


def apply(chunk, depth, order, bits, maps, early, late, raws, shape, result):
    _, planes, _, rows_y = raws[0][0][0].shape
    high = len(own_rows(chunk, depth))
    half = shape[0]
    flat = [raw for stream in raws for arrays in stream for raw in arrays]
    first = [] if result is None else [result]
    give = jax.ShapeDtypeStruct((high, planes, half, rows_y), jnp.float32)
    count = 2 + 4 + len(flat)

    def body(*refs):
        refs = refs[:count] + refs[count + len(first) :]
        apply_kernel(chunk, depth, order, bits, *refs)

    return pl.pallas_call(
        body,
        out_shape=[jax.ShapeDtypeStruct(shape, jnp.float32), give, give],
        in_specs=[VMEM] * count + [HBM] * len(first),
        out_specs=[HBM, VMEM, VMEM],
        scratch_shapes=[
            pltpu.VMEM((2 * high, planes, half, rows_y), jnp.float32),
            pltpu.SemaphoreType.DMA((2 * high, planes)),
        ],
        input_output_aliases={count: 0} if first else {},
        compiler_params=pltpu.CompilerParams(vmem_limit_bytes=VMEM_LIMIT),
        cost_estimate=cost(10),
        name="apply",
    )(*maps, *early, *late, *flat, *first)


def place_kernel(chunk, depth, bits, got_a, got_b, _, out_ref, sems):
    _, planes, rows_x, _ = out_ref.shape
    copies = []
    for stream, got in enumerate((got_a, got_b)):
        for at, row in enumerate(own_rows(chunk, depth)):
            x = block_row(stream, 1 - my_side(bits[stream]), row, depth, rows_x)
            for z in range(planes):
                copies.append(pltpu.make_async_copy(got.at[at, z], out_ref.at[:, z, x], sems.at[len(copies)]))
    run(copies)


def place(chunk, depth, bits, got, result):
    planes = result.shape[1]
    return pl.pallas_call(
        functools.partial(place_kernel, chunk, depth, bits),
        out_shape=jax.ShapeDtypeStruct(result.shape, jnp.float32),
        in_specs=[VMEM, VMEM, HBM],
        out_specs=HBM,
        scratch_shapes=[pltpu.SemaphoreType.DMA((2 * len(own_rows(chunk, depth)) * planes,))],
        input_output_aliases={2: 0},
        compiler_params=pltpu.CompilerParams(vmem_limit_bytes=8 * 2**20),
        cost_estimate=cost(2),
        name="place",
    )(*got, result)


def after(value, *others):
    return lax.optimization_barrier((value, *others))[0]


def maps_kernel(bits, ahead_ref, back_ref, eigen_ref, *outs):
    steps = ahead_ref.shape[1]
    local_steps = outs[0].shape[0] // 4
    me = lax.axis_index("tm")
    real_part = 6.0 + eigen_ref[0:1, :]
    imag_part = eigen_ref[1:2, :]
    denom = real_part * real_part + imag_part * imag_part
    coef_re = real_part / denom
    coef_im = -imag_part / denom
    left = []
    for block in (me, jnp.bitwise_xor(me, bits[0]), jnp.bitwise_xor(me, bits[1])):
        span = pl.ds(pl.multiple_of(block * local_steps, local_steps), local_steps)
        back_re, back_im = back_ref[0, span, :], back_ref[1, span, :]
        for _ in range(2):
            back_re, back_im = back_re * coef_re - back_im * coef_im, back_re * coef_im + back_im * coef_re
            left += [back_re, back_im]
    left = jnp.concatenate(left, axis=0)
    by_re = jnp.dot(left, ahead_ref[0], precision=lax.Precision.HIGHEST, preferred_element_type=jnp.float32)
    by_im = jnp.dot(left, ahead_ref[1], precision=lax.Precision.HIGHEST, preferred_element_type=jnp.float32)

    def piece(data, which):
        return data[which * local_steps : (which + 1) * local_steps]

    row = lax.broadcasted_iota(jnp.int32, (steps, steps), 0)
    column = lax.broadcasted_iota(jnp.int32, (steps, steps), 1)
    turn = (row == jnp.bitwise_xor(column, me * local_steps)).astype(jnp.float32).astype(jnp.bfloat16)
    parts = []
    for block in range(3):
        for power in range(2):
            at = 2 * (2 * block + power)
            both = jnp.concatenate(
                [piece(by_re, at) - piece(by_im, at + 1), piece(by_im, at) + piece(by_re, at + 1)], axis=0
            )
            pair = jnp.concatenate(halves(both), axis=0)
            parts.append(jnp.dot(pair, turn, preferred_element_type=jnp.float32).astype(jnp.bfloat16))
    half = 2 * local_steps
    for out, blocks in zip(outs, ((0, 1), (0, 2))):
        for place, block in enumerate(blocks):
            once, twice = parts[2 * block], parts[2 * block + 1]
            columns = (once[:half], once[half:], once[:half], twice[:half], twice[half:], twice[:half])
            for c, value in enumerate(columns):
                out[place * half : (place + 1) * half, c * steps : (c + 1) * steps] = value


def make_maps(forward_map, back_map, eigen_values, count, bits):
    steps = forward_map.shape[1]
    shape = jax.ShapeDtypeStruct((4 * steps // count, 6 * steps), jnp.bfloat16)
    return pl.pallas_call(
        functools.partial(maps_kernel, bits),
        out_shape=[shape, shape],
        in_specs=[VMEM] * 3,
        out_specs=[VMEM] * 2,
        compiler_params=pltpu.CompilerParams(vmem_limit_bytes=VMEM_LIMIT),
        cost_estimate=cost(2),
        name="maps",
    )(forward_map, back_map, eigen_values)


def local(residual, step_ratio, forward_map, back_map, eigen_values):
    local_steps, planes, rows_x, rows_y = residual.shape
    depth = rows_x // 4
    count = lax.axis_size("tm")
    bits = (1, count // 2)
    all_bits = [1 << k for k in range(count.bit_length() - 1)]
    ratio = jnp.broadcast_to((step_ratio.astype(jnp.float32) / 8.0)[:, None], (local_steps, rows_y))

    def swap(data, bit):
        return lax.ppermute(data, "tm", [(i, i ^ bit) for i in range(count)])

    spaces = lax.axis_size("space")
    upward = [(i, i + 1) for i in range(spaces - 1)]
    downward = [(i + 1, i) for i in range(spaces - 1)]

    queues = [[], []]

    def swap_in_turn(data, bit, *others, flight=1):
        queue = queues[0 if bit == bits[0] else 1]
        if len(queue) >= flight:
            others = (queue[-flight], *others)
        if others:
            data = after(data, *others)
        got = swap(data, bit)
        queue.append(got)
        return got

    masks = range(count)
    order = [[[m for m in masks if m in (0, b)], [m for m in masks if m not in (0, b)]] for b in bits]
    held = [[None] * CHUNKS for _ in range(2)]

    maps = make_maps(forward_map, back_map, eigen_values, count, bits)
    firsts = []

    def raw(chunk):
        data = after(residual, *firsts[-1]) if firsts else residual
        sent, kept = ((0, 1), (1, 1)), ((0, 0), (1, 0))
        mine = {}
        for kinds in (sent + kept,) if chunk else (sent, kept):
            mine.update(pick(chunk, kinds, data, step_ratio, bits, depth))
        have = [{0: mine[s, 0], bits[s]: swap_in_turn(mine[s, 1], bits[s])} for s in range(2)]
        firsts.append([have[s][bits[s]] for s in range(2)])
        for bit in all_bits:
            for mask in masks:
                for stream in (1, 0):
                    now = have[stream]
                    free = bit != bits[stream] and not mask & bit
                    if free and mask in now and (mask | bit) not in now:
                        others = maps if mask and chunk == 0 else []
                        now[mask | bit] = swap_in_turn(now[mask], bit, *others, flight=2 if chunk == 0 else 1)
        for stream in range(2):
            held[stream][chunk] = [have[stream][mask] for mask in masks]

    def beside(chunk, kind, *others):
        arrays = [
            [[a[m] for m in order[s][kind]] for a in held[s][max(chunk - 1, 0) : chunk + 1]] for s in range(2)
        ]
        if others:
            arrays[0][-1][0] = after(arrays[0][-1][0], *others)
        up, down = edges(chunk, depth, arrays)
        return lax.ppermute(up, "space", upward), lax.ppermute(down, "space", downward)

    gots = []
    gives = []
    result = None
    for chunk in range(CHUNKS):
        raw(chunk)
    shape = (2 * local_steps, planes, rows_x, rows_y)
    for chunk in range(CHUNKS):
        early = beside(chunk, 0)
        late = beside(chunk, 1, *early, *(gives[-1] if gives else []))
        used = [held[s][max(chunk - 1, 0) : chunk + 1] for s in range(2)]
        result, *give = apply(chunk, depth, order, bits, maps, early, late, used, shape, result)
        gives.append(give)
        gots.append([swap_in_turn(give[s], bits[s], flight=1 + min(chunk, 1)) for s in range(2)])
    for chunk in range(CHUNKS):
        result = place(chunk, depth, bits, gots[chunk], result)
    return result.reshape(2, local_steps, planes, rows_x, rows_y)


def solution(mesh):
    in_specs = (P("tm", "space", None, None), P("tm"), P(), P(), P())
    out_specs = P(None, "tm", "space", None, None)
    return jax.shard_map(local, mesh=mesh, in_specs=in_specs, out_specs=out_specs, check_vma=False)
```

```python
import functools

import jax
import jax.numpy as jnp
from jax import lax
from jax.experimental import pallas as pl
from jax.experimental.pallas import tpu as pltpu
from jax.sharding import PartitionSpec as P


CUTS = (0, 4, 8)
CHUNKS = len(CUTS) - 1
VMEM_LIMIT = 16 * 2**20
HBM = pl.BlockSpec(memory_space=pl.ANY)
VMEM = pl.BlockSpec(memory_space=pltpu.VMEM)
COST = 370000


def cost(weight):
    return pl.CostEstimate(flops=0, bytes_accessed=weight * COST, transcendentals=0)


def my_side(bit):
    return jnp.where(jnp.bitwise_and(lax.axis_index("tm"), bit) > 0, 1, 0)


def block_row(stream, side, row, depth, rows_x):
    if stream == 0:
        return row + side * (rows_x - 1 - 2 * row)
    return depth * (1 + side) + row


def own_rows(chunk, depth):
    bounds = [depth * cut // 8 for cut in CUTS]
    return list(range(bounds[chunk], bounds[chunk + 1]))


def chunk_rows(stream, chunk, depth):
    rows = own_rows(chunk, depth)
    first = rows[0] + 1 if chunk else (0 if stream == 0 else -1)
    return list(range(first, rows[-1] + 2))


def where_rows(stream, chunk, depth):
    places = {}
    for back in (1, 0):
        if chunk >= back:
            for at, row in enumerate(chunk_rows(stream, chunk - back, depth)):
                places[row] = (1 - back, at)
    return places


def run(copies):
    for copy in copies:
        copy.start()
    for copy in copies:
        copy.wait()


def pick_kernel(chunk, depth, kinds, bits, step_ref, in_ref, *refs):
    outs, sems = refs[:-1], refs[-1]
    steps, planes, rows_x, _ = in_ref.shape
    jobs = []
    for place, (stream, other) in enumerate(kinds):
        side = my_side(bits[stream])
        side = 1 - side if other else side
        for at, row in enumerate(chunk_rows(stream, chunk, depth)):
            x = block_row(stream, side, row, depth, rows_x)
            for z in range(planes):
                out = outs[place].at[at, z]
                jobs.append((pltpu.make_async_copy(in_ref.at[:, z, x], out, sems.at[len(jobs)]), out))
    for copy, _ in jobs:
        copy.start()
    line = step_ref[...].astype(jnp.float32) / 8.0
    down = lax.broadcasted_iota(jnp.int32, (steps, steps), 0)
    along = lax.broadcasted_iota(jnp.int32, (steps, steps), 1)
    ratio = jnp.sum(jnp.where(down == along, line, 0.0), axis=1, keepdims=True)
    for copy, out in jobs:
        copy.wait()
        out[...] = out[...] * ratio


def pick(chunk, kinds, residual, step_ratio, bits, depth):
    steps, planes, _, rows_y = residual.shape
    counts = [len(chunk_rows(stream, chunk, depth)) for stream, _ in kinds]
    first = chunk == 0 and kinds[0][1]
    limit = (56 if first else 8) * 2**20
    outs = pl.pallas_call(
        functools.partial(pick_kernel, chunk, depth, kinds, bits),
        out_shape=[jax.ShapeDtypeStruct((c, planes, steps, rows_y), jnp.float32) for c in counts],
        in_specs=[VMEM, HBM],
        out_specs=[VMEM] * len(kinds),
        scratch_shapes=[pltpu.SemaphoreType.DMA((sum(counts) * planes,))],
        compiler_params=pltpu.CompilerParams(vmem_limit_bytes=limit),
        cost_estimate=cost(5),
        name="pick",
    )(step_ratio.reshape(1, steps), residual)
    return dict(zip(kinds, outs))


def edge_kernel(chunk, depth, groups, *refs):
    raws, (up_ref, down_ref) = refs[:-2], refs[-2:]
    planes = raws[0].shape[1]
    backs = 2 if chunk else 1
    for stream in range(2):
        places = where_rows(stream, chunk, depth)
        for at, row in enumerate(own_rows(chunk, depth)):
            back, index = places[row]
            for group in range(groups):
                raw = raws[(stream * backs + back - 2 + backs) * groups + group]
                for z, out in ((planes - 1, up_ref), (0, down_ref)):
                    out[stream, at, group] = raw[index, z]


def edges(chunk, depth, raws):
    groups = len(raws[0][0])
    _, _, steps, rows_y = raws[0][0][0].shape
    flat = [raw for stream in raws for arrays in stream for raw in arrays]
    high = len(own_rows(chunk, depth))
    shape = jax.ShapeDtypeStruct((2, high, groups, steps, rows_y), jnp.float32)
    return pl.pallas_call(
        functools.partial(edge_kernel, chunk, depth, groups),
        out_shape=[shape] * 2,
        in_specs=[VMEM] * len(flat),
        out_specs=[VMEM] * 2,
        compiler_params=pltpu.CompilerParams(vmem_limit_bytes=8 * 2**20),
        cost_estimate=cost(3),
        name="edges",
    )(*flat)


def halves(value):
    high = value.astype(jnp.bfloat16)
    return high, (value - high.astype(jnp.float32)).astype(jnp.bfloat16)


def apply_kernel(chunk, depth, order, bits, map_a_ref, map_b_ref, *refs):
    (early_low, early_high, late_low, late_high), raws = refs[:4], refs[4:-5]
    out_ref, gives, own, sems = refs[-5], refs[-4:-2], refs[-2], refs[-1]
    groups = sum(len(part) for part in order[0])
    backs = 2 if chunk else 1
    _, planes, rows_x, rows_y = out_ref.shape
    stores = []
    for stream in range(2):
        maps = (map_a_ref, map_b_ref)[stream][...]
        half = maps.shape[0] // 2
        places = where_rows(stream, chunk, depth)

        def load(row, z):
            back, index = places[row]
            start = (stream * backs + back - 2 + backs) * groups
            return jnp.concatenate([raw[index, z] for raw in raws[start : start + groups]], axis=0)

        def outside(early, late, at):
            parts = {}
            for kind, ref in enumerate((early, late)):
                for place, group in enumerate(order[stream][kind]):
                    parts[group] = ref[stream, at, place]
            return jnp.concatenate([parts[group] for group in range(groups)], axis=0)

        for at, row in enumerate(own_rows(chunk, depth)):
            number = stream * len(own_rows(chunk, depth)) + at
            x = block_row(stream, my_side(bits[stream]), row, depth, rows_x)
            mids = [load(row, z) for z in range(planes)]
            for z, mid in enumerate(mids):
                lane = lax.broadcasted_iota(jnp.int32, mid.shape, 1)
                total = jnp.where(lane == 0, 0.0, pltpu.roll(mid, 1, 1))
                total = total + jnp.where(lane == rows_y - 1, 0.0, pltpu.roll(mid, rows_y - 1, 1))
                for beside in (row - 1, row + 1):
                    if beside in places:
                        total = total + load(beside, z)
                total = total + (mids[z - 1] if z else outside(early_low, late_low, at))
                total = total + (mids[z + 1] if z < planes - 1 else outside(early_high, late_high, at))
                mid_h, mid_l = halves(mid)
                sum_h, sum_l = halves(total)
                stack = jnp.concatenate([mid_h, mid_h, mid_l, sum_h, sum_h, sum_l], axis=0)
                value = jnp.dot(maps, stack, preferred_element_type=jnp.float32)
                own[number, z] = value[:half]
                gives[stream][at, z] = value[half:]
                store = pltpu.make_async_copy(own.at[number, z], out_ref.at[:, z, x], sems.at[number, z])
                store.start()
                stores.append(store)
    for store in stores:
        store.wait()


def apply(chunk, depth, order, bits, maps, early, late, raws, shape, result):
    _, planes, _, rows_y = raws[0][0][0].shape
    high = len(own_rows(chunk, depth))
    half = shape[0]
    flat = [raw for stream in raws for arrays in stream for raw in arrays]
    first = [] if result is None else [result]
    give = jax.ShapeDtypeStruct((high, planes, half, rows_y), jnp.float32)
    count = 2 + 4 + len(flat)

    def body(*refs):
        refs = refs[:count] + refs[count + len(first) :]
        apply_kernel(chunk, depth, order, bits, *refs)

    return pl.pallas_call(
        body,
        out_shape=[jax.ShapeDtypeStruct(shape, jnp.float32), give, give],
        in_specs=[VMEM] * count + [HBM] * len(first),
        out_specs=[HBM, VMEM, VMEM],
        scratch_shapes=[
            pltpu.VMEM((2 * high, planes, half, rows_y), jnp.float32),
            pltpu.SemaphoreType.DMA((2 * high, planes)),
        ],
        input_output_aliases={count: 0} if first else {},
        compiler_params=pltpu.CompilerParams(vmem_limit_bytes=VMEM_LIMIT),
        cost_estimate=cost(10),
        name="apply",
    )(*maps, *early, *late, *flat, *first)


def place_kernel(chunk, depth, bits, got_a, got_b, _, out_ref, sems):
    _, planes, rows_x, _ = out_ref.shape
    copies = []
    for stream, got in enumerate((got_a, got_b)):
        for at, row in enumerate(own_rows(chunk, depth)):
            x = block_row(stream, 1 - my_side(bits[stream]), row, depth, rows_x)
            for z in range(planes):
                copies.append(pltpu.make_async_copy(got.at[at, z], out_ref.at[:, z, x], sems.at[len(copies)]))
    run(copies)


def place(chunk, depth, bits, got, result):
    planes = result.shape[1]
    return pl.pallas_call(
        functools.partial(place_kernel, chunk, depth, bits),
        out_shape=jax.ShapeDtypeStruct(result.shape, jnp.float32),
        in_specs=[VMEM, VMEM, HBM],
        out_specs=HBM,
        scratch_shapes=[pltpu.SemaphoreType.DMA((2 * len(own_rows(chunk, depth)) * planes,))],
        input_output_aliases={2: 0},
        compiler_params=pltpu.CompilerParams(vmem_limit_bytes=8 * 2**20),
        cost_estimate=cost(2),
        name="place",
    )(*got, result)


def after(value, *others):
    return lax.optimization_barrier((value, *others))[0]


def maps_kernel(bits, ahead_ref, back_ref, eigen_ref, *outs):
    steps = ahead_ref.shape[1]
    local_steps = outs[0].shape[0] // 4
    me = lax.axis_index("tm")
    real_part = 6.0 + eigen_ref[0:1, :]
    imag_part = eigen_ref[1:2, :]
    denom = real_part * real_part + imag_part * imag_part
    coef_re = real_part / denom
    coef_im = -imag_part / denom
    left = []
    for block in (me, jnp.bitwise_xor(me, bits[0]), jnp.bitwise_xor(me, bits[1])):
        span = pl.ds(pl.multiple_of(block * local_steps, local_steps), local_steps)
        back_re, back_im = back_ref[0, span, :], back_ref[1, span, :]
        for _ in range(2):
            back_re, back_im = back_re * coef_re - back_im * coef_im, back_re * coef_im + back_im * coef_re
            left += [back_re, back_im]
    left = jnp.concatenate(left, axis=0)
    by_re = jnp.dot(left, ahead_ref[0], precision=lax.Precision.HIGHEST, preferred_element_type=jnp.float32)
    by_im = jnp.dot(left, ahead_ref[1], precision=lax.Precision.HIGHEST, preferred_element_type=jnp.float32)

    def piece(data, which):
        return data[which * local_steps : (which + 1) * local_steps]

    row = lax.broadcasted_iota(jnp.int32, (steps, steps), 0)
    column = lax.broadcasted_iota(jnp.int32, (steps, steps), 1)
    turn = (row == jnp.bitwise_xor(column, me * local_steps)).astype(jnp.float32).astype(jnp.bfloat16)
    parts = []
    for block in range(3):
        for power in range(2):
            at = 2 * (2 * block + power)
            both = jnp.concatenate(
                [piece(by_re, at) - piece(by_im, at + 1), piece(by_im, at) + piece(by_re, at + 1)], axis=0
            )
            pair = jnp.concatenate(halves(both), axis=0)
            parts.append(jnp.dot(pair, turn, preferred_element_type=jnp.float32).astype(jnp.bfloat16))
    half = 2 * local_steps
    for out, blocks in zip(outs, ((0, 1), (0, 2))):
        for place, block in enumerate(blocks):
            once, twice = parts[2 * block], parts[2 * block + 1]
            columns = (once[:half], once[half:], once[:half], twice[:half], twice[half:], twice[:half])
            for c, value in enumerate(columns):
                out[place * half : (place + 1) * half, c * steps : (c + 1) * steps] = value


def make_maps(forward_map, back_map, eigen_values, count, bits):
    steps = forward_map.shape[1]
    shape = jax.ShapeDtypeStruct((4 * steps // count, 6 * steps), jnp.bfloat16)
    return pl.pallas_call(
        functools.partial(maps_kernel, bits),
        out_shape=[shape, shape],
        in_specs=[VMEM] * 3,
        out_specs=[VMEM] * 2,
        compiler_params=pltpu.CompilerParams(vmem_limit_bytes=VMEM_LIMIT),
        cost_estimate=cost(2),
        name="maps",
    )(forward_map, back_map, eigen_values)


def local(residual, step_ratio, forward_map, back_map, eigen_values):
    local_steps, planes, rows_x, rows_y = residual.shape
    depth = rows_x // 4
    count = lax.axis_size("tm")
    bits = (1, count // 2)
    all_bits = [1 << k for k in range(count.bit_length() - 1)]
    ratio = jnp.broadcast_to((step_ratio.astype(jnp.float32) / 8.0)[:, None], (local_steps, rows_y))

    def swap(data, bit):
        return lax.ppermute(data, "tm", [(i, i ^ bit) for i in range(count)])

    spaces = lax.axis_size("space")
    upward = [(i, i + 1) for i in range(spaces - 1)]
    downward = [(i + 1, i) for i in range(spaces - 1)]

    queues = [[], []]

    def swap_in_turn(data, bit, *others, flight=1):
        queue = queues[0 if bit == bits[0] else 1]
        if len(queue) >= flight:
            others = (queue[-flight], *others)
        if others:
            data = after(data, *others)
        got = swap(data, bit)
        queue.append(got)
        return got

    masks = range(count)
    order = [[[m for m in masks if m in (0, b)], [m for m in masks if m not in (0, b)]] for b in bits]
    held = [[None] * CHUNKS for _ in range(2)]

    maps = make_maps(forward_map, back_map, eigen_values, count, bits)
    firsts = []

    def raw(chunk):
        data = after(residual, *firsts[-1]) if firsts else residual
        sent, kept = ((0, 1), (1, 1)), ((0, 0), (1, 0))
        mine = {}
        for kinds in (sent + kept,) if chunk else (sent, kept):
            mine.update(pick(chunk, kinds, data, step_ratio, bits, depth))
        have = [{0: mine[s, 0], bits[s]: swap_in_turn(mine[s, 1], bits[s])} for s in range(2)]
        firsts.append([have[s][bits[s]] for s in range(2)])
        for bit in all_bits:
            for mask in masks:
                for stream in (1, 0):
                    now = have[stream]
                    free = bit != bits[stream] and not mask & bit
                    if free and mask in now and (mask | bit) not in now:
                        others = maps if mask and chunk == 0 else []
                        now[mask | bit] = swap_in_turn(now[mask], bit, *others, flight=2 if chunk == 0 else 1)
        for stream in range(2):
            held[stream][chunk] = [have[stream][mask] for mask in masks]

    def beside(chunk, kind, *others):
        arrays = [
            [[a[m] for m in order[s][kind]] for a in held[s][max(chunk - 1, 0) : chunk + 1]] for s in range(2)
        ]
        if others:
            arrays[0][-1][0] = after(arrays[0][-1][0], *others)
        up, down = edges(chunk, depth, arrays)
        return lax.ppermute(up, "space", upward), lax.ppermute(down, "space", downward)

    gots = []
    gives = []
    result = None
    for chunk in range(CHUNKS):
        raw(chunk)
    shape = (2 * local_steps, planes, rows_x, rows_y)
    for chunk in range(CHUNKS):
        early = beside(chunk, 0)
        late = beside(chunk, 1, *early, *(gives[-1] if gives else []))
        used = [held[s][max(chunk - 1, 0) : chunk + 1] for s in range(2)]
        result, *give = apply(chunk, depth, order, bits, maps, early, late, used, shape, result)
        gives.append(give)
        gots.append([swap_in_turn(give[s], bits[s], flight=1 + min(chunk, 1)) for s in range(2)])
    for chunk in range(CHUNKS):
        result = place(chunk, depth, bits, gots[chunk], result)
    return result.reshape(2, local_steps, planes, rows_x, rows_y)


def solution(mesh):
    in_specs = (P("tm", "space", None, None), P("tm"), P(), P(), P())
    out_specs = P(None, "tm", "space", None, None)
    return jax.shard_map(local, mesh=mesh, in_specs=in_specs, out_specs=out_specs, check_vma=False)
```
